256 devices in a mesh: ctx: 32 (over x, y, core), fsdp: 8 (over z).
Axes of the slice: x: 4, y: 4, z: 8, core: 2. Of those that a mesh axis runs over, the one named last changes fastest.
Arguments:
- query_mr: bfloat16 [4096, 4096], P('ctx', 'fsdp'), may hold values from -6 to 6
- key_mr: bfloat16 [4096, 4096], P('ctx', 'fsdp'), may hold values from -6 to 6
- value_mr: bfloat16 [4096, 4096], P('ctx', 'fsdp'), may hold values from -6 to 6
- query_li: bfloat16 [4096, 4096], P('ctx', 'fsdp'), may hold values from -6 to 6
- key_li: bfloat16 [4096, 4096], P('ctx', 'fsdp'), may hold values from -6 to 6
- mr_taps: float32 [128, 4096], P(None, 'fsdp'), may hold values from -0.5 to 0.5
- li_time: float32 [16, 4096], P(None, 'fsdp'), may hold values from 30 to 81920
- li_residue: float32 [16, 4096], P(None, 'fsdp'), may hold values from -5 to 5
- li_skip: float32 [4096], P('fsdp'), may hold values from -6 to 6
- out_weight: bfloat16 [4096, 4096], P('ctx', 'fsdp'), may hold values from -0.09375 to 0.09375
- cotangent: bfloat16 [4096, 4096], P('ctx', 'fsdp'), may hold values from -6 to 6
Outputs:
- output: float32 [4096, 4096], P('ctx', 'fsdp')
- grad_query_mr: float32 [4096, 4096], P('ctx', 'fsdp')
- grad_key_mr: float32 [4096, 4096], P('ctx', 'fsdp')
- grad_value_mr: float32 [4096, 4096], P('ctx', 'fsdp')
- grad_query_li: float32 [4096, 4096], P('ctx', 'fsdp')
- grad_key_li: float32 [4096, 4096], P('ctx', 'fsdp')
- grad_taps: float32 [128, 4096], P(None, 'fsdp')
- grad_weight: float32 [4096, 4096], P('ctx', 'fsdp')
The draws below stay inside these ranges and needn't reach their ends.
All inputs are finite; a program needn't handle non-finite values.
Results may differ from the reference program's by a relative error of at most 0.014.
Values may be sent and summed in bfloat16 or wider, within the bound.
A program may use at most 64 MiB of HBM per device.

```python
import math
import jax
import jax.numpy as jnp
from jax import lax

WIDTH = 4096
CHANNELS = 4096
TAPS = 128
MODES = 16
SEQ = 4096
N_FSDP = 8


def draw_li_time(key, part):
    choose_key, fast_key, middle_key, slow_key = jax.random.split(key, 4)
    array_shape = (MODES, CHANNELS)
    quick_share = 0.2
    middle_share = 0.3
    quick_times = 30.0 + 20.0 * jax.random.uniform(fast_key, array_shape, jnp.float32)
    middle_top = 0.5 * SEQ
    middle_span = jnp.log(jnp.float32(middle_top / 50.0))
    middle_times = jnp.clip(50.0 * jnp.exp(middle_span * jax.random.uniform(middle_key, array_shape, jnp.float32)), 50.0, middle_top)
    slow_times = jnp.clip(0.5 * SEQ * jnp.exp(3.6888794541139363 * jax.random.uniform(slow_key, array_shape, jnp.float32)), 0.5 * SEQ, 20.0 * SEQ)
    chooser = jax.random.uniform(choose_key, array_shape, jnp.float32)
    picked = jnp.where(chooser < quick_share, quick_times, jnp.where(chooser < quick_share + middle_share, middle_times, slow_times))
    return jnp.clip(picked, 30.0, 20.0 * SEQ).astype(jnp.float32)


def steps_of(stream_key, shape, cuts, low, high):
    level = 1.0
    for axis_at, shards_of in cuts:
        heights = jax.random.uniform(jax.random.fold_in(jax.random.fold_in(stream_key, 6), axis_at), (shards_of,), jnp.float32, low / len(cuts), high / len(cuts))
        level = level * jnp.repeat(jnp.exp(heights), shape[axis_at] // shards_of).reshape((-1,) + (1,) * (len(shape) - 1 - axis_at))
    return level


def scatter_about(key, shape, deviation, reach, cuts=(), kind=jnp.bfloat16):
    loudness = steps_of(key, shape, cuts, -0.22, 0.18) if cuts else 1.0
    values = jax.random.normal(key, shape, jnp.float32) * deviation * loudness
    return jnp.minimum(jnp.maximum(values, -reach), reach).astype(kind)


def setup_inputs(seed: int = 0) -> dict:
    splits = jax.random.split(jax.random.key(seed), 12)
    return {
        "query_mr": scatter_about(splits[0], (SEQ, CHANNELS), 1.0, 6.0, ((0, 32), (1, 8))),
        "key_mr": scatter_about(splits[1], (SEQ, CHANNELS), 1.0, 6.0, ((0, 32), (1, 8))),
        "value_mr": scatter_about(splits[2], (SEQ, CHANNELS), 1.0, 6.0, ((0, 32), (1, 8))),
        "query_li": scatter_about(splits[3], (SEQ, CHANNELS), 1.0, 6.0, ((0, 32), (1, 8))),
        "key_li": scatter_about(splits[4], (SEQ, CHANNELS), 1.0, 6.0, ((0, 32), (1, 8))),
        "mr_taps": scatter_about(splits[5], (TAPS, CHANNELS), TAPS ** -0.5, 0.5, ((1, 8),), jnp.float32),
        "li_time": draw_li_time(jax.random.fold_in(splits[11], 71), 0),
        "li_residue": scatter_about(splits[7], (MODES, CHANNELS), 0.35, 5.0, ((1, 8),), jnp.float32),
        "li_skip": scatter_about(splits[8], (CHANNELS,), 0.5, 6.0, ((0, 8),), jnp.float32),
        "out_weight": scatter_about(splits[9], (WIDTH, CHANNELS), CHANNELS ** -0.5, 0.09375, ((0, 32), (1, 8))),
        "cotangent": scatter_about(splits[10], (SEQ, WIDTH), 1.0, 6.0, ((0, 32), (1, 8))),
    }


def shifted_taps(padded, tap_weights, row_count, backward):
    rim_size = tap_weights.shape[0] - 1

    def one_tap(tap_index, running):
        tap_index = jnp.asarray(tap_index).astype(jnp.int32)
        if backward:
            first_row = tap_index
        else:
            first_row = (rim_size - tap_index).astype(jnp.int32)
        window = lax.dynamic_slice_in_dim(padded, first_row, row_count, 0).astype(jnp.float32)
        weight_row = lax.dynamic_index_in_dim(tap_weights, tap_index, 0, keepdims=False)
        return running + weight_row[None, :] * window
    return lax.fori_loop(0, tap_weights.shape[0], one_tap, jnp.zeros((row_count, padded.shape[1]), jnp.float32))

def tap_gradient(grad_conv, padded, tap_count):
    row_count = grad_conv.shape[0]
    rim_size = tap_count - 1

    def one_tap(tap_index):
        first_row = (rim_size - tap_index).astype(jnp.int32)
        window = lax.dynamic_slice_in_dim(padded, first_row, row_count, 0).astype(jnp.float32)
        return lax.optimization_barrier(jnp.sum(grad_conv * window, axis=0))
    return lax.map(one_tap, jnp.arange(tap_count).astype(jnp.int32))

def causal_conv(signal, kernel):
    length = signal.shape[0]
    doubled = 2 * length
    spectrum = jnp.fft.rfft(signal, n=doubled, axis=0) * jnp.fft.rfft(kernel, n=doubled, axis=0)
    return jnp.fft.irfft(spectrum, n=doubled, axis=0)[:length]

def long_filter(li_time, li_residue, length):
    rate = 1.0 / li_time
    mode_coef = li_residue * jnp.sqrt(-jnp.expm1(-2.0 * rate))
    places = jnp.arange(length).astype(jnp.float32)
    kernel = jnp.zeros((length, li_time.shape[1]), jnp.float32)
    for mode_index in range(li_time.shape[0]):
        kernel = kernel + mode_coef[mode_index][None, :] * jnp.exp(-rate[mode_index][None, :] * places[:, None])
    return kernel

def reference(query_mr, key_mr, value_mr, query_li, key_li, mr_taps, li_time, li_residue, li_skip, out_weight, cotangent):
    groups = N_FSDP
    chan_dev = CHANNELS // groups
    length = query_mr.shape[0]
    rim_size = mr_taps.shape[0] - 1
    grad_scale = 1.0 / math.sqrt(length)

    def split_cols(array):
        return array.reshape(array.shape[0], groups, chan_dev).transpose(1, 0, 2)

    def merge_cols(array):
        return array.transpose(1, 0, 2).reshape(array.shape[1], groups * chan_dev)
    stacked = (split_cols(query_mr), split_cols(key_mr), split_cols(value_mr), split_cols(query_li), split_cols(key_li), split_cols(mr_taps), split_cols(li_time), split_cols(li_residue), split_cols(out_weight), li_skip.reshape(groups, chan_dev))

    def one_group(running, pieces):
        query_mr, key_mr, value_mr, query_li, key_li, mr_taps, li_time, li_residue, out_weight, li_skip = pieces
        mr_product = (key_mr.astype(jnp.float32) * value_mr.astype(jnp.float32)).astype(jnp.bfloat16)
        padded = jnp.concatenate([jnp.zeros((rim_size, chan_dev), jnp.bfloat16), mr_product], axis=0)
        mr_conv = shifted_taps(padded, mr_taps, length, False)
        mixed_mr = (query_mr.astype(jnp.float32) * mr_conv).astype(jnp.bfloat16)
        li_input = (key_li.astype(jnp.float32) * mixed_mr.astype(jnp.float32)).astype(jnp.bfloat16)
        kernel = long_filter(li_time, li_residue, length)
        li_signal = li_input.astype(jnp.float32)
        li_out = li_skip[None, :] * li_signal + causal_conv(li_signal, kernel)
        mixed_li = (query_li.astype(jnp.float32) * li_out).astype(jnp.bfloat16)
        group_part = lax.dot_general(mixed_li, out_weight, (((1,), (1,)), ((), ())), preferred_element_type=jnp.float32)
        running = running + group_part
        grad_mixed = jnp.dot(cotangent, out_weight, preferred_element_type=jnp.float32)
        grad_query_li = grad_mixed * li_out
        grad_li_out = grad_mixed * query_li.astype(jnp.float32)
        grad_li_input = li_skip[None, :] * grad_li_out + causal_conv(grad_li_out[::-1], kernel)[::-1]
        grad_key_li = grad_li_input * mixed_mr.astype(jnp.float32)
        grad_mixed_mr = grad_li_input * key_li.astype(jnp.float32)
        grad_query_mr = grad_mixed_mr * mr_conv
        grad_conv = grad_mixed_mr * query_mr.astype(jnp.float32)
        grad_padded = jnp.concatenate([grad_conv, jnp.zeros((rim_size, chan_dev), jnp.float32)], axis=0)
        grad_product = shifted_taps(grad_padded, mr_taps, length, True)
        grad_key_mr = grad_product * value_mr.astype(jnp.float32)
        grad_value_mr = grad_product * key_mr.astype(jnp.float32)
        grad_taps = tap_gradient(grad_conv, padded, mr_taps.shape[0]) * grad_scale
        grad_weight = lax.dot_general(cotangent, mixed_li, (((0,), (0,)), ((), ())), preferred_element_type=jnp.float32) * grad_scale
        return (running, (grad_query_mr, grad_key_mr, grad_value_mr, grad_query_li, grad_key_li, grad_taps, grad_weight))
    starting = jnp.zeros((length, cotangent.shape[1]), jnp.float32)
    running, results = lax.scan(one_group, starting, stacked)
    return (running, merge_cols(results[0]), merge_cols(results[1]), merge_cols(results[2]), merge_cols(results[3]), merge_cols(results[4]), merge_cols(results[5]), merge_cols(results[6]))
```

```python
import functools
import math

import jax
import jax.numpy as jnp
import ml_dtypes
import numpy as np
from jax import lax
from jax.experimental import pallas as pl
from jax.experimental.pallas import tpu as pltpu
from jax.sharding import PartitionSpec as P

BF = jnp.bfloat16
F32 = jnp.float32
MESH = pl.DeviceIdType.MESH
ROWS = 128
COLS = 512
MODES = 16
RING = 4
CHIPS = RING * RING
LANES = 128
GROUPS = COLS // LANES


def split_const(m):
    hi = m.astype(ml_dtypes.bfloat16)
    lo = (m - hi.astype(np.float64)).astype(ml_dtypes.bfloat16)
    return hi, lo


def transforms():
    theta = 2.0 * np.pi * (np.arange(ROWS) + 0.5)[:, None] / (2 * ROWS)

    def forward(places):
        return np.concatenate([np.cos(theta * places), -np.sin(theta * places)], axis=0)

    here = forward(np.arange(ROWS)[None, :].astype(np.float64))
    past = forward(np.arange(-ROWS, 0)[None, :].astype(np.float64))
    here_hi, here_lo = split_const(here)
    past_hi, past_lo = split_const(past)
    back_hi, back_lo = split_const(here.T / ROWS)
    return (
        np.concatenate([here_hi, here_hi, here_lo], axis=1),
        np.concatenate([past_hi, past_lo], axis=1),
        np.concatenate([back_hi, back_hi, back_lo], axis=1),
    )


def dot(a, b):
    return jnp.dot(a, b, preferred_element_type=F32)


def split3(v):
    hi = v.astype(BF)
    lo = (v - hi.astype(F32)).astype(BF)
    return jnp.concatenate([hi, lo, hi], axis=0)


def times(a, b):
    ar, ai, br, bi = a[:ROWS], a[ROWS:], b[:ROWS], b[ROWS:]
    return jnp.concatenate([ar * br - ai * bi, ar * bi + ai * br], axis=0)


def conj_times(a, b):
    ar, ai, br, bi = a[:ROWS], a[ROWS:], b[:ROWS], b[ROWS:]
    return jnp.concatenate([ar * br + ai * bi, ar * bi - ai * br], axis=0)


ID_A1 = 0
ID_A2 = 4
ID_C = 20
ID_HALO = 38
ID_BACK_HALO = 39
ID_SF1 = 40
ID_SF3 = 41
ID_SB1 = 42
ID_SB3 = 43
ID_MIX = 44
ID_GM = 45
ID_OUT = 46
ID_T1 = 47
ID_T4 = 48
ID_SF2 = 49
ID_SB2 = 65
ID_D = 81
ID_T2 = 97
ID_T3 = 113
ID_B = 129
ID_COUNT = 140

SCRATCH = dict(
    product=((ROWS, COLS), BF),
    prev=((ROWS, COLS), BF),
    grad_halo=((ROWS, COLS), BF),
    after=((ROWS, COLS), BF),
    wg=((CHIPS, ROWS, COLS), BF),
    cg=((8, 2 * ROWS, 256), BF),
    mixed=((2 * ROWS, COLS), BF),
    mixed_mr=((ROWS, COLS), BF),
    tap_spec=((2 * ROWS, COLS), F32),
    long_spec=((2 * ROWS, COLS), F32),
    prod_spec=((2 * ROWS, COLS), F32),
    mr_conv=((ROWS, COLS), F32),
    signal=((ROWS, COLS), F32),
    li_out=((ROWS, COLS), F32),
    work=((ROWS, COLS), F32),
    d8=((MODES, 8, COLS), F32),
    up0=((MODES, 8, COLS), F32),
    up7=((MODES, 8, COLS), F32),
    c0=((MODES, 8, COLS), F32),
    c1=((MODES, 8, COLS), F32),
    c8=((MODES, 8, COLS), F32),
    dev_decay=((MODES, COLS), F32),
    chip_decay=((MODES, COLS), F32),
    f_own=((MODES, COLS), F32),
    f_mate=((MODES, COLS), F32),
    f_chip=((8, COLS), F32),
    f_slots=((CHIPS, 8, COLS), F32),
    f_in=((MODES, COLS), F32),
    b_own=((MODES, COLS), F32),
    b_mate=((MODES, COLS), F32),
    b_chip=((8, COLS), F32),
    b_slots=((CHIPS, 8, COLS), F32),
    b_in=((MODES, COLS), F32),
    enter=((MODES, COLS), F32),
    gm_part=((2 * ROWS, COLS), F32),
    gm_mate=((ROWS, COLS), F32),
    spec=((2 * ROWS, COLS), F32),
    grad_out=((ROWS, COLS), F32),
    dw_send=((CHIPS, ROWS, COLS), BF),
    dw_slots=((CHIPS, ROWS, COLS), BF),
    o_send=((8, 2 * ROWS, 256), BF),
    o_slots=((8, 2 * ROWS, 256), BF),
    o_sum=((2 * ROWS, 256), F32),
    o_mate=((ROWS, 256), F32),
    t_own=((ROWS, COLS), F32),
    t_mate=((ROWS // 2, COLS), F32),
    t_half=((ROWS // 2, COLS), F32),
    t_slots=((CHIPS, 8, 256), F32),
    t_done=((8, 256), F32),
    t_all=((ROWS, COLS), F32),
    out=((ROWS, COLS), F32),
    gqm=((ROWS, COLS), F32),
    gkm=((ROWS, COLS), F32),
    gvm=((ROWS, COLS), F32),
    gql=((ROWS, COLS), F32),
    gkl=((ROWS, COLS), F32),
    gw=((ROWS, COLS), F32),
)


INPUTS = (
    ((ROWS, COLS), BF),
    ((ROWS, COLS), BF),
    ((ROWS, COLS), BF),
    ((ROWS, COLS), BF),
    ((ROWS, COLS), F32),
    ((MODES, COLS), F32),
    ((MODES, COLS), F32),
    ((ROWS, COLS), BF),
    ((ROWS, COLS), BF),
    ((ROWS, COLS), BF),
    ((1, COLS), F32),
    ((2 * ROWS, 3 * ROWS), BF),
    ((2 * ROWS, 2 * ROWS), BF),
    ((ROWS, 6 * ROWS), BF),
)


def kernel(*refs):
    n_in = len(INPUTS)
    given = refs[:n_in]
    results = refs[n_in : n_in + 8]
    held = refs[n_in + 8 : n_in + 8 + n_in]
    (km, vm, cot, w, taps, time, residue, qm, kl, ql, skip, fwd3, past2, inv3) = held
    s = dict(zip(SCRATCH, refs[2 * n_in + 8 :]))
    out, gqm, gkm, gvm, gql, gkl, gw = (s[n] for n in ("out", "gqm", "gkm", "gvm", "gql", "gkl", "gw"))
    snd, rcv, ld, st = refs[2 * n_in + 8 + len(SCRATCH) :]

    def load(i):
        return pltpu.make_async_copy(given[i], held[i], ld.at[i])

    for i in range(n_in):
        load(i).start()

    stored = []

    def store(source, i):
        c = pltpu.make_async_copy(source, results[i], st.at[i])
        c.start()
        stored.append(c)

    n_z = 8
    grad_scale = 1.0 / math.sqrt(ROWS * 2 * CHIPS)
    me = lax.axis_index("ctx")
    z = lax.axis_index("fsdp")
    k = lax.rem(me, 2)
    chip = lax.div(me, 2)
    x, y = lax.div(chip, RING), lax.rem(chip, RING)
    a = x * (1 - k) + y * k
    b = y * (1 - k) + x * k

    def ring(v, by):
        return lax.rem(v + by + RING, RING)

    def at(pa, pb):
        return (pa * RING + pb) * (1 - k) + (pb * RING + pa) * k

    def plane(c, core):
        return (c * 2 + core, z)

    mate = (chip * 2 + (1 - k), z)

    def up(dz):
        return (me, lax.rem(z + dz + n_z, n_z))

    def copy(src, dst, i, to):
        return pltpu.make_async_remote_copy(
            src_ref=src, dst_ref=dst, send_sem=snd.at[i], recv_sem=rcv.at[i], device_id=to, device_id_type=MESH
        )

    pending = []

    def send(src, dst, i, to):
        c = copy(src, dst, i, to)
        c.start()
        pending.append(c)

    def arrived(dst, i, to):
        copy(dst, dst, i, to).wait_recv()

    def half(h):
        return pl.ds(pl.multiple_of(h * ROWS, ROWS), ROWS)

    def chip_off(by):
        return lax.rem(chip + by + CHIPS, CHIPS)

    barrier = pltpu.get_barrier_semaphore()
    pl.semaphore_signal(barrier, inc=1, device_id=mate, device_id_type=MESH)

    def greet_chip(d, carry):
        pl.semaphore_signal(barrier, inc=1, device_id=plane(chip_off(d), k), device_id_type=MESH)
        return carry

    lax.fori_loop(1, CHIPS, greet_chip, 0)

    def greet_z(d, carry):
        pl.semaphore_signal(barrier, inc=1, device_id=up(d), device_id_type=MESH)
        return carry

    lax.fori_loop(1, n_z, greet_z, 0)
    last = 2 * CHIPS - 1
    across = (me + 2 * k - 1, z)

    @pl.when((me > 0) & (me < last))
    def _():
        pl.semaphore_signal(barrier, inc=1, device_id=across, device_id_type=MESH)

    for i in range(4):
        load(i).wait()
    s["product"][...] = (km[...].astype(F32) * vm[...].astype(F32)).astype(BF)
    for h in range(2):
        s["cg"][z, half(k), h * LANES : (h + 1) * LANES] = cot[
            :, pl.ds(pl.multiple_of((2 * h + k) * LANES, LANES), LANES)
        ]
    s["wg"][chip] = w[...]

    peers = 1 + (CHIPS - 1) + (n_z - 1)

    @pl.when((me == 0) | (me == last))
    def _():
        pl.semaphore_wait(barrier, peers)

    @pl.when((me > 0) & (me < last))
    def _():
        pl.semaphore_wait(barrier, peers + 1)

    nxt = (lax.rem(me + 1, last + 1), z)
    prv = (lax.rem(me + last, last + 1), z)

    halo = copy(s["product"], s["prev"], ID_HALO, nxt)

    @pl.when(me < last)
    def _():
        halo.start()

    a_next, a_prev = plane(at(ring(a, 1), b), k), plane(at(ring(a, -1), b), k)
    b_next, b_prev = plane(at(a, ring(b, 1)), k), plane(at(a, ring(b, -1)), k)
    low, high = pl.ds(0, ROWS // 2), pl.ds(ROWS // 2, ROWS // 2)
    wg = s["wg"]

    def wblock(ra, rb):
        return wg.at[at(ring(a, ra), ring(b, rb))]

    def whalf(ra, rb, rows):
        return wg.at[at(ring(a, ra), ring(b, rb)), rows]

    REL = (0, -1, 1, 2)

    def a2_send(j):
        block = wblock(REL[j], 0)
        send(block, block, ID_A2 + 4 * j, b_next)
        send(block, block, ID_A2 + 4 * j + 1, b_prev)

    def a1_send():
        block = wblock(0, 0)
        send(block, block, ID_A1, a_next)
        send(block, block, ID_A1 + 1, a_prev)

    def a1_forward():
        arrived(wblock(-1, 0), ID_A1, a_next)
        send(whalf(-1, 0, low), whalf(-1, 0, low), ID_A1 + 2, a_next)
        a2_send(1)
        arrived(wblock(1, 0), ID_A1 + 1, a_prev)
        send(whalf(1, 0, high), whalf(1, 0, high), ID_A1 + 3, a_prev)
        a2_send(2)

    def a1_finish():
        arrived(whalf(2, 0, low), ID_A1 + 2, a_next)
        arrived(whalf(2, 0, high), ID_A1 + 3, a_prev)
        a2_send(3)

    def a2_forward(j):
        ra = REL[j]
        arrived(wblock(ra, -1), ID_A2 + 4 * j, b_next)
        send(whalf(ra, -1, low), whalf(ra, -1, low), ID_A2 + 4 * j + 2, b_next)
        arrived(wblock(ra, 1), ID_A2 + 4 * j + 1, b_prev)
        send(whalf(ra, 1, high), whalf(ra, 1, high), ID_A2 + 4 * j + 3, b_prev)

    def a2_finish(j):
        ra = REL[j]
        arrived(whalf(ra, 2, low), ID_A2 + 4 * j + 2, b_next)
        arrived(whalf(ra, 2, high), ID_A2 + 4 * j + 3, b_prev)

    cg = s["cg"]
    z_next, z_prev = up(1), up(-1)

    def cblock(rz, chunk):
        rows = half(k) if chunk == 0 else half(1 - k)
        return cg.at[lax.rem(z + rz + n_z, n_z), rows]

    def c_id(direction, step, chunk):
        return ID_C + 2 + direction * 8 + (step - 1) * 2 + chunk

    def c_mate_refs(h, core):
        return cg.at[z, half(k if core else 1 - k), pl.ds(h * LANES, LANES)]

    def c_start():
        for h in range(2):
            send(
                cot.at[:, pl.ds(pl.multiple_of((2 * h + 1 - k) * LANES, LANES), LANES)],
                c_mate_refs(h, True),
                ID_C + h,
                mate,
            )
        send(cblock(0, 0), cblock(0, 0), c_id(0, 1, 0), z_next)
        send(cblock(0, 0), cblock(0, 0), c_id(1, 1, 0), z_prev)

    def c_second():
        for h in range(2):
            arrived(c_mate_refs(h, False), ID_C + h, mate)
        send(cblock(0, 1), cblock(0, 1), c_id(0, 1, 1), z_next)
        send(cblock(0, 1), cblock(0, 1), c_id(1, 1, 1), z_prev)

    def c_forward(step, chunk):
        arrived(cblock(-step, chunk), c_id(0, step, chunk), z_next)
        if step < 3 or chunk == 0:
            send(cblock(-step, chunk), cblock(-step, chunk), c_id(0, step + 1, chunk), z_next)
        arrived(cblock(step, chunk), c_id(1, step, chunk), z_prev)
        if step < 3 or chunk == 1:
            send(cblock(step, chunk), cblock(step, chunk), c_id(1, step + 1, chunk), z_prev)

    def c_finish():
        arrived(cblock(-4, 0), c_id(0, 4, 0), z_next)
        arrived(cblock(4, 1), c_id(1, 4, 1), z_prev)

    a1_send()
    c_start()
    a2_send(0)

    for i in range(4, n_in):
        load(i).wait()

    within = lax.broadcasted_iota(jnp.int32, (1, 8, LANES), 1).astype(F32)

    def tables(g, carry):
        lanes = pl.ds(pl.multiple_of(g * LANES, LANES), LANES)
        rate = 1.0 / time[:, lanes]
        u = 2.0 * rate
        series = 1.0 - u * (1.0 / 7.0)
        for n in (6, 5, 4, 3, 2):
            series = 1.0 - u * (1.0 / n) * series
        coef = residue[:, lanes] * jnp.sqrt(u * series)
        s["dev_decay"][:, lanes] = jnp.exp(-rate * ROWS)
        s["chip_decay"][:, lanes] = jnp.exp(-rate * (2 * ROWS))
        r3 = jnp.broadcast_to(rate[:, None, :], (MODES, 8, LANES))
        c3 = jnp.broadcast_to(coef[:, None, :], (MODES, 8, LANES))
        s["d8"][:, :, lanes] = jnp.exp(-r3 * 8.0)
        up0 = jnp.exp(-r3 * within)
        s["up0"][:, :, lanes] = up0
        s["up7"][:, :, lanes] = jnp.exp(-r3 * (7.0 - within))
        s["c0"][:, :, lanes] = c3 * up0
        s["c1"][:, :, lanes] = c3 * jnp.exp(-r3 * (within + 1.0))
        s["c8"][:, :, lanes] = c3 * jnp.exp(-r3 * (8.0 - within))
        return carry

    lax.fori_loop(0, GROUPS, tables, 0)

    def spread(table, state, target, descending):
        def one(g, carry):
            lanes = pl.ds(pl.multiple_of(g * LANES, LANES), LANES)
            d8 = s["d8"][:, :, lanes]
            v = table[:, :, lanes]
            if state is not None:
                v = v * jnp.broadcast_to(state[:, lanes][:, None, :], (MODES, 8, LANES))
            for t in range(ROWS // 8):
                tile = ROWS // 8 - 1 - t if descending else t
                target[tile * 8 : tile * 8 + 8, lanes] = jnp.sum(v, axis=0)
                if t < ROWS // 8 - 1:
                    v = v * d8
            return carry

        lax.fori_loop(0, GROUPS, one, 0)

    def gather_state(source, table, target, descending):
        def one(g, carry):
            lanes = pl.ds(pl.multiple_of(g * LANES, LANES), LANES)
            d8 = s["d8"][:, :, lanes]
            v = jnp.zeros((MODES, 8, LANES), F32)
            for t in range(ROWS // 8):
                tile = ROWS // 8 - 1 - t if descending else t
                rows = source[tile * 8 : tile * 8 + 8, lanes][None]
                v = v * d8 + rows if t else v + rows
            target[:, lanes] = jnp.sum(v * table[:, :, lanes], axis=1)
            return carry

        lax.fori_loop(0, GROUPS, one, 0)

    def transform(v):
        return dot(fwd3[...], split3(v))

    def inverse(v):
        return dot(inv3[...], split3(v))

    c_second()
    s["tap_spec"][...] = transform(taps[...])
    a1_forward()
    spread(s["c0"], None, s["work"], False)
    c_forward(1, 0)
    s["long_spec"][...] = transform(s["work"][...])

    @pl.when(me > 0)
    def _():
        halo.wait_recv()

    @pl.when(me == 0)
    def _():
        s["prev"][...] = jnp.zeros((ROWS, COLS), BF)

    here2 = jnp.concatenate([fwd3[:, :ROWS], fwd3[:, 2 * ROWS :]], axis=1)
    p, q = s["product"][...], s["prev"][...]
    s["prod_spec"][...] = dot(here2, jnp.concatenate([p, p], axis=0)) + dot(
        past2[...], jnp.concatenate([q, q], axis=0)
    )
    a1_finish()
    s["mr_conv"][...] = inverse(times(s["prod_spec"][...], s["tap_spec"][...]))
    mixed_mr = (qm[...].astype(F32) * s["mr_conv"][...]).astype(BF)
    s["mixed_mr"][...] = mixed_mr
    s["signal"][...] = (kl[...].astype(F32) * mixed_mr.astype(F32)).astype(BF).astype(F32)

    own8 = pl.ds(pl.multiple_of(k * 8, 8), 8)

    def chip_state(own, theirs, into, slots, id2, id3, target, descending):
        decay = s["dev_decay"][own8, :]
        mine, other = own[own8, :], theirs[own8, :]
        near = jnp.where(k == 0, mine, other)
        far = jnp.where(k == 0, other, mine)
        into[...] = near + decay * far if descending else decay * near + far
        sign = -1 if descending else 1
        ahead = chip if descending else CHIPS - 1 - chip
        behind = CHIPS - 1 - chip if descending else chip

        def put(d, carry):
            @pl.when(d <= ahead)
            def _():
                copy(into, slots.at[d], id2 + d, plane(chip_off(sign * d), k)).start()

            return carry

        lax.fori_loop(1, CHIPS, put, 0)

    def chip_finish(into, slots, id2, id3, target, descending):
        sign = -1 if descending else 1
        ahead = chip if descending else CHIPS - 1 - chip
        behind = CHIPS - 1 - chip if descending else chip

        def take(d, carry):
            @pl.when(d <= behind)
            def _():
                copy(into, slots.at[d], id2 + d, plane(chip_off(sign * d), k)).wait_recv()

            return carry

        lax.fori_loop(1, CHIPS, take, 0)
        decay = s["chip_decay"][own8, :]
        total = jnp.zeros((8, COLS), F32)
        for d in range(CHIPS - 1, 0, -1):
            total = jnp.where(d <= behind, total * decay + slots[d], 0.0)
        target[own8, :] = total
        send(target.at[own8], target.at[own8], id3, mate)

        def sent(d, carry):
            @pl.when(d <= ahead)
            def _():
                copy(into, slots.at[d], id2 + d, plane(chip_off(sign * d), k)).wait_send()

            return carry

        return lambda: lax.fori_loop(1, CHIPS, sent, 0)

    other8 = pl.ds(pl.multiple_of((1 - k) * 8, 8), 8)

    gather_state(s["signal"], s["up7"], s["f_own"], False)
    send(s["f_own"], s["f_mate"], ID_SF1, mate)
    a2_forward(0)
    c_forward(1, 1)
    arrived(s["f_mate"], ID_SF1, mate)
    chip_state(s["f_own"], s["f_mate"], s["f_chip"], s["f_slots"], ID_SF2, ID_SF3, s["f_in"], False)
    a2_forward(1)
    spectrum = times(transform(s["signal"][...]), s["long_spec"][...])
    s["li_out"][...] = inverse(spectrum) + skip[...] * s["signal"][...]
    c_forward(2, 0)
    a2_forward(2)
    f_sent = chip_finish(s["f_chip"], s["f_slots"], ID_SF2, ID_SF3, s["f_in"], False)
    c_forward(2, 1)
    arrived(s["f_in"].at[other8], ID_SF3, mate)
    s["enter"][...] = jnp.where(
        k == 0, s["f_in"][...], s["dev_decay"][...] * s["f_in"][...] + s["f_mate"][...]
    )
    spread(s["c1"], s["enter"], s["work"], False)
    s["li_out"][...] = s["li_out"][...] + s["work"][...]
    s["mixed"][half(k), :] = (ql[...].astype(F32) * s["li_out"][...]).astype(BF)
    send(s["mixed"].at[half(k)], s["mixed"].at[half(k)], ID_MIX, mate)
    a2_forward(3)
    c_forward(3, 0)
    c_forward(3, 1)
    for j in range(4):
        a2_finish(j)
    c_finish()

    s["gm_part"][...] = jnp.zeros((2 * ROWS, COLS), F32)

    def contract(j, carry):
        block = wg[pl.ds(2 * j, 2)].reshape(2 * ROWS, COLS)
        s["gm_part"][...] += dot(cg[j], block)
        return carry

    lax.fori_loop(0, n_z, contract, 0)
    send(s["gm_part"].at[half(1 - k)], s["gm_mate"], ID_GM, mate)

    arrived(s["mixed"].at[half(1 - k)], ID_MIX, mate)

    def project(j, carry):
        part = lax.dot_general(
            cg[j], s["mixed"][...], (((0,), (0,)), ((), ())), preferred_element_type=F32
        ).astype(BF)
        s["dw_send"][2 * j] = part[:ROWS]
        s["dw_send"][2 * j + 1] = part[ROWS:]
        return carry

    lax.fori_loop(0, n_z, project, 0)

    def d_copy(d):
        to = chip_off(d)
        return copy(s["dw_send"].at[to], s["dw_slots"].at[d], ID_D + d, plane(to, k))

    def loop(first, count, action):
        def step(d, carry):
            action(d)
            return carry

        lax.fori_loop(first, count, step, 0)

    arrived(s["gm_mate"], ID_GM, mate)
    gm = s["gm_part"][half(k), :] + s["gm_mate"][...]
    gql[...] = gm * s["li_out"][...]
    store(gql, 4)
    s["grad_out"][...] = gm * ql[...].astype(F32)
    gather_state(s["grad_out"], s["up0"], s["b_own"], True)
    send(s["b_own"], s["b_mate"], ID_SB1, mate)
    spectrum = conj_times(s["long_spec"][...], transform(s["grad_out"][...]))
    arrived(s["b_mate"], ID_SB1, mate)
    chip_state(s["b_own"], s["b_mate"], s["b_chip"], s["b_slots"], ID_SB2, ID_SB3, s["b_in"], True)
    loop(1, CHIPS, lambda d: d_copy(d).start())
    s["grad_out"][...] = inverse(spectrum) + skip[...] * s["grad_out"][...]

    def o_copy(dz):
        return copy(s["o_send"].at[dz], s["o_slots"].at[dz], ID_B + dz, up(dz))

    def share(dz, carry):
        j = lax.rem(z + dz, n_z)
        block = wg[pl.ds(2 * j, 2)].reshape(2 * ROWS, COLS)
        s["o_send"][dz] = lax.dot_general(
            s["mixed"][...], block, (((1,), (1,)), ((), ())), preferred_element_type=F32
        ).astype(BF)
        o_copy(dz).start()
        return carry

    lax.fori_loop(1, n_z, share, 0)
    s["o_sum"][...] = lax.dot_general(
        s["mixed"][...],
        wg[pl.ds(2 * z, 2)].reshape(2 * ROWS, COLS),
        (((1,), (1,)), ((), ())),
        preferred_element_type=F32,
    )

    b_sent = chip_finish(s["b_chip"], s["b_slots"], ID_SB2, ID_SB3, s["b_in"], True)
    arrived(s["b_in"].at[other8], ID_SB3, mate)
    s["enter"][...] = jnp.where(
        k == 1, s["b_in"][...], s["dev_decay"][...] * s["b_in"][...] + s["b_mate"][...]
    )
    spread(s["c8"], s["enter"], s["work"], True)
    gli = s["grad_out"][...] + s["work"][...]
    gkl[...] = gli * s["mixed_mr"][...].astype(F32)
    gmm = gli * kl[...].astype(F32)
    gqm[...] = gmm * s["mr_conv"][...]
    gconv = gmm * qm[...].astype(F32)
    s["work"][...] = gconv
    s["grad_halo"][...] = gconv.astype(BF)
    back = copy(s["grad_halo"], s["after"], ID_BACK_HALO, prv)

    @pl.when(me > 0)
    def _():
        back.start()

    store(gkl, 5)
    store(gqm, 1)

    spec = transform(s["work"][...])
    s["spec"][...] = spec
    s["t_own"][...] = inverse(conj_times(s["prod_spec"][...], spec))
    th = ROWS // 2

    def trows(core):
        return pl.ds(pl.multiple_of(core * th, th), th)

    send(s["t_own"].at[trows(1 - k)], s["t_mate"], ID_T1, mate)

    @pl.when(me == last)
    def _():
        s["after"][...] = jnp.zeros((ROWS, COLS), BF)

    @pl.when(me < last)
    def _():
        back.wait_recv()

    arrived(s["t_mate"], ID_T1, mate)
    s["t_half"][...] = s["t_own"][trows(k), :] + s["t_mate"][...]

    def piece(c, base):
        rows = pl.ds(pl.multiple_of(base + lax.div(c, 2) * 8, 8), 8)
        lanes = pl.ds(pl.multiple_of(lax.rem(c, 2) * 256, 256), 256)
        return rows, lanes

    def t2_copy(d):
        to = chip_off(d)
        rows, lanes = piece(to, 0)
        return copy(s["t_half"].at[rows, lanes], s["t_slots"].at[d], ID_T2 + d, plane(to, k))

    loop(1, CHIPS, lambda d: t2_copy(d).start())

    n = s["after"][...]
    spec = s["spec"][...] - dot(past2[...], jnp.concatenate([n, n], axis=0))
    gp = inverse(conj_times(s["tap_spec"][...], spec))
    gkm[...] = gp * vm[...].astype(F32)
    gvm[...] = gp * km[...].astype(F32)
    store(gkm, 2)
    store(gvm, 3)

    loop(1, CHIPS, lambda d: t2_copy(d).wait_recv())
    rows, lanes = piece(chip, 0)
    total = s["t_half"][rows, lanes]
    for d in range(1, CHIPS):
        total = total + s["t_slots"][d]
    total = total * grad_scale
    s["t_done"][...] = total
    rows, lanes = piece(chip, k * th)
    s["t_all"][rows, lanes] = total

    def t3_copy(d):
        return copy(s["t_done"], s["t_all"].at[rows, lanes], ID_T3 + d, plane(chip_off(d), k))

    def t3_arrived(d):
        rows_from, lanes_from = piece(chip_off(-d), k * th)
        copy(s["t_done"], s["t_all"].at[rows_from, lanes_from], ID_T3 + d, plane(chip_off(d), k)).wait_recv()

    loop(1, CHIPS, lambda d: t3_copy(d).start())

    loop(1, n_z, lambda d: o_copy(d).wait_recv())
    total = s["o_sum"][...]
    for d in range(1, n_z):
        total = total + s["o_slots"][d].astype(F32)
    s["o_sum"][...] = total
    send(s["o_sum"].at[half(1 - k)], s["o_mate"], ID_OUT, mate)

    loop(1, CHIPS, t3_arrived)
    send(s["t_all"].at[trows(k)], s["t_all"].at[trows(k)], ID_T4, mate)

    loop(1, CHIPS, lambda d: d_copy(d).wait_recv())
    total = s["dw_send"][chip].astype(F32)
    for d in range(1, CHIPS):
        total = total + s["dw_slots"][d].astype(F32)
    gw[...] = total * grad_scale
    store(gw, 7)

    arrived(s["o_mate"], ID_OUT, mate)
    for h in range(2):
        mine = pl.ds(pl.multiple_of((2 * h + k) * LANES, LANES), LANES)
        theirs = pl.ds(pl.multiple_of((2 * h + 1 - k) * LANES, LANES), LANES)
        out[:, mine] = s["o_sum"][half(k), h * LANES : (h + 1) * LANES]
        out[:, theirs] = s["o_mate"][:, h * LANES : (h + 1) * LANES]
    store(out, 0)

    arrived(s["t_all"].at[trows(1 - k)], ID_T4, mate)
    store(s["t_all"], 6)

    for c in stored:
        c.wait()
    for c in pending:
        c.wait_send()
    f_sent()
    b_sent()
    loop(1, CHIPS, lambda d: d_copy(d).wait_send())
    loop(1, CHIPS, lambda d: t2_copy(d).wait_send())
    loop(1, CHIPS, lambda d: t3_copy(d).wait_send())
    loop(1, n_z, lambda d: o_copy(d).wait_send())

    @pl.when(me < last)
    def _():
        halo.wait_send()

    @pl.when(me > 0)
    def _():
        back.wait_send()


def shards(query_mr, key_mr, value_mr, query_li, key_li, mr_taps, li_time, li_residue, li_skip, out_weight, cotangent):
    consts = [jnp.asarray(m) for m in transforms()]
    args = (
        key_mr,
        value_mr,
        cotangent,
        out_weight,
        mr_taps,
        li_time,
        li_residue,
        query_mr,
        key_li,
        query_li,
        li_skip.reshape(1, COLS),
        *consts,
    )
    block = jax.ShapeDtypeStruct((ROWS, COLS), F32)
    hbm = pl.BlockSpec(memory_space=pltpu.HBM)
    results = pl.pallas_call(
        kernel,
        out_shape=(block,) * 8,
        in_specs=[hbm] * len(args),
        out_specs=(hbm,) * 8,
        scratch_shapes=[pltpu.VMEM(shape, kind) for shape, kind in INPUTS + tuple(SCRATCH.values())]
        + [pltpu.SemaphoreType.DMA((ID_COUNT,)), pltpu.SemaphoreType.DMA((ID_COUNT,)), pltpu.SemaphoreType.DMA((len(INPUTS),)), pltpu.SemaphoreType.DMA((8,))],
        compiler_params=pltpu.CompilerParams(
            collective_id=0, has_side_effects=True, vmem_limit_bytes=60 * 1024 * 1024
        ),
        cost_estimate=pl.CostEstimate(flops=3_000_000_000, bytes_accessed=4_000_000, transcendentals=1_000_000),
    )(*args)
    return pl.pallas_call(
        write_out,
        out_shape=(block,) * 8,
        in_specs=[hbm] * 8,
        out_specs=(hbm,) * 8,
        scratch_shapes=[pltpu.SemaphoreType.DMA((8,))],
        compiler_params=pltpu.CompilerParams(vmem_limit_bytes=60 * 1024 * 1024),
        cost_estimate=pl.CostEstimate(flops=0, bytes_accessed=4_000_000, transcendentals=0),
    )(*results)


def write_out(*refs):
    copies = [pltpu.make_async_copy(refs[i], refs[8 + i], refs[16].at[i]) for i in range(8)]
    for c in copies:
        c.start()
    for c in copies:
        c.wait()


def solution(mesh):
    rows = P("ctx", "fsdp")
    wide = P(None, "fsdp")
    return jax.shard_map(
        shards,
        mesh=mesh,
        in_specs=(rows, rows, rows, rows, rows, wide, wide, wide, P("fsdp"), rows, rows),
        out_specs=(rows, rows, rows, rows, rows, rows, wide, rows),
        check_vma=False,
    )
```

```python
import functools
import math

import jax
import jax.numpy as jnp
import ml_dtypes
import numpy as np
from jax import lax
from jax.experimental import pallas as pl
from jax.experimental.pallas import tpu as pltpu
from jax.sharding import PartitionSpec as P

BF = jnp.bfloat16
F32 = jnp.float32
MESH = pl.DeviceIdType.MESH
ROWS = 128
COLS = 512
MODES = 16
RING = 4
CHIPS = RING * RING
LANES = 128
GROUPS = COLS // LANES


def split_const(m):
    hi = m.astype(ml_dtypes.bfloat16)
    lo = (m - hi.astype(np.float64)).astype(ml_dtypes.bfloat16)
    return hi, lo


def transforms():
    theta = 2.0 * np.pi * (np.arange(ROWS) + 0.5)[:, None] / (2 * ROWS)

    def forward(places):
        return np.concatenate([np.cos(theta * places), -np.sin(theta * places)], axis=0)

    here = forward(np.arange(ROWS)[None, :].astype(np.float64))
    past = forward(np.arange(-ROWS, 0)[None, :].astype(np.float64))
    here_hi, here_lo = split_const(here)
    past_hi, past_lo = split_const(past)
    back_hi, back_lo = split_const(here.T / ROWS)
    return (
        np.concatenate([here_hi, here_hi, here_lo], axis=1),
        np.concatenate([past_hi, past_lo], axis=1),
        np.concatenate([back_hi, back_hi, back_lo], axis=1),
    )


def dot(a, b):
    return jnp.dot(a, b, preferred_element_type=F32)


def split3(v):
    hi = v.astype(BF)
    lo = (v - hi.astype(F32)).astype(BF)
    return jnp.concatenate([hi, lo, hi], axis=0)


def times(a, b):
    ar, ai, br, bi = a[:ROWS], a[ROWS:], b[:ROWS], b[ROWS:]
    return jnp.concatenate([ar * br - ai * bi, ar * bi + ai * br], axis=0)


def conj_times(a, b):
    ar, ai, br, bi = a[:ROWS], a[ROWS:], b[:ROWS], b[ROWS:]
    return jnp.concatenate([ar * br + ai * bi, ar * bi - ai * br], axis=0)


ID_A1 = 0
ID_A2 = 4
ID_C = 20
ID_HALO = 38
ID_BACK_HALO = 39
ID_SF1 = 40
ID_SF3 = 41
ID_SB1 = 42
ID_SB3 = 43
ID_MIX = 44
ID_GM = 45
ID_OUT = 46
ID_T1 = 47
ID_T4 = 48
ID_SF2 = 49
ID_SB2 = 65
ID_T2 = 81
ID_T3 = 97
ID_D1 = 113
ID_D2 = 129
ID_B = 133
ID_COUNT = 149

SCRATCH = dict(
    product=((ROWS, COLS), BF),
    prev=((ROWS, COLS), BF),
    grad_halo=((ROWS, COLS), BF),
    after=((ROWS, COLS), BF),
    wg=((CHIPS, ROWS, COLS), BF),
    cg=((8, 2 * ROWS, 256), BF),
    mixed=((2 * ROWS, COLS), BF),
    mixed_mr=((ROWS, COLS), BF),
    tap_spec=((2 * ROWS, COLS), F32),
    long_spec=((2 * ROWS, COLS), F32),
    prod_spec=((2 * ROWS, COLS), F32),
    mr_conv=((ROWS, COLS), F32),
    signal=((ROWS, COLS), F32),
    li_out=((ROWS, COLS), F32),
    work=((ROWS, COLS), F32),
    d8=((MODES, 8, COLS), F32),
    up0=((MODES, 8, COLS), F32),
    up7=((MODES, 8, COLS), F32),
    c0=((MODES, 8, COLS), F32),
    c1=((MODES, 8, COLS), F32),
    c8=((MODES, 8, COLS), F32),
    dev_decay=((MODES, COLS), F32),
    chip_decay=((MODES, COLS), F32),
    f_own=((MODES, COLS), F32),
    f_mate=((MODES, COLS), F32),
    f_chip=((8, COLS), F32),
    f_slots=((CHIPS, 8, COLS), F32),
    f_in=((MODES, COLS), F32),
    b_own=((MODES, COLS), F32),
    b_mate=((MODES, COLS), F32),
    b_chip=((8, COLS), F32),
    b_slots=((CHIPS, 8, COLS), F32),
    b_in=((MODES, COLS), F32),
    enter=((MODES, COLS), F32),
    gm_part=((2 * ROWS, COLS), F32),
    gm_mate=((ROWS, COLS), F32),
    spec=((2 * ROWS, COLS), F32),
    grad_out=((ROWS, COLS), F32),
    dw_part=((CHIPS, ROWS, COLS), BF),
    dw_half=((RING, ROWS, COLS), BF),
    dw_from_prev=((RING, ROWS, COLS), BF),
    dw_from_next=((RING, ROWS, COLS), BF),
    dw_ring=((RING, ROWS, COLS), BF),
    dw_half2=((ROWS, COLS), BF),
    dw_from_prev2=((ROWS, COLS), BF),
    dw_from_next2=((ROWS, COLS), BF),
    o_part=((8, 2 * ROWS, 256), BF),
    o_came=((8, 2 * ROWS, 256), BF),
    o_sum=((2 * ROWS, 256), F32),
    o_mate=((ROWS, 256), F32),
    t_own=((ROWS, COLS), F32),
    t_mate=((ROWS // 2, COLS), F32),
    t_half=((ROWS // 2, COLS), F32),
    t_slots=((CHIPS, 8, 256), F32),
    t_done=((8, 256), F32),
    t_all=((ROWS, COLS), F32),
    out=((ROWS, COLS), F32),
    gqm=((ROWS, COLS), F32),
    gkm=((ROWS, COLS), F32),
    gvm=((ROWS, COLS), F32),
    gql=((ROWS, COLS), F32),
    gkl=((ROWS, COLS), F32),
    gw=((ROWS, COLS), F32),
)


INPUTS = (
    ((ROWS, COLS), BF),
    ((ROWS, COLS), BF),
    ((ROWS, COLS), BF),
    ((ROWS, COLS), BF),
    ((ROWS, COLS), F32),
    ((MODES, COLS), F32),
    ((MODES, COLS), F32),
    ((ROWS, COLS), BF),
    ((ROWS, COLS), BF),
    ((ROWS, COLS), BF),
    ((1, COLS), F32),
    ((2 * ROWS, 3 * ROWS), BF),
    ((2 * ROWS, 2 * ROWS), BF),
    ((ROWS, 6 * ROWS), BF),
)


def kernel(*refs):
    n_in = len(INPUTS)
    given = refs[:n_in]
    results = refs[n_in : n_in + 8]
    held = refs[n_in + 8 : n_in + 8 + n_in]
    (km, vm, cot, w, taps, time, residue, qm, kl, ql, skip, fwd3, past2, inv3) = held
    s = dict(zip(SCRATCH, refs[2 * n_in + 8 :]))
    out, gqm, gkm, gvm, gql, gkl, gw = (s[n] for n in ("out", "gqm", "gkm", "gvm", "gql", "gkl", "gw"))
    snd, rcv, ld, st = refs[2 * n_in + 8 + len(SCRATCH) :]

    def load(i):
        return pltpu.make_async_copy(given[i], held[i], ld.at[i])

    for i in range(n_in):
        load(i).start()

    stored = []

    def store(source, i):
        c = pltpu.make_async_copy(source, results[i], st.at[i])
        c.start()
        stored.append(c)

    n_z = 8
    grad_scale = 1.0 / math.sqrt(ROWS * 2 * CHIPS)
    me = lax.axis_index("ctx")
    z = lax.axis_index("fsdp")
    k = lax.rem(me, 2)
    chip = lax.div(me, 2)
    x, y = lax.div(chip, RING), lax.rem(chip, RING)
    a = x * (1 - k) + y * k
    b = y * (1 - k) + x * k

    def ring(v, by):
        return lax.rem(v + by + RING, RING)

    def at(pa, pb):
        return (pa * RING + pb) * (1 - k) + (pb * RING + pa) * k

    def plane(c, core):
        return (c * 2 + core, z)

    mate = (chip * 2 + (1 - k), z)

    def up(dz):
        return (me, lax.rem(z + dz + n_z, n_z))

    def copy(src, dst, i, to):
        return pltpu.make_async_remote_copy(
            src_ref=src, dst_ref=dst, send_sem=snd.at[i], recv_sem=rcv.at[i], device_id=to, device_id_type=MESH
        )

    pending = []

    def send(src, dst, i, to):
        c = copy(src, dst, i, to)
        c.start()
        pending.append(c)

    def arrived(dst, i, to):
        copy(dst, dst, i, to).wait_recv()

    def half(h):
        return pl.ds(pl.multiple_of(h * ROWS, ROWS), ROWS)

    def chip_off(by):
        return lax.rem(chip + by + CHIPS, CHIPS)

    barrier = pltpu.get_barrier_semaphore()
    pl.semaphore_signal(barrier, inc=1, device_id=mate, device_id_type=MESH)

    def greet_chip(d, carry):
        pl.semaphore_signal(barrier, inc=1, device_id=plane(chip_off(d), k), device_id_type=MESH)
        return carry

    lax.fori_loop(1, CHIPS, greet_chip, 0)

    def greet_z(d, carry):
        pl.semaphore_signal(barrier, inc=1, device_id=up(d), device_id_type=MESH)
        return carry

    lax.fori_loop(1, n_z, greet_z, 0)
    last = 2 * CHIPS - 1
    across = (me + 2 * k - 1, z)

    @pl.when((me > 0) & (me < last))
    def _():
        pl.semaphore_signal(barrier, inc=1, device_id=across, device_id_type=MESH)

    for i in range(4):
        load(i).wait()
    s["product"][...] = (km[...].astype(F32) * vm[...].astype(F32)).astype(BF)
    for h in range(2):
        s["cg"][z, half(k), h * LANES : (h + 1) * LANES] = cot[
            :, pl.ds(pl.multiple_of((2 * h + k) * LANES, LANES), LANES)
        ]
    s["wg"][chip] = w[...]

    peers = 1 + (CHIPS - 1) + (n_z - 1)

    @pl.when((me == 0) | (me == last))
    def _():
        pl.semaphore_wait(barrier, peers)

    @pl.when((me > 0) & (me < last))
    def _():
        pl.semaphore_wait(barrier, peers + 1)

    nxt = (lax.rem(me + 1, last + 1), z)
    prv = (lax.rem(me + last, last + 1), z)

    halo = copy(s["product"], s["prev"], ID_HALO, nxt)

    @pl.when(me < last)
    def _():
        halo.start()

    a_next, a_prev = plane(at(ring(a, 1), b), k), plane(at(ring(a, -1), b), k)
    b_next, b_prev = plane(at(a, ring(b, 1)), k), plane(at(a, ring(b, -1)), k)
    low, high = pl.ds(0, ROWS // 2), pl.ds(ROWS // 2, ROWS // 2)
    wg = s["wg"]

    def wblock(ra, rb):
        return wg.at[at(ring(a, ra), ring(b, rb))]

    def whalf(ra, rb, rows):
        return wg.at[at(ring(a, ra), ring(b, rb)), rows]

    REL = (0, -1, 1, 2)

    def a2_send(j):
        block = wblock(REL[j], 0)
        send(block, block, ID_A2 + 4 * j, b_next)
        send(block, block, ID_A2 + 4 * j + 1, b_prev)

    def a1_send():
        block = wblock(0, 0)
        send(block, block, ID_A1, a_next)
        send(block, block, ID_A1 + 1, a_prev)

    def a1_forward():
        arrived(wblock(-1, 0), ID_A1, a_next)
        send(whalf(-1, 0, low), whalf(-1, 0, low), ID_A1 + 2, a_next)
        a2_send(1)
        arrived(wblock(1, 0), ID_A1 + 1, a_prev)
        send(whalf(1, 0, high), whalf(1, 0, high), ID_A1 + 3, a_prev)
        a2_send(2)

    def a1_finish():
        arrived(whalf(2, 0, low), ID_A1 + 2, a_next)
        arrived(whalf(2, 0, high), ID_A1 + 3, a_prev)
        a2_send(3)

    def a2_forward(j):
        ra = REL[j]
        arrived(wblock(ra, -1), ID_A2 + 4 * j, b_next)
        send(whalf(ra, -1, low), whalf(ra, -1, low), ID_A2 + 4 * j + 2, b_next)
        arrived(wblock(ra, 1), ID_A2 + 4 * j + 1, b_prev)
        send(whalf(ra, 1, high), whalf(ra, 1, high), ID_A2 + 4 * j + 3, b_prev)

    def a2_finish(j):
        ra = REL[j]
        arrived(whalf(ra, 2, low), ID_A2 + 4 * j + 2, b_next)
        arrived(whalf(ra, 2, high), ID_A2 + 4 * j + 3, b_prev)

    cg = s["cg"]
    z_next, z_prev = up(1), up(-1)

    def cblock(rz, chunk):
        rows = half(k) if chunk == 0 else half(1 - k)
        return cg.at[lax.rem(z + rz + n_z, n_z), rows]

    def c_id(direction, step, chunk):
        return ID_C + 2 + direction * 8 + (step - 1) * 2 + chunk

    def c_mate_refs(h, core):
        return cg.at[z, half(k if core else 1 - k), pl.ds(h * LANES, LANES)]

    def c_start():
        for h in range(2):
            send(
                cot.at[:, pl.ds(pl.multiple_of((2 * h + 1 - k) * LANES, LANES), LANES)],
                c_mate_refs(h, True),
                ID_C + h,
                mate,
            )
        send(cblock(0, 0), cblock(0, 0), c_id(0, 1, 0), z_next)
        send(cblock(0, 0), cblock(0, 0), c_id(1, 1, 0), z_prev)

    def c_second():
        for h in range(2):
            arrived(c_mate_refs(h, False), ID_C + h, mate)
        send(cblock(0, 1), cblock(0, 1), c_id(0, 1, 1), z_next)
        send(cblock(0, 1), cblock(0, 1), c_id(1, 1, 1), z_prev)

    def c_forward(step, chunk):
        arrived(cblock(-step, chunk), c_id(0, step, chunk), z_next)
        if step < 3 or chunk == 0:
            send(cblock(-step, chunk), cblock(-step, chunk), c_id(0, step + 1, chunk), z_next)
        arrived(cblock(step, chunk), c_id(1, step, chunk), z_prev)
        if step < 3 or chunk == 1:
            send(cblock(step, chunk), cblock(step, chunk), c_id(1, step + 1, chunk), z_prev)

    def c_finish():
        arrived(cblock(-4, 0), c_id(0, 4, 0), z_next)
        arrived(cblock(4, 1), c_id(1, 4, 1), z_prev)

    a1_send()
    c_start()
    a2_send(0)

    for i in range(4, n_in):
        load(i).wait()

    within = lax.broadcasted_iota(jnp.int32, (1, 8, LANES), 1).astype(F32)

    def tables(g, carry):
        lanes = pl.ds(pl.multiple_of(g * LANES, LANES), LANES)
        rate = 1.0 / time[:, lanes]
        u = 2.0 * rate
        series = 1.0 - u * (1.0 / 7.0)
        for n in (6, 5, 4, 3, 2):
            series = 1.0 - u * (1.0 / n) * series
        coef = residue[:, lanes] * jnp.sqrt(u * series)
        s["dev_decay"][:, lanes] = jnp.exp(-rate * ROWS)
        s["chip_decay"][:, lanes] = jnp.exp(-rate * (2 * ROWS))
        r3 = jnp.broadcast_to(rate[:, None, :], (MODES, 8, LANES))
        c3 = jnp.broadcast_to(coef[:, None, :], (MODES, 8, LANES))
        s["d8"][:, :, lanes] = jnp.exp(-r3 * 8.0)
        up0 = jnp.exp(-r3 * within)
        s["up0"][:, :, lanes] = up0
        s["up7"][:, :, lanes] = jnp.exp(-r3 * (7.0 - within))
        s["c0"][:, :, lanes] = c3 * up0
        s["c1"][:, :, lanes] = c3 * jnp.exp(-r3 * (within + 1.0))
        s["c8"][:, :, lanes] = c3 * jnp.exp(-r3 * (8.0 - within))
        return carry

    lax.fori_loop(0, GROUPS, tables, 0)

    def spread(table, state, target, descending):
        def one(g, carry):
            lanes = pl.ds(pl.multiple_of(g * LANES, LANES), LANES)
            d8 = s["d8"][:, :, lanes]
            v = table[:, :, lanes]
            if state is not None:
                v = v * jnp.broadcast_to(state[:, lanes][:, None, :], (MODES, 8, LANES))
            for t in range(ROWS // 8):
                tile = ROWS // 8 - 1 - t if descending else t
                target[tile * 8 : tile * 8 + 8, lanes] = jnp.sum(v, axis=0)
                if t < ROWS // 8 - 1:
                    v = v * d8
            return carry

        lax.fori_loop(0, GROUPS, one, 0)

    def gather_state(source, table, target, descending):
        def one(g, carry):
            lanes = pl.ds(pl.multiple_of(g * LANES, LANES), LANES)
            d8 = s["d8"][:, :, lanes]
            v = jnp.zeros((MODES, 8, LANES), F32)
            for t in range(ROWS // 8):
                tile = ROWS // 8 - 1 - t if descending else t
                rows = source[tile * 8 : tile * 8 + 8, lanes][None]
                v = v * d8 + rows if t else v + rows
            target[:, lanes] = jnp.sum(v * table[:, :, lanes], axis=1)
            return carry

        lax.fori_loop(0, GROUPS, one, 0)

    def transform(v):
        return dot(fwd3[...], split3(v))

    def inverse(v):
        return dot(inv3[...], split3(v))

    c_second()
    s["tap_spec"][...] = transform(taps[...])
    a1_forward()
    spread(s["c0"], None, s["work"], False)
    c_forward(1, 0)
    s["long_spec"][...] = transform(s["work"][...])

    @pl.when(me > 0)
    def _():
        halo.wait_recv()

    @pl.when(me == 0)
    def _():
        s["prev"][...] = jnp.zeros((ROWS, COLS), BF)

    here2 = jnp.concatenate([fwd3[:, :ROWS], fwd3[:, 2 * ROWS :]], axis=1)
    p, q = s["product"][...], s["prev"][...]
    s["prod_spec"][...] = dot(here2, jnp.concatenate([p, p], axis=0)) + dot(
        past2[...], jnp.concatenate([q, q], axis=0)
    )
    a1_finish()
    s["mr_conv"][...] = inverse(times(s["prod_spec"][...], s["tap_spec"][...]))
    mixed_mr = (qm[...].astype(F32) * s["mr_conv"][...]).astype(BF)
    s["mixed_mr"][...] = mixed_mr
    s["signal"][...] = (kl[...].astype(F32) * mixed_mr.astype(F32)).astype(BF).astype(F32)

    own8 = pl.ds(pl.multiple_of(k * 8, 8), 8)

    def chip_state(own, theirs, into, slots, id2, id3, target, descending):
        decay = s["dev_decay"][own8, :]
        mine, other = own[own8, :], theirs[own8, :]
        near = jnp.where(k == 0, mine, other)
        far = jnp.where(k == 0, other, mine)
        into[...] = near + decay * far if descending else decay * near + far
        sign = -1 if descending else 1
        ahead = chip if descending else CHIPS - 1 - chip
        behind = CHIPS - 1 - chip if descending else chip

        def put(d, carry):
            @pl.when(d <= ahead)
            def _():
                copy(into, slots.at[d], id2 + d, plane(chip_off(sign * d), k)).start()

            return carry

        lax.fori_loop(1, CHIPS, put, 0)

    def chip_finish(into, slots, id2, id3, target, descending):
        sign = -1 if descending else 1
        ahead = chip if descending else CHIPS - 1 - chip
        behind = CHIPS - 1 - chip if descending else chip

        def take(d, carry):
            @pl.when(d <= behind)
            def _():
                copy(into, slots.at[d], id2 + d, plane(chip_off(sign * d), k)).wait_recv()

            return carry

        lax.fori_loop(1, CHIPS, take, 0)
        decay = s["chip_decay"][own8, :]
        total = jnp.zeros((8, COLS), F32)
        for d in range(CHIPS - 1, 0, -1):
            total = jnp.where(d <= behind, total * decay + slots[d], 0.0)
        target[own8, :] = total
        send(target.at[own8], target.at[own8], id3, mate)

        def sent(d, carry):
            @pl.when(d <= ahead)
            def _():
                copy(into, slots.at[d], id2 + d, plane(chip_off(sign * d), k)).wait_send()

            return carry

        return lambda: lax.fori_loop(1, CHIPS, sent, 0)

    other8 = pl.ds(pl.multiple_of((1 - k) * 8, 8), 8)

    gather_state(s["signal"], s["up7"], s["f_own"], False)
    send(s["f_own"], s["f_mate"], ID_SF1, mate)
    a2_forward(0)
    c_forward(1, 1)
    arrived(s["f_mate"], ID_SF1, mate)
    chip_state(s["f_own"], s["f_mate"], s["f_chip"], s["f_slots"], ID_SF2, ID_SF3, s["f_in"], False)
    a2_forward(1)
    spectrum = times(transform(s["signal"][...]), s["long_spec"][...])
    s["li_out"][...] = inverse(spectrum) + skip[...] * s["signal"][...]
    c_forward(2, 0)
    a2_forward(2)
    f_sent = chip_finish(s["f_chip"], s["f_slots"], ID_SF2, ID_SF3, s["f_in"], False)
    c_forward(2, 1)
    arrived(s["f_in"].at[other8], ID_SF3, mate)
    s["enter"][...] = jnp.where(
        k == 0, s["f_in"][...], s["dev_decay"][...] * s["f_in"][...] + s["f_mate"][...]
    )
    spread(s["c1"], s["enter"], s["work"], False)
    s["li_out"][...] = s["li_out"][...] + s["work"][...]
    s["mixed"][half(k), :] = (ql[...].astype(F32) * s["li_out"][...]).astype(BF)
    send(s["mixed"].at[half(k)], s["mixed"].at[half(k)], ID_MIX, mate)
    a2_forward(3)
    c_forward(3, 0)
    c_forward(3, 1)
    for j in range(4):
        a2_finish(j)
    c_finish()

    s["gm_part"][...] = jnp.zeros((2 * ROWS, COLS), F32)

    def contract(j, carry):
        block = wg[pl.ds(2 * j, 2)].reshape(2 * ROWS, COLS)
        s["gm_part"][...] += dot(cg[j], block)
        return carry

    lax.fori_loop(0, n_z, contract, 0)
    send(s["gm_part"].at[half(1 - k)], s["gm_mate"], ID_GM, mate)

    arrived(s["mixed"].at[half(1 - k)], ID_MIX, mate)

    def project(j, carry):
        part = lax.dot_general(
            cg[j], s["mixed"][...], (((0,), (0,)), ((), ())), preferred_element_type=F32
        ).astype(BF)
        s["dw_part"][2 * j] = part[:ROWS]
        s["dw_part"][2 * j + 1] = part[ROWS:]
        return carry

    lax.fori_loop(0, n_z, project, 0)

    def dpart(ra, rb):
        return s["dw_part"].at[at(ring(a, ra), ring(b, rb))]

    def drows(ra, rb, rows):
        return s["dw_part"].at[at(ring(a, ra), ring(b, rb)), rows]

    def accumulate(target, came):
        target[...] = (target[...].astype(F32) + came[...].astype(F32)).astype(BF)

    def d_start(j):
        ra, i = REL[j], ID_D1 + 4 * j
        send(drows(ra, 2, low), s["dw_half"].at[j, low], i, b_next)
        send(drows(ra, 2, high), s["dw_half"].at[j, high], i + 1, b_prev)

    def d_middle(j):
        ra, i = REL[j], ID_D1 + 4 * j
        arrived(s["dw_half"].at[j, low], i, b_next)
        accumulate(drows(ra, 1, low), s["dw_half"].at[j, low])
        send(dpart(ra, 1), s["dw_from_prev"].at[j], i + 2, b_next)
        arrived(s["dw_half"].at[j, high], i + 1, b_prev)
        accumulate(drows(ra, -1, high), s["dw_half"].at[j, high])
        send(dpart(ra, -1), s["dw_from_next"].at[j], i + 3, b_prev)

    def d_sum(j):
        ra, i = REL[j], ID_D1 + 4 * j
        arrived(s["dw_from_prev"].at[j], i + 2, b_next)
        arrived(s["dw_from_next"].at[j], i + 3, b_prev)
        return (
            dpart(ra, 0)[...].astype(F32)
            + s["dw_from_prev"][j].astype(F32)
            + s["dw_from_next"][j].astype(F32)
        )

    def d_end(j):
        s["dw_ring"][j] = d_sum(j).astype(BF)

    def d_turn():
        send(s["dw_ring"].at[3, low], s["dw_half2"].at[low], ID_D2, a_next)
        send(s["dw_ring"].at[3, high], s["dw_half2"].at[high], ID_D2 + 1, a_prev)

    def d_turn_middle():
        arrived(s["dw_half2"].at[low], ID_D2, a_next)
        accumulate(s["dw_ring"].at[2, low], s["dw_half2"].at[low])
        send(s["dw_ring"].at[2], s["dw_from_prev2"], ID_D2 + 2, a_next)
        arrived(s["dw_half2"].at[high], ID_D2 + 1, a_prev)
        accumulate(s["dw_ring"].at[1, high], s["dw_half2"].at[high])
        send(s["dw_ring"].at[1], s["dw_from_next2"], ID_D2 + 3, a_prev)

    for j in (3, 2, 1, 0):
        d_start(j)

    def share(j, carry):
        block = wg[pl.ds(2 * j, 2)].reshape(2 * ROWS, COLS)
        s["o_part"][j] = lax.dot_general(
            s["mixed"][...], block, (((1,), (1,)), ((), ())), preferred_element_type=F32
        ).astype(BF)
        return carry

    def opart(dz, chunk):
        return s["o_part"].at[lax.rem(z + dz + n_z, n_z), pl.ds(chunk * ROWS, ROWS)]

    def ocame(direction, step, chunk):
        return s["o_came"].at[direction * 4 + step - 1, pl.ds(chunk * ROWS, ROWS)]

    def b_send(direction, step, chunk):
        dz = (5 - step) * (1 if direction == 0 else -1)
        send(
            opart(dz, chunk),
            ocame(direction, step, chunk),
            ID_B + direction * 8 + (step - 1) * 2 + chunk,
            z_next if direction == 0 else z_prev,
        )

    def b_arrived(direction, step, chunk):
        arrived(
            ocame(direction, step, chunk),
            ID_B + direction * 8 + (step - 1) * 2 + chunk,
            z_next if direction == 0 else z_prev,
        )

    def b_start():
        for direction in range(2):
            b_send(direction, 1, direction)
            b_send(direction, 2, 1 - direction)

    def b_forward(step, chunk):
        for direction in range(2):
            if step == 1 and chunk != direction:
                continue
            b_arrived(direction, step, chunk)
            dz = (4 - step) * (1 if direction == 0 else -1)
            accumulate(opart(dz, chunk), ocame(direction, step, chunk))
            b_send(direction, step + 1, chunk)

    def loop(first, count, action):
        def step(d, carry):
            action(d)
            return carry

        lax.fori_loop(first, count, step, 0)

    arrived(s["gm_mate"], ID_GM, mate)
    gm = s["gm_part"][half(k), :] + s["gm_mate"][...]
    gql[...] = gm * s["li_out"][...]
    store(gql, 4)
    s["grad_out"][...] = gm * ql[...].astype(F32)
    gather_state(s["grad_out"], s["up0"], s["b_own"], True)
    send(s["b_own"], s["b_mate"], ID_SB1, mate)
    lax.fori_loop(0, n_z, share, 0)
    b_start()
    arrived(s["b_mate"], ID_SB1, mate)
    chip_state(s["b_own"], s["b_mate"], s["b_chip"], s["b_slots"], ID_SB2, ID_SB3, s["b_in"], True)
    d_middle(3)
    d_middle(2)
    s["o_sum"][...] = lax.dot_general(
        s["mixed"][...],
        wg[pl.ds(2 * z, 2)].reshape(2 * ROWS, COLS),
        (((1,), (1,)), ((), ())),
        preferred_element_type=F32,
    )
    b_forward(1, 0)
    b_forward(1, 1)
    d_middle(1)
    d_middle(0)
    spectrum = conj_times(s["long_spec"][...], transform(s["grad_out"][...]))
    s["grad_out"][...] = inverse(spectrum) + skip[...] * s["grad_out"][...]
    b_forward(2, 0)
    b_sent = chip_finish(s["b_chip"], s["b_slots"], ID_SB2, ID_SB3, s["b_in"], True)
    b_forward(2, 1)
    arrived(s["b_in"].at[other8], ID_SB3, mate)
    s["enter"][...] = jnp.where(
        k == 1, s["b_in"][...], s["dev_decay"][...] * s["b_in"][...] + s["b_mate"][...]
    )
    spread(s["c8"], s["enter"], s["work"], True)
    gli = s["grad_out"][...] + s["work"][...]
    gkl[...] = gli * s["mixed_mr"][...].astype(F32)
    gmm = gli * kl[...].astype(F32)
    gqm[...] = gmm * s["mr_conv"][...]
    gconv = gmm * qm[...].astype(F32)
    s["work"][...] = gconv
    s["grad_halo"][...] = gconv.astype(BF)
    back = copy(s["grad_halo"], s["after"], ID_BACK_HALO, prv)

    @pl.when(me > 0)
    def _():
        back.start()

    store(gkl, 5)
    store(gqm, 1)

    spec = transform(s["work"][...])
    s["spec"][...] = spec
    s["t_own"][...] = inverse(conj_times(s["prod_spec"][...], spec))
    th = ROWS // 2

    def trows(core):
        return pl.ds(pl.multiple_of(core * th, th), th)

    send(s["t_own"].at[trows(1 - k)], s["t_mate"], ID_T1, mate)
    d_end(3)
    d_turn()
    b_forward(3, 0)
    arrived(s["t_mate"], ID_T1, mate)
    s["t_half"][...] = s["t_own"][trows(k), :] + s["t_mate"][...]

    def piece(c, base):
        rows = pl.ds(pl.multiple_of(base + lax.div(c, 2) * 8, 8), 8)
        lanes = pl.ds(pl.multiple_of(lax.rem(c, 2) * 256, 256), 256)
        return rows, lanes

    def t2_copy(d):
        to = chip_off(d)
        rows, lanes = piece(to, 0)
        return copy(s["t_half"].at[rows, lanes], s["t_slots"].at[d], ID_T2 + d, plane(to, k))

    loop(1, CHIPS, lambda d: t2_copy(d).start())
    b_forward(3, 1)
    d_end(2)
    d_end(1)
    d_turn_middle()

    @pl.when(me == last)
    def _():
        s["after"][...] = jnp.zeros((ROWS, COLS), BF)

    @pl.when(me < last)
    def _():
        back.wait_recv()

    n = s["after"][...]
    spec = s["spec"][...] - dot(past2[...], jnp.concatenate([n, n], axis=0))
    gp = inverse(conj_times(s["tap_spec"][...], spec))
    gkm[...] = gp * vm[...].astype(F32)
    gvm[...] = gp * km[...].astype(F32)
    store(gkm, 2)
    store(gvm, 3)

    loop(1, CHIPS, lambda d: t2_copy(d).wait_recv())
    rows, lanes = piece(chip, 0)
    total = s["t_half"][rows, lanes]
    for d in range(1, CHIPS):
        total = total + s["t_slots"][d]
    total = total * grad_scale
    s["t_done"][...] = total
    rows, lanes = piece(chip, k * th)
    s["t_all"][rows, lanes] = total

    def t3_copy(d):
        return copy(s["t_done"], s["t_all"].at[rows, lanes], ID_T3 + d, plane(chip_off(d), k))

    def t3_arrived(d):
        rows_from, lanes_from = piece(chip_off(-d), k * th)
        copy(s["t_done"], s["t_all"].at[rows_from, lanes_from], ID_T3 + d, plane(chip_off(d), k)).wait_recv()

    loop(1, CHIPS, lambda d: t3_copy(d).start())

    for direction in range(2):
        for chunk in range(2):
            b_arrived(direction, 4, chunk)
    s["o_sum"][...] = s["o_sum"][...] + s["o_came"][3].astype(F32) + s["o_came"][7].astype(F32)
    send(s["o_sum"].at[half(1 - k)], s["o_mate"], ID_OUT, mate)

    total = d_sum(0)
    arrived(s["dw_from_prev2"], ID_D2 + 2, a_next)
    arrived(s["dw_from_next2"], ID_D2 + 3, a_prev)
    total = total + s["dw_from_prev2"][...].astype(F32) + s["dw_from_next2"][...].astype(F32)
    gw[...] = total * grad_scale
    store(gw, 7)

    arrived(s["o_mate"], ID_OUT, mate)
    for h in range(2):
        mine = pl.ds(pl.multiple_of((2 * h + k) * LANES, LANES), LANES)
        theirs = pl.ds(pl.multiple_of((2 * h + 1 - k) * LANES, LANES), LANES)
        out[:, mine] = s["o_sum"][half(k), h * LANES : (h + 1) * LANES]
        out[:, theirs] = s["o_mate"][:, h * LANES : (h + 1) * LANES]
    store(out, 0)

    loop(1, CHIPS, t3_arrived)
    send(s["t_all"].at[trows(k)], s["t_all"].at[trows(k)], ID_T4, mate)
    arrived(s["t_all"].at[trows(1 - k)], ID_T4, mate)
    store(s["t_all"], 6)

    for c in stored:
        c.wait()
    for c in pending:
        c.wait_send()
    f_sent()
    b_sent()
    loop(1, CHIPS, lambda d: t2_copy(d).wait_send())
    loop(1, CHIPS, lambda d: t3_copy(d).wait_send())

    @pl.when(me < last)
    def _():
        halo.wait_send()

    @pl.when(me > 0)
    def _():
        back.wait_send()


def shards(query_mr, key_mr, value_mr, query_li, key_li, mr_taps, li_time, li_residue, li_skip, out_weight, cotangent):
    consts = [jnp.asarray(m) for m in transforms()]
    args = (
        key_mr,
        value_mr,
        cotangent,
        out_weight,
        mr_taps,
        li_time,
        li_residue,
        query_mr,
        key_li,
        query_li,
        li_skip.reshape(1, COLS),
        *consts,
    )
    block = jax.ShapeDtypeStruct((ROWS, COLS), F32)
    hbm = pl.BlockSpec(memory_space=pltpu.HBM)
    results = pl.pallas_call(
        kernel,
        out_shape=(block,) * 8,
        in_specs=[hbm] * len(args),
        out_specs=(hbm,) * 8,
        scratch_shapes=[pltpu.VMEM(shape, kind) for shape, kind in INPUTS + tuple(SCRATCH.values())]
        + [pltpu.SemaphoreType.DMA((ID_COUNT,)), pltpu.SemaphoreType.DMA((ID_COUNT,)), pltpu.SemaphoreType.DMA((len(INPUTS),)), pltpu.SemaphoreType.DMA((8,))],
        compiler_params=pltpu.CompilerParams(
            collective_id=0, has_side_effects=True, vmem_limit_bytes=60 * 1024 * 1024
        ),
        cost_estimate=pl.CostEstimate(flops=3_000_000_000, bytes_accessed=4_000_000, transcendentals=1_000_000),
    )(*args)
    return pl.pallas_call(
        write_out,
        out_shape=(block,) * 8,
        in_specs=[hbm] * 8,
        out_specs=(hbm,) * 8,
        scratch_shapes=[
            pltpu.VMEM((8, ROWS, COLS), F32),
            pltpu.SemaphoreType.DMA((8,)),
            pltpu.SemaphoreType.DMA((8,)),
        ],
        compiler_params=pltpu.CompilerParams(vmem_limit_bytes=60 * 1024 * 1024),
        cost_estimate=pl.CostEstimate(flops=0, bytes_accessed=4_000_000, transcendentals=0),
    )(*results)


def write_out(*refs):
    held, load_sem, store_sem = refs[16:]
    loads = [pltpu.make_async_copy(refs[i], held.at[i], load_sem.at[i]) for i in range(8)]
    stores = [pltpu.make_async_copy(held.at[i], refs[8 + i], store_sem.at[i]) for i in range(8)]
    for c in loads:
        c.start()
    for load, store in zip(loads, stores):
        load.wait()
        store.start()
    for c in stores:
        c.wait()


def solution(mesh):
    rows = P("ctx", "fsdp")
    wide = P(None, "fsdp")
    return jax.shard_map(
        shards,
        mesh=mesh,
        in_specs=(rows, rows, rows, rows, rows, wide, wide, wide, P("fsdp"), rows, rows),
        out_specs=(rows, rows, rows, rows, rows, rows, wide, rows),
        check_vma=False,
    )
```

```python
import math
import types

import jax
import jax.numpy as jnp
import ml_dtypes
import numpy as np
from jax import lax
from jax.experimental import pallas as pl
from jax.experimental.pallas import tpu as pltpu
from jax.sharding import PartitionSpec as P

BF = jnp.bfloat16
F32 = jnp.float32
MESH = pl.DeviceIdType.MESH
ROWS = 128
COLS = 512
MODES = 16
RING = 4
CHIPS = RING * RING
LANES = 128
GROUPS = COLS // LANES


def split_const(m):
    hi = m.astype(ml_dtypes.bfloat16)
    lo = (m - hi.astype(np.float64)).astype(ml_dtypes.bfloat16)
    return hi, lo


def transforms():
    theta = 2.0 * np.pi * (np.arange(ROWS) + 0.5)[:, None] / (2 * ROWS)

    def forward(places):
        return np.concatenate([np.cos(theta * places), -np.sin(theta * places)], axis=0)

    here = forward(np.arange(ROWS)[None, :].astype(np.float64))
    past = forward(np.arange(-ROWS, 0)[None, :].astype(np.float64))
    here_hi, here_lo = split_const(here)
    past_hi, past_lo = split_const(past)
    back_hi, back_lo = split_const(here.T / ROWS)
    return (
        np.concatenate([here_hi, here_hi, here_lo], axis=1),
        np.concatenate([past_hi, past_lo], axis=1),
        np.concatenate([back_hi, back_hi, back_lo], axis=1),
    )


def dot(a, b):
    return jnp.dot(a, b, preferred_element_type=F32)


def split3(v):
    hi = v.astype(BF)
    lo = (v - hi.astype(F32)).astype(BF)
    return jnp.concatenate([hi, lo, hi], axis=0)


def times(a, b):
    ar, ai, br, bi = a[:ROWS], a[ROWS:], b[:ROWS], b[ROWS:]
    return jnp.concatenate([ar * br - ai * bi, ar * bi + ai * br], axis=0)


def conj_times(a, b):
    ar, ai, br, bi = a[:ROWS], a[ROWS:], b[:ROWS], b[ROWS:]
    return jnp.concatenate([ar * br + ai * bi, ar * bi - ai * br], axis=0)


ID_A1 = 0
ID_A2 = 4
ID_C = 20
ID_HALO = 38
ID_BACK_HALO = 39
ID_SF1 = 40
ID_SF3 = 41
ID_SB1 = 42
ID_SB3 = 43
ID_MIX = 44
ID_GM = 45
ID_OUT = 46
ID_T1 = 47
ID_T4 = 48
ID_SF2 = 49
ID_SB2 = 65
ID_T2 = 81
ID_T3 = 97
ID_D1 = 113
ID_D2 = 129
ID_B = 133
ID_CR = 149
ID_COUNT = 181

SCRATCH = dict(
    product=((ROWS, COLS), BF),
    prev=((ROWS, COLS), BF),
    grad_halo=((ROWS, COLS), BF),
    after=((ROWS, COLS), BF),
    wg=((CHIPS, ROWS, COLS), BF),
    cg=((8, 2 * ROWS, 256), BF),
    mixed=((2 * ROWS, COLS), BF),
    mixed_mr=((ROWS, COLS), BF),
    tap_spec=((2 * ROWS, COLS), F32),
    long_spec=((2 * ROWS, COLS), F32),
    prod_spec=((2 * ROWS, COLS), F32),
    mr_conv=((ROWS, COLS), F32),
    signal=((ROWS, COLS), F32),
    li_out=((ROWS, COLS), F32),
    work=((ROWS, COLS), F32),
    d8=((MODES, 8, COLS), F32),
    up0=((MODES, 8, COLS), F32),
    up7=((MODES, 8, COLS), F32),
    c0=((MODES, 8, COLS), F32),
    c1=((MODES, 8, COLS), F32),
    c8=((MODES, 8, COLS), F32),
    dev_decay=((MODES, COLS), F32),
    chip_decay=((MODES, COLS), F32),
    f_own=((MODES, COLS), F32),
    f_mate=((MODES, COLS), F32),
    f_chip=((8, COLS), F32),
    f_slots=((CHIPS, 8, COLS), F32),
    f_in=((MODES, COLS), F32),
    b_own=((MODES, COLS), F32),
    b_mate=((MODES, COLS), F32),
    b_chip=((8, COLS), F32),
    b_slots=((CHIPS, 8, COLS), F32),
    b_in=((MODES, COLS), F32),
    enter=((MODES, COLS), F32),
    gm_part=((2 * ROWS, COLS), F32),
    gm_mate=((ROWS, COLS), F32),
    spec=((2 * ROWS, COLS), F32),
    grad_out=((ROWS, COLS), F32),
    dw_part=((CHIPS, ROWS, COLS), BF),
    dw_half=((RING, ROWS, COLS), BF),
    dw_from_prev=((RING, ROWS, COLS), BF),
    dw_from_next=((RING, ROWS, COLS), BF),
    dw_ring=((RING, ROWS, COLS), BF),
    dw_half2=((ROWS, COLS), BF),
    dw_from_prev2=((ROWS, COLS), BF),
    dw_from_next2=((ROWS, COLS), BF),
    o_part=((8, 2 * ROWS, 256), BF),
    o_came=((8, 2 * ROWS, 256), BF),
    o_sum=((2 * ROWS, 256), F32),
    o_mate=((ROWS, 256), F32),
    t_own=((ROWS, COLS), F32),
    t_mate=((ROWS // 2, COLS), F32),
    t_half=((ROWS // 2, COLS), F32),
    t_slots=((CHIPS, 8, 256), F32),
    t_done=((8, 256), F32),
    t_all=((ROWS, COLS), F32),
    out=((ROWS, COLS), F32),
    gqm=((ROWS, COLS), F32),
    gkm=((ROWS, COLS), F32),
    gvm=((ROWS, COLS), F32),
    gql=((ROWS, COLS), F32),
    gkl=((ROWS, COLS), F32),
    gw=((ROWS, COLS), F32),
)


INPUTS = (
    ((ROWS, COLS), BF),
    ((ROWS, COLS), BF),
    ((ROWS, COLS), BF),
    ((ROWS, COLS), BF),
    ((ROWS, COLS), F32),
    ((MODES, COLS), F32),
    ((MODES, COLS), F32),
    ((ROWS, COLS), BF),
    ((ROWS, COLS), BF),
    ((ROWS, COLS), BF),
    ((1, COLS), F32),
    ((2 * ROWS, 3 * ROWS), BF),
    ((2 * ROWS, 2 * ROWS), BF),
    ((ROWS, 6 * ROWS), BF),
)


def kernel(*refs):
    n_in = len(INPUTS)
    given = refs[:n_in]
    results = refs[n_in : n_in + 8]
    held = refs[n_in + 8 : n_in + 8 + n_in]
    (km, vm, cot, w, taps, time, residue, qm, kl, ql, skip, fwd3, past2, inv3) = held
    s = types.SimpleNamespace(**dict(zip(SCRATCH, refs[2 * n_in + 8 :])))
    out, gqm, gkm, gvm, gql, gkl, gw = s.out, s.gqm, s.gkm, s.gvm, s.gql, s.gkl, s.gw
    snd, rcv, ld, st = refs[2 * n_in + 8 + len(SCRATCH) :]

    def load(i):
        return pltpu.make_async_copy(given[i], held[i], ld.at[i])

    for i in range(n_in):
        load(i).start()

    stored = []

    def store(source, i):
        c = pltpu.make_async_copy(source, results[i], st.at[i])
        c.start()
        stored.append(c)

    n_z = 8
    grad_scale = 1.0 / math.sqrt(ROWS * 2 * CHIPS)
    me = lax.axis_index("ctx")
    z = lax.axis_index("fsdp")
    k = lax.rem(me, 2)
    chip = lax.div(me, 2)
    x, y = lax.div(chip, RING), lax.rem(chip, RING)
    a = x * (1 - k) + y * k
    b = y * (1 - k) + x * k

    def ring(v, by):
        return lax.rem(v + by + RING, RING)

    def at(pa, pb):
        return (pa * RING + pb) * (1 - k) + (pb * RING + pa) * k

    def plane(c, core):
        return (c * 2 + core, z)

    mate = (chip * 2 + (1 - k), z)

    def up(dz):
        return (me, lax.rem(z + dz + n_z, n_z))

    def copy(src, dst, i, to):
        return pltpu.make_async_remote_copy(
            src_ref=src, dst_ref=dst, send_sem=snd.at[i], recv_sem=rcv.at[i], device_id=to, device_id_type=MESH
        )

    pending = []

    def send(src, dst, i, to):
        c = copy(src, dst, i, to)
        c.start()
        pending.append(c)

    def arrived(dst, i, to):
        copy(dst, dst, i, to).wait_recv()

    def half(h):
        return pl.ds(pl.multiple_of(h * ROWS, ROWS), ROWS)

    def chip_off(by):
        return lax.rem(chip + by + CHIPS, CHIPS)

    barrier = pltpu.get_barrier_semaphore()
    pl.semaphore_signal(barrier, inc=1, device_id=mate, device_id_type=MESH)

    def greet_chip(d, carry):
        pl.semaphore_signal(barrier, inc=1, device_id=plane(chip_off(d), k), device_id_type=MESH)
        return carry

    lax.fori_loop(1, CHIPS, greet_chip, 0)

    for d in (1, -1):
        pl.semaphore_signal(barrier, inc=1, device_id=up(d), device_id_type=MESH)
    last = 2 * CHIPS - 1
    across = (me + 2 * k - 1, z)

    @pl.when((me > 0) & (me < last))
    def _():
        pl.semaphore_signal(barrier, inc=1, device_id=across, device_id_type=MESH)

    for i in range(4):
        load(i).wait()
    s.product[...] = (km[...].astype(F32) * vm[...].astype(F32)).astype(BF)
    for h in range(2):
        s.cg[z, half(k), h * LANES : (h + 1) * LANES] = cot[
            :, pl.ds(pl.multiple_of((2 * h + k) * LANES, LANES), LANES)
        ]
    s.wg[chip] = w[...]

    peers = 1 + (CHIPS - 1) + 2

    @pl.when((me == 0) | (me == last))
    def _():
        pl.semaphore_wait(barrier, peers)

    @pl.when((me > 0) & (me < last))
    def _():
        pl.semaphore_wait(barrier, peers + 1)

    nxt = (lax.rem(me + 1, last + 1), z)
    prv = (lax.rem(me + last, last + 1), z)

    halo = copy(s.product, s.prev, ID_HALO, nxt)

    @pl.when(me < last)
    def _():
        halo.start()

    a_next, a_prev = plane(at(ring(a, 1), b), k), plane(at(ring(a, -1), b), k)
    b_next, b_prev = plane(at(a, ring(b, 1)), k), plane(at(a, ring(b, -1)), k)
    a_over, b_over = plane(at(ring(a, 2), b), k), plane(at(a, ring(b, 2)), k)
    low, high = pl.ds(0, ROWS // 2), pl.ds(ROWS // 2, ROWS // 2)
    wg = s.wg

    def wblock(ra, rb):
        return wg.at[at(ring(a, ra), ring(b, rb))]

    REL = (0, -1, 1, 2)

    def a2_send(j):
        block = wblock(REL[j], 0)
        if j == 3:
            send(block, block, ID_A2 + 4 * j + 2, b_over)
        send(block, block, ID_A2 + 4 * j, b_next)
        send(block, block, ID_A2 + 4 * j + 1, b_prev)

    def a1_send():
        block = wblock(0, 0)
        send(block, block, ID_A1 + 2, a_over)
        send(block, block, ID_A1, a_next)
        send(block, block, ID_A1 + 1, a_prev)

    def a1_forward():
        arrived(wblock(1, 0), ID_A1 + 1, a_prev)
        a2_send(2)
        arrived(wblock(-1, 0), ID_A1, a_next)
        a2_send(1)

    def a1_finish():
        arrived(wblock(2, 0), ID_A1 + 2, a_over)
        a2_send(3)

    def a2_forward(j):
        block = wblock(REL[j], 1)
        arrived(block, ID_A2 + 4 * j + 1, b_prev)
        send(block, block, ID_A2 + 4 * j + 3, b_prev)

    def a2_finish(j):
        arrived(wblock(REL[j], -1), ID_A2 + 4 * j, b_next)
        if j == 3:
            arrived(wblock(REL[j], 1), ID_A2 + 4 * j + 1, b_prev)
            arrived(wblock(REL[j], 2), ID_A2 + 4 * j + 2, b_over)
        else:
            arrived(wblock(REL[j], 2), ID_A2 + 4 * j + 3, b_prev)

    cg = s.cg
    z_next, z_prev = up(1), up(-1)

    def cblock(rz, chunk):
        core = k if chunk < 2 else 1 - k
        rows = pl.ds(pl.multiple_of(core * ROWS + chunk % 2 * 64, 64), 64)
        return cg.at[lax.rem(z + rz + n_z, n_z), rows]

    def c_id(direction, step, chunk):
        return ID_CR + direction * 16 + (step - 1) * 4 + chunk

    def c_send(direction, step, chunk):
        block = cblock(1 - step if direction == 0 else step - 1, chunk)
        send(block, block, c_id(direction, step, chunk), z_prev if direction else z_next)

    def c_mate_refs(h, core):
        return cg.at[z, half(k if core else 1 - k), pl.ds(h * LANES, LANES)]

    def c_start():
        for h in range(2):
            send(
                cot.at[:, pl.ds(pl.multiple_of((2 * h + 1 - k) * LANES, LANES), LANES)],
                c_mate_refs(h, True),
                ID_C + h,
                mate,
            )
        for chunk in range(2):
            for direction in range(2):
                c_send(direction, 1, chunk)

    def c_second():
        for h in range(2):
            arrived(c_mate_refs(h, False), ID_C + h, mate)
        for chunk in (2, 3):
            for direction in range(2):
                c_send(direction, 1, chunk)

    def c_forward(step, chunk):
        for direction in range(2):
            rz = step if direction else -step
            arrived(cblock(rz, chunk), c_id(direction, step, chunk), z_prev if direction else z_next)
            if step < 3 or chunk % 2 == direction:
                c_send(direction, step + 1, chunk)

    def c_finish():
        for chunk in range(4):
            direction = chunk % 2
            arrived(cblock(4, chunk), c_id(direction, 4, chunk), z_prev if direction else z_next)

    a1_send()
    c_start()
    a2_send(0)

    for i in range(4, n_in):
        load(i).wait()

    within = lax.broadcasted_iota(jnp.int32, (1, 8, LANES), 1).astype(F32)

    def tables(g, carry):
        lanes = pl.ds(pl.multiple_of(g * LANES, LANES), LANES)
        rate = 1.0 / time[:, lanes]
        u = 2.0 * rate
        series = 1.0 - u * (1.0 / 7.0)
        for n in (6, 5, 4, 3, 2):
            series = 1.0 - u * (1.0 / n) * series
        coef = residue[:, lanes] * jnp.sqrt(u * series)
        s.dev_decay[:, lanes] = jnp.exp(-rate * ROWS)
        s.chip_decay[:, lanes] = jnp.exp(-rate * (2 * ROWS))
        r3 = jnp.broadcast_to(rate[:, None, :], (MODES, 8, LANES))
        c3 = jnp.broadcast_to(coef[:, None, :], (MODES, 8, LANES))
        s.d8[:, :, lanes] = jnp.exp(-r3 * 8.0)
        up0 = jnp.exp(-r3 * within)
        s.up0[:, :, lanes] = up0
        s.up7[:, :, lanes] = jnp.exp(-r3 * (7.0 - within))
        s.c0[:, :, lanes] = c3 * up0
        s.c1[:, :, lanes] = c3 * jnp.exp(-r3 * (within + 1.0))
        s.c8[:, :, lanes] = c3 * jnp.exp(-r3 * (8.0 - within))
        return carry

    lax.fori_loop(0, GROUPS, tables, 0)

    def spread(table, state, target, descending):
        def one(g, carry):
            lanes = pl.ds(pl.multiple_of(g * LANES, LANES), LANES)
            d8 = s.d8[:, :, lanes]
            v = table[:, :, lanes]
            if state is not None:
                v = v * jnp.broadcast_to(state[:, lanes][:, None, :], (MODES, 8, LANES))
            for t in range(ROWS // 8):
                tile = ROWS // 8 - 1 - t if descending else t
                target[tile * 8 : tile * 8 + 8, lanes] = jnp.sum(v, axis=0)
                if t < ROWS // 8 - 1:
                    v = v * d8
            return carry

        lax.fori_loop(0, GROUPS, one, 0)

    def gather_state(source, table, target, descending):
        def one(g, carry):
            lanes = pl.ds(pl.multiple_of(g * LANES, LANES), LANES)
            d8 = s.d8[:, :, lanes]
            v = jnp.zeros((MODES, 8, LANES), F32)
            for t in range(ROWS // 8):
                tile = ROWS // 8 - 1 - t if descending else t
                rows = source[tile * 8 : tile * 8 + 8, lanes][None]
                v = v * d8 + rows if t else v + rows
            target[:, lanes] = jnp.sum(v * table[:, :, lanes], axis=1)
            return carry

        lax.fori_loop(0, GROUPS, one, 0)

    def transform(v):
        return dot(fwd3[...], split3(v))

    def inverse(v):
        return dot(inv3[...], split3(v))

    c_second()
    s.tap_spec[...] = transform(taps[...])
    spread(s.c0, None, s.work, False)
    c_forward(1, 0)
    c_forward(1, 1)
    a1_forward()
    c_forward(1, 2)
    a2_forward(0)
    c_forward(1, 3)
    s.long_spec[...] = transform(s.work[...])

    @pl.when(me > 0)
    def _():
        halo.wait_recv()

    @pl.when(me == 0)
    def _():
        s.prev[...] = jnp.zeros((ROWS, COLS), BF)

    here2 = jnp.concatenate([fwd3[:, :ROWS], fwd3[:, 2 * ROWS :]], axis=1)
    p, q = s.product[...], s.prev[...]
    s.prod_spec[...] = dot(here2, jnp.concatenate([p, p], axis=0)) + dot(
        past2[...], jnp.concatenate([q, q], axis=0)
    )
    a1_finish()
    c_forward(2, 0)
    s.mr_conv[...] = inverse(times(s.prod_spec[...], s.tap_spec[...]))
    mixed_mr = (qm[...].astype(F32) * s.mr_conv[...]).astype(BF)
    s.mixed_mr[...] = mixed_mr
    s.signal[...] = (kl[...].astype(F32) * mixed_mr.astype(F32)).astype(BF).astype(F32)

    own8 = pl.ds(pl.multiple_of(k * 8, 8), 8)

    def chip_state(own, theirs, into, slots, id2, descending):
        decay = s.dev_decay[own8, :]
        mine, other = own[own8, :], theirs[own8, :]
        near = jnp.where(k == 0, mine, other)
        far = jnp.where(k == 0, other, mine)
        into[...] = near + decay * far if descending else decay * near + far
        sign = -1 if descending else 1
        ahead = chip if descending else CHIPS - 1 - chip

        def put(d, carry):
            @pl.when(d <= ahead)
            def _():
                copy(into, slots.at[d], id2 + d, plane(chip_off(sign * d), k)).start()

            return carry

        for d in range(1, CHIPS):
            put(d, 0)

    def chip_finish(into, slots, id2, id3, target, descending):
        sign = -1 if descending else 1
        ahead = chip if descending else CHIPS - 1 - chip
        behind = CHIPS - 1 - chip if descending else chip

        def take(d, carry):
            @pl.when(d <= behind)
            def _():
                copy(into, slots.at[d], id2 + d, plane(chip_off(sign * d), k)).wait_recv()

            return carry

        lax.fori_loop(1, CHIPS, take, 0)
        decay = s.chip_decay[own8, :]
        total = jnp.zeros((8, COLS), F32)
        for d in range(CHIPS - 1, 0, -1):
            total = jnp.where(d <= behind, total * decay + slots[d], 0.0)
        target[own8, :] = total
        send(target.at[own8], target.at[own8], id3, mate)

        def sent(d, carry):
            @pl.when(d <= ahead)
            def _():
                copy(into, slots.at[d], id2 + d, plane(chip_off(sign * d), k)).wait_send()

            return carry

        return lambda: lax.fori_loop(1, CHIPS, sent, 0)

    other8 = pl.ds(pl.multiple_of((1 - k) * 8, 8), 8)

    c_forward(2, 1)
    c_forward(2, 2)
    gather_state(s.signal, s.up7, s.f_own, False)
    send(s.f_own, s.f_mate, ID_SF1, mate)
    c_forward(2, 3)
    a2_forward(2)
    a2_forward(1)
    arrived(s.f_mate, ID_SF1, mate)
    chip_state(s.f_own, s.f_mate, s.f_chip, s.f_slots, ID_SF2, False)
    c_forward(3, 0)
    c_forward(3, 1)
    spectrum = times(transform(s.signal[...]), s.long_spec[...])
    c_forward(3, 2)
    c_forward(3, 3)
    s.li_out[...] = inverse(spectrum) + skip[...] * s.signal[...]

    f_sent = chip_finish(s.f_chip, s.f_slots, ID_SF2, ID_SF3, s.f_in, False)
    arrived(s.f_in.at[other8], ID_SF3, mate)
    s.enter[...] = jnp.where(k == 0, s.f_in[...], s.dev_decay[...] * s.f_in[...] + s.f_mate[...])
    spread(s.c1, s.enter, s.work, False)
    s.li_out[...] = s.li_out[...] + s.work[...]
    s.mixed[half(k), :] = (ql[...].astype(F32) * s.li_out[...]).astype(BF)
    send(s.mixed.at[half(k)], s.mixed.at[half(k)], ID_MIX, mate)
    for j in range(4):
        a2_finish(j)
    c_finish()

    s.gm_part[...] = jnp.zeros((2 * ROWS, COLS), F32)

    def contract(j, carry):
        block = wg[pl.ds(2 * j, 2)].reshape(2 * ROWS, COLS)
        s.gm_part[...] += dot(cg[j], block)
        return carry

    lax.fori_loop(0, n_z, contract, 0)
    send(s.gm_part.at[half(1 - k)], s.gm_mate, ID_GM, mate)

    arrived(s.mixed.at[half(1 - k)], ID_MIX, mate)

    def project(j, carry):
        part = lax.dot_general(
            cg[j], s.mixed[...], (((0,), (0,)), ((), ())), preferred_element_type=F32
        ).astype(BF)
        s.dw_part[2 * j] = part[:ROWS]
        s.dw_part[2 * j + 1] = part[ROWS:]
        return carry

    lax.fori_loop(0, n_z, project, 0)

    def dpart(ra, rb):
        return s.dw_part.at[at(ring(a, ra), ring(b, rb))]

    def drows(ra, rb, rows):
        return s.dw_part.at[at(ring(a, ra), ring(b, rb)), rows]

    def accumulate(target, came):
        target[...] = (target[...].astype(F32) + came[...].astype(F32)).astype(BF)

    def d_start(j):
        ra, i = REL[j], ID_D1 + 4 * j
        send(drows(ra, 2, low), s.dw_half.at[j, low], i, b_next)
        send(drows(ra, 2, high), s.dw_half.at[j, high], i + 1, b_prev)

    def d_middle(j):
        ra, i = REL[j], ID_D1 + 4 * j
        arrived(s.dw_half.at[j, low], i, b_next)
        accumulate(drows(ra, 1, low), s.dw_half.at[j, low])
        send(dpart(ra, 1), s.dw_from_prev.at[j], i + 2, b_next)
        arrived(s.dw_half.at[j, high], i + 1, b_prev)
        accumulate(drows(ra, -1, high), s.dw_half.at[j, high])
        send(dpart(ra, -1), s.dw_from_next.at[j], i + 3, b_prev)

    def d_sum(j):
        ra, i = REL[j], ID_D1 + 4 * j
        arrived(s.dw_from_prev.at[j], i + 2, b_next)
        arrived(s.dw_from_next.at[j], i + 3, b_prev)
        return (
            dpart(ra, 0)[...].astype(F32)
            + s.dw_from_prev[j].astype(F32)
            + s.dw_from_next[j].astype(F32)
        )

    def d_end(j):
        s.dw_ring[j] = d_sum(j).astype(BF)

    def d_turn():
        send(s.dw_ring.at[3, low], s.dw_half2.at[low], ID_D2, a_next)
        send(s.dw_ring.at[3, high], s.dw_half2.at[high], ID_D2 + 1, a_prev)

    def d_turn_middle():
        arrived(s.dw_half2.at[low], ID_D2, a_next)
        accumulate(s.dw_ring.at[2, low], s.dw_half2.at[low])
        send(s.dw_ring.at[2], s.dw_from_prev2, ID_D2 + 2, a_next)
        arrived(s.dw_half2.at[high], ID_D2 + 1, a_prev)
        accumulate(s.dw_ring.at[1, high], s.dw_half2.at[high])
        send(s.dw_ring.at[1], s.dw_from_next2, ID_D2 + 3, a_prev)

    for j in (3, 2, 1, 0):
        d_start(j)

    def share(j, carry):
        block = wg[pl.ds(2 * j, 2)].reshape(2 * ROWS, COLS)
        s.o_part[j] = lax.dot_general(
            s.mixed[...], block, (((1,), (1,)), ((), ())), preferred_element_type=F32
        ).astype(BF)
        return carry

    def opart(dz, chunk):
        return s.o_part.at[lax.rem(z + dz + n_z, n_z), pl.ds(chunk * ROWS, ROWS)]

    def ocame(direction, step, chunk):
        return s.o_came.at[direction * 4 + step - 1, pl.ds(chunk * ROWS, ROWS)]

    def b_send(direction, step, chunk):
        dz = (5 - step) * (1 if direction == 0 else -1)
        send(
            opart(dz, chunk),
            ocame(direction, step, chunk),
            ID_B + direction * 8 + (step - 1) * 2 + chunk,
            z_next if direction == 0 else z_prev,
        )

    def b_arrived(direction, step, chunk):
        arrived(
            ocame(direction, step, chunk),
            ID_B + direction * 8 + (step - 1) * 2 + chunk,
            z_next if direction == 0 else z_prev,
        )

    def b_start():
        for direction in range(2):
            b_send(direction, 1, direction)
            b_send(direction, 2, 1 - direction)

    def b_forward(step, chunk):
        for direction in range(2):
            if step == 1 and chunk != direction:
                continue
            b_arrived(direction, step, chunk)
            dz = (4 - step) * (1 if direction == 0 else -1)
            accumulate(opart(dz, chunk), ocame(direction, step, chunk))
            b_send(direction, step + 1, chunk)

    def loop(first, count, action):
        def step(d, carry):
            action(d)
            return carry

        lax.fori_loop(first, count, step, 0)

    arrived(s.gm_mate, ID_GM, mate)
    gm = s.gm_part[half(k), :] + s.gm_mate[...]
    s.grad_out[...] = gm * ql[...].astype(F32)
    gather_state(s.grad_out, s.up0, s.b_own, True)
    send(s.b_own, s.b_mate, ID_SB1, mate)
    gql[...] = gm * s.li_out[...]
    store(gql, 4)
    lax.fori_loop(0, n_z, share, 0)
    b_start()
    arrived(s.b_mate, ID_SB1, mate)
    chip_state(s.b_own, s.b_mate, s.b_chip, s.b_slots, ID_SB2, True)
    s.spec[...] = conj_times(s.long_spec[...], transform(s.grad_out[...]))
    d_middle(3)
    s.o_sum[...] = lax.dot_general(
        s.mixed[...],
        wg[pl.ds(2 * z, 2)].reshape(2 * ROWS, COLS),
        (((1,), (1,)), ((), ())),
        preferred_element_type=F32,
    )
    d_middle(2)
    b_forward(1, 0)
    b_forward(1, 1)
    s.grad_out[...] = inverse(s.spec[...]) + skip[...] * s.grad_out[...]
    d_middle(1)
    d_middle(0)

    b_sent = chip_finish(s.b_chip, s.b_slots, ID_SB2, ID_SB3, s.b_in, True)
    b_forward(2, 0)
    b_forward(2, 1)
    arrived(s.b_in.at[other8], ID_SB3, mate)
    s.enter[...] = jnp.where(
        k == 1, s.b_in[...], s.dev_decay[...] * s.b_in[...] + s.b_mate[...]
    )
    spread(s.c8, s.enter, s.work, True)
    gli = s.grad_out[...] + s.work[...]
    gkl[...] = gli * s.mixed_mr[...].astype(F32)
    gmm = gli * kl[...].astype(F32)
    gqm[...] = gmm * s.mr_conv[...]
    gconv = gmm * qm[...].astype(F32)
    s.work[...] = gconv
    s.grad_halo[...] = gconv.astype(BF)
    back = copy(s.grad_halo, s.after, ID_BACK_HALO, prv)

    @pl.when(me > 0)
    def _():
        back.start()

    store(gkl, 5)
    store(gqm, 1)

    spec = transform(s.work[...])
    s.spec[...] = spec
    s.t_own[...] = inverse(conj_times(s.prod_spec[...], spec))
    th = ROWS // 2

    def trows(core):
        return pl.ds(pl.multiple_of(core * th, th), th)

    send(s.t_own.at[trows(1 - k)], s.t_mate, ID_T1, mate)
    arrived(s.t_mate, ID_T1, mate)
    s.t_half[...] = s.t_own[trows(k), :] + s.t_mate[...]

    def piece(c, base):
        rows = pl.ds(pl.multiple_of(base + lax.div(c, 2) * 8, 8), 8)
        lanes = pl.ds(pl.multiple_of(lax.rem(c, 2) * 256, 256), 256)
        return rows, lanes

    def t2_copy(d):
        to = chip_off(d)
        rows, lanes = piece(to, 0)
        return copy(s.t_half.at[rows, lanes], s.t_slots.at[d], ID_T2 + d, plane(to, k))

    for d in range(1, CHIPS):
        t2_copy(d).start()
    d_end(3)
    d_turn()
    b_forward(3, 0)
    b_forward(3, 1)
    d_end(2)
    d_end(1)
    d_turn_middle()

    @pl.when(me == last)
    def _():
        s.after[...] = jnp.zeros((ROWS, COLS), BF)

    @pl.when(me < last)
    def _():
        back.wait_recv()

    n = s.after[...]
    spec = s.spec[...] - dot(past2[...], jnp.concatenate([n, n], axis=0))
    gp = inverse(conj_times(s.tap_spec[...], spec))
    gkm[...] = gp * vm[...].astype(F32)
    gvm[...] = gp * km[...].astype(F32)
    store(gkm, 2)
    store(gvm, 3)

    loop(1, CHIPS, lambda d: t2_copy(d).wait_recv())
    rows, lanes = piece(chip, 0)
    total = s.t_half[rows, lanes]
    for d in range(1, CHIPS):
        total = total + s.t_slots[d]
    total = total * grad_scale
    s.t_done[...] = total
    rows, lanes = piece(chip, k * th)
    s.t_all[rows, lanes] = total

    def t3_copy(d):
        return copy(s.t_done, s.t_all.at[rows, lanes], ID_T3 + d, plane(chip_off(d), k))

    def t3_arrived(d):
        rows_from, lanes_from = piece(chip_off(-d), k * th)
        copy(s.t_done, s.t_all.at[rows_from, lanes_from], ID_T3 + d, plane(chip_off(d), k)).wait_recv()

    for d in range(1, CHIPS):
        t3_copy(d).start()

    for direction in range(2):
        for chunk in range(2):
            b_arrived(direction, 4, chunk)
    s.o_sum[...] = s.o_sum[...] + s.o_came[3].astype(F32) + s.o_came[7].astype(F32)
    send(s.o_sum.at[half(1 - k)], s.o_mate, ID_OUT, mate)

    total = d_sum(0)
    arrived(s.dw_from_prev2, ID_D2 + 2, a_next)
    arrived(s.dw_from_next2, ID_D2 + 3, a_prev)
    total = total + s.dw_from_prev2[...].astype(F32) + s.dw_from_next2[...].astype(F32)
    gw[...] = total * grad_scale
    store(gw, 7)

    arrived(s.o_mate, ID_OUT, mate)
    for h in range(2):
        mine = pl.ds(pl.multiple_of((2 * h + k) * LANES, LANES), LANES)
        theirs = pl.ds(pl.multiple_of((2 * h + 1 - k) * LANES, LANES), LANES)
        out[:, mine] = s.o_sum[half(k), h * LANES : (h + 1) * LANES]
        out[:, theirs] = s.o_mate[:, h * LANES : (h + 1) * LANES]
    store(out, 0)

    loop(1, CHIPS, t3_arrived)
    send(s.t_all.at[trows(k)], s.t_all.at[trows(k)], ID_T4, mate)
    arrived(s.t_all.at[trows(1 - k)], ID_T4, mate)
    store(s.t_all, 6)

    for c in stored:
        c.wait()
    for c in pending:
        c.wait_send()
    f_sent()
    b_sent()
    loop(1, CHIPS, lambda d: t2_copy(d).wait_send())
    loop(1, CHIPS, lambda d: t3_copy(d).wait_send())

    @pl.when(me < last)
    def _():
        halo.wait_send()

    @pl.when(me > 0)
    def _():
        back.wait_send()


def shards(query_mr, key_mr, value_mr, query_li, key_li, mr_taps, li_time, li_residue, li_skip, out_weight, cotangent):
    consts = [jnp.asarray(m) for m in transforms()]
    args = (
        key_mr,
        value_mr,
        cotangent,
        out_weight,
        mr_taps,
        li_time,
        li_residue,
        query_mr,
        key_li,
        query_li,
        li_skip.reshape(1, COLS),
        *consts,
    )
    block = jax.ShapeDtypeStruct((ROWS, COLS), F32)
    hbm = pl.BlockSpec(memory_space=pltpu.HBM)
    results = pl.pallas_call(
        kernel,
        out_shape=(block,) * 8,
        in_specs=[hbm] * len(args),
        out_specs=(hbm,) * 8,
        scratch_shapes=[pltpu.VMEM(shape, kind) for shape, kind in INPUTS + tuple(SCRATCH.values())]
        + [pltpu.SemaphoreType.DMA((ID_COUNT,)), pltpu.SemaphoreType.DMA((ID_COUNT,)), pltpu.SemaphoreType.DMA((len(INPUTS),)), pltpu.SemaphoreType.DMA((8,))],
        compiler_params=pltpu.CompilerParams(
            collective_id=0, has_side_effects=True, vmem_limit_bytes=60 * 1024 * 1024
        ),
        cost_estimate=pl.CostEstimate(flops=3_000_000_000, bytes_accessed=4_000_000, transcendentals=1_000_000),
    )(*args)
    return pl.pallas_call(
        write_out,
        out_shape=(block,) * 8,
        in_specs=[hbm] * 8,
        out_specs=(hbm,) * 8,
        scratch_shapes=[
            pltpu.VMEM((8, ROWS, COLS), F32),
            pltpu.SemaphoreType.DMA((8,)),
            pltpu.SemaphoreType.DMA((8,)),
        ],
        compiler_params=pltpu.CompilerParams(vmem_limit_bytes=60 * 1024 * 1024),
        cost_estimate=pl.CostEstimate(flops=0, bytes_accessed=4_000_000, transcendentals=0),
    )(*results)


def write_out(*refs):
    held, load_sem, store_sem = refs[16:]
    loads = [pltpu.make_async_copy(refs[i], held.at[i], load_sem.at[i]) for i in range(8)]
    stores = [pltpu.make_async_copy(held.at[i], refs[8 + i], store_sem.at[i]) for i in range(8)]
    for c in loads:
        c.start()
    for load, store in zip(loads, stores):
        load.wait()
        store.start()
    for c in stores:
        c.wait()


def solution(mesh):
    rows = P("ctx", "fsdp")
    wide = P(None, "fsdp")
    return jax.shard_map(
        shards,
        mesh=mesh,
        in_specs=(rows, rows, rows, rows, rows, wide, wide, wide, P("fsdp"), rows, rows),
        out_specs=(rows, rows, rows, rows, rows, rows, wide, rows),
        check_vma=False,
    )
```

```python
import math
import types

import jax
import jax.numpy as jnp
import ml_dtypes
import numpy as np
from jax import lax
from jax.experimental import pallas as pl
from jax.experimental.pallas import tpu as pltpu
from jax.sharding import PartitionSpec as P

BF = jnp.bfloat16
F32 = jnp.float32
MESH = pl.DeviceIdType.MESH
ROWS = 128
COLS = 512
MODES = 16
RING = 4
CHIPS = RING * RING
LANES = 128
GROUPS = COLS // LANES


def split_const(m):
    hi = m.astype(ml_dtypes.bfloat16)
    lo = (m - hi.astype(np.float64)).astype(ml_dtypes.bfloat16)
    return hi, lo


def transforms():
    theta = 2.0 * np.pi * (np.arange(ROWS) + 0.5)[:, None] / (2 * ROWS)

    def forward(places):
        return np.concatenate([np.cos(theta * places), -np.sin(theta * places)], axis=0)

    here = forward(np.arange(ROWS)[None, :].astype(np.float64))
    past = forward(np.arange(-ROWS, 0)[None, :].astype(np.float64))
    here_hi, here_lo = split_const(here)
    past_hi, past_lo = split_const(past)
    back_hi, back_lo = split_const(here.T / ROWS)
    return (
        np.concatenate([here_hi, here_hi, here_lo], axis=1),
        np.concatenate([past_hi, past_lo], axis=1),
        np.concatenate([back_hi, back_hi, back_lo], axis=1),
    )


def dot(a, b):
    return jnp.dot(a, b, preferred_element_type=F32)


def split3(v):
    hi = v.astype(BF)
    lo = (v - hi.astype(F32)).astype(BF)
    return jnp.concatenate([hi, lo, hi], axis=0)


def times(a, b):
    ar, ai, br, bi = a[:ROWS], a[ROWS:], b[:ROWS], b[ROWS:]
    return jnp.concatenate([ar * br - ai * bi, ar * bi + ai * br], axis=0)


def conj_times(a, b):
    ar, ai, br, bi = a[:ROWS], a[ROWS:], b[:ROWS], b[ROWS:]
    return jnp.concatenate([ar * br + ai * bi, ar * bi - ai * br], axis=0)


ID_A1 = 0
ID_A2 = 4
ID_C = 20
ID_HALO = 38
ID_BACK_HALO = 39
ID_SF1 = 40
ID_SF3 = 41
ID_SB1 = 42
ID_SB3 = 43
ID_MIX = 44
ID_GM = 45
ID_OUT = 46
ID_T1 = 47
ID_T4 = 48
ID_SF2 = 49
ID_SB2 = 65
ID_T2 = 81
ID_T3 = 97
ID_D1 = 113
ID_D2 = 129
ID_B = 133
ID_CR = 149
ID_COUNT = 181

SCRATCH = dict(
    product=((ROWS, COLS), BF),
    prev=((ROWS, COLS), BF),
    grad_halo=((ROWS, COLS), BF),
    after=((ROWS, COLS), BF),
    wg=((CHIPS, ROWS, COLS), BF),
    cg=((8, 2 * ROWS, 256), BF),
    mixed=((2 * ROWS, COLS), BF),
    mixed_mr=((ROWS, COLS), BF),
    tap_spec=((2 * ROWS, COLS), F32),
    long_spec=((2 * ROWS, COLS), F32),
    prod_spec=((2 * ROWS, COLS), F32),
    mr_conv=((ROWS, COLS), F32),
    signal=((ROWS, COLS), F32),
    li_out=((ROWS, COLS), F32),
    work=((ROWS, COLS), F32),
    d8=((MODES, 8, COLS), F32),
    up0=((MODES, 8, COLS), F32),
    up7=((MODES, 8, COLS), F32),
    c0=((MODES, 8, COLS), F32),
    c1=((MODES, 8, COLS), F32),
    c8=((MODES, 8, COLS), F32),
    dev_decay=((MODES, COLS), F32),
    chip_decay=((MODES, COLS), F32),
    f_own=((MODES, COLS), F32),
    f_mate=((MODES, COLS), F32),
    f_chip=((8, COLS), F32),
    f_slots=((CHIPS, 8, COLS), F32),
    f_in=((MODES, COLS), F32),
    b_own=((MODES, COLS), F32),
    b_mate=((MODES, COLS), F32),
    b_chip=((8, COLS), F32),
    b_slots=((CHIPS, 8, COLS), F32),
    b_in=((MODES, COLS), F32),
    enter=((MODES, COLS), F32),
    gm_part=((2 * ROWS, COLS), F32),
    gm_mate=((ROWS, COLS), F32),
    spec=((2 * ROWS, COLS), F32),
    grad_out=((ROWS, COLS), F32),
    dw_part=((CHIPS, ROWS, COLS), BF),
    dw_half=((RING, ROWS, COLS), BF),
    dw_from_prev=((RING, ROWS, COLS), BF),
    dw_from_next=((RING, ROWS, COLS), BF),
    dw_ring=((RING, ROWS, COLS), BF),
    dw_half2=((ROWS, COLS), BF),
    dw_from_prev2=((ROWS, COLS), BF),
    dw_from_next2=((ROWS, COLS), BF),
    o_part=((8, 2 * ROWS, 256), BF),
    o_came=((8, 2 * ROWS, 256), BF),
    o_sum=((2 * ROWS, 256), F32),
    o_mate=((ROWS, 256), F32),
    t_own=((ROWS, COLS), F32),
    t_mate=((ROWS // 2, COLS), F32),
    t_half=((ROWS // 2, COLS), F32),
    t_slots=((CHIPS, 8, 256), F32),
    t_done=((8, 256), F32),
    t_all=((ROWS, COLS), F32),
    out=((ROWS, COLS), F32),
    gqm=((ROWS, COLS), F32),
    gkm=((ROWS, COLS), F32),
    gvm=((ROWS, COLS), F32),
    gql=((ROWS, COLS), F32),
    gkl=((ROWS, COLS), F32),
    gw=((ROWS, COLS), F32),
)


INPUTS = (
    ((ROWS, COLS), BF),
    ((ROWS, COLS), BF),
    ((ROWS, COLS), BF),
    ((ROWS, COLS), BF),
    ((ROWS, COLS), F32),
    ((MODES, COLS), F32),
    ((MODES, COLS), F32),
    ((ROWS, COLS), BF),
    ((ROWS, COLS), BF),
    ((ROWS, COLS), BF),
    ((1, COLS), F32),
    ((2 * ROWS, 3 * ROWS), BF),
    ((2 * ROWS, 2 * ROWS), BF),
    ((ROWS, 6 * ROWS), BF),
)


def kernel(*refs):
    n_in = len(INPUTS)
    given = refs[:n_in]
    results = refs[n_in : n_in + 8]
    held = refs[n_in + 8 : n_in + 8 + n_in]
    (km, vm, cot, w, taps, time, residue, qm, kl, ql, skip, fwd3, past2, inv3) = held
    s = types.SimpleNamespace(**dict(zip(SCRATCH, refs[2 * n_in + 8 :])))
    out, gqm, gkm, gvm, gql, gkl, gw = s.out, s.gqm, s.gkm, s.gvm, s.gql, s.gkl, s.gw
    snd, rcv, ld, st = refs[2 * n_in + 8 + len(SCRATCH) :]

    def load(i):
        return pltpu.make_async_copy(given[i], held[i], ld.at[i])

    for i in range(n_in):
        load(i).start()

    stored = []

    def store(source, i):
        c = pltpu.make_async_copy(source, results[i], st.at[i])
        c.start()
        stored.append(c)

    n_z = 8
    grad_scale = 1.0 / math.sqrt(ROWS * 2 * CHIPS)
    me = lax.axis_index("ctx")
    z = lax.axis_index("fsdp")
    k = lax.rem(me, 2)
    chip = lax.div(me, 2)
    x, y = lax.div(chip, RING), lax.rem(chip, RING)
    a = x * (1 - k) + y * k
    b = y * (1 - k) + x * k

    def ring(v, by):
        return lax.rem(v + by + RING, RING)

    def at(pa, pb):
        return (pa * RING + pb) * (1 - k) + (pb * RING + pa) * k

    def plane(c, core):
        return (c * 2 + core, z)

    mate = (chip * 2 + (1 - k), z)

    def up(dz):
        return (me, lax.rem(z + dz + n_z, n_z))

    def copy(src, dst, i, to):
        return pltpu.make_async_remote_copy(
            src_ref=src, dst_ref=dst, send_sem=snd.at[i], recv_sem=rcv.at[i], device_id=to, device_id_type=MESH
        )

    pending = []

    def send(src, dst, i, to):
        c = copy(src, dst, i, to)
        c.start()
        pending.append(c)

    def arrived(dst, i, to):
        copy(dst, dst, i, to).wait_recv()

    def half(h):
        return pl.ds(pl.multiple_of(h * ROWS, ROWS), ROWS)

    def chip_off(by):
        return lax.rem(chip + by + CHIPS, CHIPS)

    barrier = pltpu.get_barrier_semaphore()
    pl.semaphore_signal(barrier, inc=1, device_id=mate, device_id_type=MESH)

    def greet_chip(d, carry):
        pl.semaphore_signal(barrier, inc=1, device_id=plane(chip_off(d), k), device_id_type=MESH)
        return carry

    lax.fori_loop(1, CHIPS, greet_chip, 0)

    for d in (1, -1):
        pl.semaphore_signal(barrier, inc=1, device_id=up(d), device_id_type=MESH)
    last = 2 * CHIPS - 1
    across = (me + 2 * k - 1, z)

    @pl.when((me > 0) & (me < last))
    def _():
        pl.semaphore_signal(barrier, inc=1, device_id=across, device_id_type=MESH)

    for i in range(4):
        load(i).wait()
    s.product[...] = (km[...].astype(F32) * vm[...].astype(F32)).astype(BF)
    for h in range(2):
        s.cg[z, half(k), h * LANES : (h + 1) * LANES] = cot[
            :, pl.ds(pl.multiple_of((2 * h + k) * LANES, LANES), LANES)
        ]
    s.wg[chip] = w[...]

    peers = 1 + (CHIPS - 1) + 2

    @pl.when((me == 0) | (me == last))
    def _():
        pl.semaphore_wait(barrier, peers)

    @pl.when((me > 0) & (me < last))
    def _():
        pl.semaphore_wait(barrier, peers + 1)

    nxt = (lax.rem(me + 1, last + 1), z)
    prv = (lax.rem(me + last, last + 1), z)

    halo = copy(s.product, s.prev, ID_HALO, nxt)

    @pl.when(me < last)
    def _():
        halo.start()

    a_next, a_prev = plane(at(ring(a, 1), b), k), plane(at(ring(a, -1), b), k)
    b_next, b_prev = plane(at(a, ring(b, 1)), k), plane(at(a, ring(b, -1)), k)
    a_over, b_over = plane(at(ring(a, 2), b), k), plane(at(a, ring(b, 2)), k)
    low, high = pl.ds(0, ROWS // 2), pl.ds(ROWS // 2, ROWS // 2)
    wg = s.wg

    def wblock(ra, rb):
        return wg.at[at(ring(a, ra), ring(b, rb))]

    REL = (0, -1, 1, 2)

    def a2_send(j):
        block = wblock(REL[j], 0)
        if j == 3:
            send(block, block, ID_A2 + 4 * j + 2, b_over)
        send(block, block, ID_A2 + 4 * j, b_next)
        send(block, block, ID_A2 + 4 * j + 1, b_prev)

    def a1_send():
        block = wblock(0, 0)
        send(block, block, ID_A1 + 2, a_over)
        send(block, block, ID_A1, a_next)
        send(block, block, ID_A1 + 1, a_prev)

    def a1_forward():
        arrived(wblock(1, 0), ID_A1 + 1, a_prev)
        a2_send(2)
        arrived(wblock(-1, 0), ID_A1, a_next)
        a2_send(1)

    def a1_finish():
        arrived(wblock(2, 0), ID_A1 + 2, a_over)
        a2_send(3)

    def a2_forward(j):
        block = wblock(REL[j], 1)
        arrived(block, ID_A2 + 4 * j + 1, b_prev)
        send(block, block, ID_A2 + 4 * j + 3, b_prev)

    def a2_finish(j):
        arrived(wblock(REL[j], -1), ID_A2 + 4 * j, b_next)
        if j == 3:
            arrived(wblock(REL[j], 1), ID_A2 + 4 * j + 1, b_prev)
            arrived(wblock(REL[j], 2), ID_A2 + 4 * j + 2, b_over)
        else:
            arrived(wblock(REL[j], 2), ID_A2 + 4 * j + 3, b_prev)

    cg = s.cg
    z_next, z_prev = up(1), up(-1)

    def cblock(rz, chunk):
        core = k if chunk < 2 else 1 - k
        rows = pl.ds(pl.multiple_of(core * ROWS + chunk % 2 * 64, 64), 64)
        return cg.at[lax.rem(z + rz + n_z, n_z), rows]

    def c_id(direction, step, chunk):
        return ID_CR + direction * 16 + (step - 1) * 4 + chunk

    def c_send(direction, step, chunk):
        block = cblock(1 - step if direction == 0 else step - 1, chunk)
        send(block, block, c_id(direction, step, chunk), z_prev if direction else z_next)

    def c_mate_refs(h, core):
        return cg.at[z, half(k if core else 1 - k), pl.ds(h * LANES, LANES)]

    def c_start():
        for h in range(2):
            send(
                cot.at[:, pl.ds(pl.multiple_of((2 * h + 1 - k) * LANES, LANES), LANES)],
                c_mate_refs(h, True),
                ID_C + h,
                mate,
            )
        for chunk in range(2):
            for direction in range(2):
                c_send(direction, 1, chunk)

    def c_second():
        for h in range(2):
            arrived(c_mate_refs(h, False), ID_C + h, mate)
        for chunk in (2, 3):
            for direction in range(2):
                c_send(direction, 1, chunk)

    def c_forward(step, chunk):
        for direction in range(2):
            rz = step if direction else -step
            arrived(cblock(rz, chunk), c_id(direction, step, chunk), z_prev if direction else z_next)
            if step < 3 or chunk % 2 == direction:
                c_send(direction, step + 1, chunk)

    def c_finish():
        for chunk in range(4):
            direction = chunk % 2
            arrived(cblock(4, chunk), c_id(direction, 4, chunk), z_prev if direction else z_next)

    a1_send()
    c_start()
    a2_send(0)

    for i in range(4, n_in):
        load(i).wait()

    within = lax.broadcasted_iota(jnp.int32, (1, 8, LANES), 1).astype(F32)

    def tables(g, carry):
        lanes = pl.ds(pl.multiple_of(g * LANES, LANES), LANES)
        rate = 1.0 / time[:, lanes]
        u = 2.0 * rate
        series = 1.0 - u * (1.0 / 7.0)
        for n in (6, 5, 4, 3, 2):
            series = 1.0 - u * (1.0 / n) * series
        coef = residue[:, lanes] * jnp.sqrt(u * series)
        s.dev_decay[:, lanes] = jnp.exp(-rate * ROWS)
        s.chip_decay[:, lanes] = jnp.exp(-rate * (2 * ROWS))
        r3 = jnp.broadcast_to(rate[:, None, :], (MODES, 8, LANES))
        c3 = jnp.broadcast_to(coef[:, None, :], (MODES, 8, LANES))
        s.d8[:, :, lanes] = jnp.exp(-r3 * 8.0)
        up0 = jnp.exp(-r3 * within)
        s.up0[:, :, lanes] = up0
        s.up7[:, :, lanes] = jnp.exp(-r3 * (7.0 - within))
        s.c0[:, :, lanes] = c3 * up0
        s.c1[:, :, lanes] = c3 * jnp.exp(-r3 * (within + 1.0))
        s.c8[:, :, lanes] = c3 * jnp.exp(-r3 * (8.0 - within))
        return carry

    lax.fori_loop(0, GROUPS, tables, 0, unroll=True)

    def spread(table, state, target, descending):
        def one(g, carry):
            lanes = pl.ds(pl.multiple_of(g * LANES, LANES), LANES)
            d8 = s.d8[:, :, lanes]
            v = table[:, :, lanes]
            if state is not None:
                v = v * jnp.broadcast_to(state[:, lanes][:, None, :], (MODES, 8, LANES))
            for t in range(ROWS // 8):
                tile = ROWS // 8 - 1 - t if descending else t
                target[tile * 8 : tile * 8 + 8, lanes] = jnp.sum(v, axis=0)
                if t < ROWS // 8 - 1:
                    v = v * d8
            return carry

        lax.fori_loop(0, GROUPS, one, 0, unroll=True)

    def gather_state(source, table, target, descending):
        def one(g, carry):
            lanes = pl.ds(pl.multiple_of(g * LANES, LANES), LANES)
            d8 = s.d8[:, :, lanes]
            v = jnp.zeros((MODES, 8, LANES), F32)
            for t in range(ROWS // 8):
                tile = ROWS // 8 - 1 - t if descending else t
                rows = source[tile * 8 : tile * 8 + 8, lanes][None]
                v = v * d8 + rows if t else v + rows
            target[:, lanes] = jnp.sum(v * table[:, :, lanes], axis=1)
            return carry

        lax.fori_loop(0, GROUPS, one, 0, unroll=True)

    def transform(v):
        return dot(fwd3[...], split3(v))

    def inverse(v):
        return dot(inv3[...], split3(v))

    c_second()
    s.tap_spec[...] = transform(taps[...])
    spread(s.c0, None, s.work, False)
    c_forward(1, 0)
    c_forward(1, 1)
    a1_forward()
    c_forward(1, 2)
    a2_forward(0)
    c_forward(1, 3)
    s.long_spec[...] = transform(s.work[...])

    @pl.when(me > 0)
    def _():
        halo.wait_recv()

    @pl.when(me == 0)
    def _():
        s.prev[...] = jnp.zeros((ROWS, COLS), BF)

    here2 = jnp.concatenate([fwd3[:, :ROWS], fwd3[:, 2 * ROWS :]], axis=1)
    p, q = s.product[...], s.prev[...]
    s.prod_spec[...] = dot(here2, jnp.concatenate([p, p], axis=0)) + dot(
        past2[...], jnp.concatenate([q, q], axis=0)
    )
    a1_finish()
    c_forward(2, 0)
    s.mr_conv[...] = inverse(times(s.prod_spec[...], s.tap_spec[...]))
    mixed_mr = (qm[...].astype(F32) * s.mr_conv[...]).astype(BF)
    s.mixed_mr[...] = mixed_mr
    s.signal[...] = (kl[...].astype(F32) * mixed_mr.astype(F32)).astype(BF).astype(F32)

    own8 = pl.ds(pl.multiple_of(k * 8, 8), 8)

    def chip_state(own, theirs, into, slots, id2, descending):
        decay = s.dev_decay[own8, :]
        mine, other = own[own8, :], theirs[own8, :]
        near = jnp.where(k == 0, mine, other)
        far = jnp.where(k == 0, other, mine)
        into[...] = near + decay * far if descending else decay * near + far
        sign = -1 if descending else 1
        ahead = chip if descending else CHIPS - 1 - chip

        def put(d, carry):
            @pl.when(d <= ahead)
            def _():
                copy(into, slots.at[d], id2 + d, plane(chip_off(sign * d), k)).start()

            return carry

        for d in range(1, CHIPS):
            put(d, 0)

    def chip_finish(into, slots, id2, id3, target, descending):
        sign = -1 if descending else 1
        ahead = chip if descending else CHIPS - 1 - chip
        behind = CHIPS - 1 - chip if descending else chip

        def take(d, carry):
            @pl.when(d <= behind)
            def _():
                copy(into, slots.at[d], id2 + d, plane(chip_off(sign * d), k)).wait_recv()

            return carry

        for d in range(1, CHIPS):
            take(d, 0)
        decay = s.chip_decay[own8, :]
        total = jnp.zeros((8, COLS), F32)
        for d in range(CHIPS - 1, 0, -1):
            total = jnp.where(d <= behind, total * decay + slots[d], 0.0)
        target[own8, :] = total
        send(target.at[own8], target.at[own8], id3, mate)

        def sent(d, carry):
            @pl.when(d <= ahead)
            def _():
                copy(into, slots.at[d], id2 + d, plane(chip_off(sign * d), k)).wait_send()

            return carry

        return lambda: lax.fori_loop(1, CHIPS, sent, 0)

    other8 = pl.ds(pl.multiple_of((1 - k) * 8, 8), 8)

    c_forward(2, 1)
    c_forward(2, 2)
    gather_state(s.signal, s.up7, s.f_own, False)
    send(s.f_own, s.f_mate, ID_SF1, mate)
    c_forward(2, 3)
    a2_forward(2)
    a2_forward(1)
    arrived(s.f_mate, ID_SF1, mate)
    chip_state(s.f_own, s.f_mate, s.f_chip, s.f_slots, ID_SF2, False)
    c_forward(3, 0)
    c_forward(3, 1)
    spectrum = times(transform(s.signal[...]), s.long_spec[...])
    c_forward(3, 2)
    c_forward(3, 3)
    s.li_out[...] = inverse(spectrum) + skip[...] * s.signal[...]

    f_sent = chip_finish(s.f_chip, s.f_slots, ID_SF2, ID_SF3, s.f_in, False)
    arrived(s.f_in.at[other8], ID_SF3, mate)
    s.enter[...] = jnp.where(k == 0, s.f_in[...], s.dev_decay[...] * s.f_in[...] + s.f_mate[...])
    spread(s.c1, s.enter, s.work, False)
    s.li_out[...] = s.li_out[...] + s.work[...]
    s.mixed[half(k), :] = (ql[...].astype(F32) * s.li_out[...]).astype(BF)
    send(s.mixed.at[half(k)], s.mixed.at[half(k)], ID_MIX, mate)
    for j in range(4):
        a2_finish(j)
    c_finish()

    s.gm_part[...] = dot(
        jnp.concatenate([cg[j] for j in range(n_z)], axis=1), wg[...].reshape(CHIPS * ROWS, COLS)
    )
    send(s.gm_part.at[half(1 - k)], s.gm_mate, ID_GM, mate)

    arrived(s.mixed.at[half(1 - k)], ID_MIX, mate)

    def project(j, carry):
        part = lax.dot_general(
            cg[j], s.mixed[...], (((0,), (0,)), ((), ())), preferred_element_type=F32
        ).astype(BF)
        s.dw_part[2 * j] = part[:ROWS]
        s.dw_part[2 * j + 1] = part[ROWS:]
        return carry

    lax.fori_loop(0, n_z, project, 0, unroll=True)

    def dpart(ra, rb):
        return s.dw_part.at[at(ring(a, ra), ring(b, rb))]

    def drows(ra, rb, rows):
        return s.dw_part.at[at(ring(a, ra), ring(b, rb)), rows]

    def accumulate(target, came):
        target[...] = (target[...].astype(F32) + came[...].astype(F32)).astype(BF)

    def d_start(j):
        ra, i = REL[j], ID_D1 + 4 * j
        send(drows(ra, 2, low), s.dw_half.at[j, low], i, b_next)
        send(drows(ra, 2, high), s.dw_half.at[j, high], i + 1, b_prev)

    def d_middle(j):
        ra, i = REL[j], ID_D1 + 4 * j
        arrived(s.dw_half.at[j, low], i, b_next)
        accumulate(drows(ra, 1, low), s.dw_half.at[j, low])
        send(dpart(ra, 1), s.dw_from_prev.at[j], i + 2, b_next)
        arrived(s.dw_half.at[j, high], i + 1, b_prev)
        accumulate(drows(ra, -1, high), s.dw_half.at[j, high])
        send(dpart(ra, -1), s.dw_from_next.at[j], i + 3, b_prev)

    def d_sum(j):
        ra, i = REL[j], ID_D1 + 4 * j
        arrived(s.dw_from_prev.at[j], i + 2, b_next)
        arrived(s.dw_from_next.at[j], i + 3, b_prev)
        return (
            dpart(ra, 0)[...].astype(F32)
            + s.dw_from_prev[j].astype(F32)
            + s.dw_from_next[j].astype(F32)
        )

    def d_end(j):
        s.dw_ring[j] = d_sum(j).astype(BF)

    def d_turn():
        send(s.dw_ring.at[3, low], s.dw_half2.at[low], ID_D2, a_next)
        send(s.dw_ring.at[3, high], s.dw_half2.at[high], ID_D2 + 1, a_prev)

    def d_turn_middle():
        arrived(s.dw_half2.at[low], ID_D2, a_next)
        accumulate(s.dw_ring.at[2, low], s.dw_half2.at[low])
        send(s.dw_ring.at[2], s.dw_from_prev2, ID_D2 + 2, a_next)
        arrived(s.dw_half2.at[high], ID_D2 + 1, a_prev)
        accumulate(s.dw_ring.at[1, high], s.dw_half2.at[high])
        send(s.dw_ring.at[1], s.dw_from_next2, ID_D2 + 3, a_prev)

    for j in (3, 2, 1, 0):
        d_start(j)

    def share(j, carry):
        block = wg[pl.ds(2 * j, 2)].reshape(2 * ROWS, COLS)
        s.o_part[j] = lax.dot_general(
            s.mixed[...], block, (((1,), (1,)), ((), ())), preferred_element_type=F32
        ).astype(BF)
        return carry

    def opart(dz, chunk):
        return s.o_part.at[lax.rem(z + dz + n_z, n_z), pl.ds(chunk * ROWS, ROWS)]

    def ocame(direction, step, chunk):
        return s.o_came.at[direction * 4 + step - 1, pl.ds(chunk * ROWS, ROWS)]

    def b_send(direction, step, chunk):
        dz = (5 - step) * (1 if direction == 0 else -1)
        send(
            opart(dz, chunk),
            ocame(direction, step, chunk),
            ID_B + direction * 8 + (step - 1) * 2 + chunk,
            z_next if direction == 0 else z_prev,
        )

    def b_arrived(direction, step, chunk):
        arrived(
            ocame(direction, step, chunk),
            ID_B + direction * 8 + (step - 1) * 2 + chunk,
            z_next if direction == 0 else z_prev,
        )

    def b_start():
        for direction in range(2):
            b_send(direction, 1, direction)
            b_send(direction, 2, 1 - direction)

    def b_forward(step, chunk):
        for direction in range(2):
            if step == 1 and chunk != direction:
                continue
            b_arrived(direction, step, chunk)
            dz = (4 - step) * (1 if direction == 0 else -1)
            accumulate(opart(dz, chunk), ocame(direction, step, chunk))
            b_send(direction, step + 1, chunk)

    def loop(first, count, action):
        for d in range(first, count):
            action(d)

    arrived(s.gm_mate, ID_GM, mate)
    gm = s.gm_part[half(k), :] + s.gm_mate[...]
    s.grad_out[...] = gm * ql[...].astype(F32)
    gather_state(s.grad_out, s.up0, s.b_own, True)
    send(s.b_own, s.b_mate, ID_SB1, mate)
    gql[...] = gm * s.li_out[...]
    store(gql, 4)
    lax.fori_loop(0, n_z, share, 0, unroll=True)
    b_start()
    arrived(s.b_mate, ID_SB1, mate)
    chip_state(s.b_own, s.b_mate, s.b_chip, s.b_slots, ID_SB2, True)
    s.spec[...] = conj_times(s.long_spec[...], transform(s.grad_out[...]))
    d_middle(3)
    s.o_sum[...] = lax.dot_general(
        s.mixed[...],
        wg[pl.ds(2 * z, 2)].reshape(2 * ROWS, COLS),
        (((1,), (1,)), ((), ())),
        preferred_element_type=F32,
    )
    d_middle(2)
    b_forward(1, 0)
    b_forward(1, 1)
    s.grad_out[...] = inverse(s.spec[...]) + skip[...] * s.grad_out[...]
    d_middle(1)
    d_middle(0)

    b_sent = chip_finish(s.b_chip, s.b_slots, ID_SB2, ID_SB3, s.b_in, True)
    b_forward(2, 0)
    b_forward(2, 1)
    arrived(s.b_in.at[other8], ID_SB3, mate)
    s.enter[...] = jnp.where(
        k == 1, s.b_in[...], s.dev_decay[...] * s.b_in[...] + s.b_mate[...]
    )
    spread(s.c8, s.enter, s.work, True)
    gli = s.grad_out[...] + s.work[...]
    gkl[...] = gli * s.mixed_mr[...].astype(F32)
    gmm = gli * kl[...].astype(F32)
    gqm[...] = gmm * s.mr_conv[...]
    gconv = gmm * qm[...].astype(F32)
    s.work[...] = gconv
    s.grad_halo[...] = gconv.astype(BF)
    back = copy(s.grad_halo, s.after, ID_BACK_HALO, prv)

    @pl.when(me > 0)
    def _():
        back.start()

    store(gkl, 5)
    store(gqm, 1)

    spec = transform(s.work[...])
    s.spec[...] = spec
    s.t_own[...] = inverse(conj_times(s.prod_spec[...], spec))
    th = ROWS // 2

    def trows(core):
        return pl.ds(pl.multiple_of(core * th, th), th)

    send(s.t_own.at[trows(1 - k)], s.t_mate, ID_T1, mate)
    arrived(s.t_mate, ID_T1, mate)
    s.t_half[...] = s.t_own[trows(k), :] + s.t_mate[...]

    def piece(c, base):
        rows = pl.ds(pl.multiple_of(base + lax.div(c, 2) * 8, 8), 8)
        lanes = pl.ds(pl.multiple_of(lax.rem(c, 2) * 256, 256), 256)
        return rows, lanes

    def t2_copy(d):
        to = chip_off(d)
        rows, lanes = piece(to, 0)
        return copy(s.t_half.at[rows, lanes], s.t_slots.at[d], ID_T2 + d, plane(to, k))

    for d in range(1, CHIPS):
        t2_copy(d).start()
    d_end(3)
    d_turn()
    b_forward(3, 0)
    b_forward(3, 1)
    d_end(2)
    d_end(1)
    d_turn_middle()

    @pl.when(me == last)
    def _():
        s.after[...] = jnp.zeros((ROWS, COLS), BF)

    @pl.when(me < last)
    def _():
        back.wait_recv()

    n = s.after[...]
    spec = s.spec[...] - dot(past2[...], jnp.concatenate([n, n], axis=0))
    gp = inverse(conj_times(s.tap_spec[...], spec))
    gkm[...] = gp * vm[...].astype(F32)
    gvm[...] = gp * km[...].astype(F32)
    store(gkm, 2)
    store(gvm, 3)

    loop(1, CHIPS, lambda d: t2_copy(d).wait_recv())
    rows, lanes = piece(chip, 0)
    total = s.t_half[rows, lanes]
    for d in range(1, CHIPS):
        total = total + s.t_slots[d]
    total = total * grad_scale
    s.t_done[...] = total
    rows, lanes = piece(chip, k * th)
    s.t_all[rows, lanes] = total

    def t3_copy(d):
        return copy(s.t_done, s.t_all.at[rows, lanes], ID_T3 + d, plane(chip_off(d), k))

    def t3_arrived(d):
        rows_from, lanes_from = piece(chip_off(-d), k * th)
        copy(s.t_done, s.t_all.at[rows_from, lanes_from], ID_T3 + d, plane(chip_off(d), k)).wait_recv()

    for d in range(1, CHIPS):
        t3_copy(d).start()

    for direction in range(2):
        for chunk in range(2):
            b_arrived(direction, 4, chunk)
    s.o_sum[...] = s.o_sum[...] + s.o_came[3].astype(F32) + s.o_came[7].astype(F32)
    send(s.o_sum.at[half(1 - k)], s.o_mate, ID_OUT, mate)

    total = d_sum(0)
    arrived(s.dw_from_prev2, ID_D2 + 2, a_next)
    arrived(s.dw_from_next2, ID_D2 + 3, a_prev)
    total = total + s.dw_from_prev2[...].astype(F32) + s.dw_from_next2[...].astype(F32)
    gw[...] = total * grad_scale
    store(gw, 7)

    arrived(s.o_mate, ID_OUT, mate)
    for h in range(2):
        mine = pl.ds(pl.multiple_of((2 * h + k) * LANES, LANES), LANES)
        theirs = pl.ds(pl.multiple_of((2 * h + 1 - k) * LANES, LANES), LANES)
        out[:, mine] = s.o_sum[half(k), h * LANES : (h + 1) * LANES]
        out[:, theirs] = s.o_mate[:, h * LANES : (h + 1) * LANES]
    store(out, 0)

    loop(1, CHIPS, t3_arrived)
    send(s.t_all.at[trows(k)], s.t_all.at[trows(k)], ID_T4, mate)
    arrived(s.t_all.at[trows(1 - k)], ID_T4, mate)
    store(s.t_all, 6)

    for c in stored:
        c.wait()
    for c in pending:
        c.wait_send()
    f_sent()
    b_sent()
    loop(1, CHIPS, lambda d: t2_copy(d).wait_send())
    loop(1, CHIPS, lambda d: t3_copy(d).wait_send())

    @pl.when(me < last)
    def _():
        halo.wait_send()

    @pl.when(me > 0)
    def _():
        back.wait_send()


def shards(query_mr, key_mr, value_mr, query_li, key_li, mr_taps, li_time, li_residue, li_skip, out_weight, cotangent):
    consts = [jnp.asarray(m) for m in transforms()]
    args = (
        key_mr,
        value_mr,
        cotangent,
        out_weight,
        mr_taps,
        li_time,
        li_residue,
        query_mr,
        key_li,
        query_li,
        li_skip.reshape(1, COLS),
        *consts,
    )
    block = jax.ShapeDtypeStruct((ROWS, COLS), F32)
    hbm = pl.BlockSpec(memory_space=pltpu.HBM)
    results = pl.pallas_call(
        kernel,
        out_shape=(block,) * 8,
        in_specs=[hbm] * len(args),
        out_specs=(hbm,) * 8,
        scratch_shapes=[pltpu.VMEM(shape, kind) for shape, kind in INPUTS + tuple(SCRATCH.values())]
        + [pltpu.SemaphoreType.DMA((ID_COUNT,)), pltpu.SemaphoreType.DMA((ID_COUNT,)), pltpu.SemaphoreType.DMA((len(INPUTS),)), pltpu.SemaphoreType.DMA((8,))],
        compiler_params=pltpu.CompilerParams(
            collective_id=0, has_side_effects=True, vmem_limit_bytes=60 * 1024 * 1024
        ),
        cost_estimate=pl.CostEstimate(flops=3_000_000_000, bytes_accessed=4_000_000, transcendentals=1_000_000),
    )(*args)
    return pl.pallas_call(
        write_out,
        out_shape=(block,) * 8,
        in_specs=[hbm] * 8,
        out_specs=(hbm,) * 8,
        scratch_shapes=[
            pltpu.VMEM((8, ROWS, COLS), F32),
            pltpu.SemaphoreType.DMA((8,)),
            pltpu.SemaphoreType.DMA((8,)),
        ],
        compiler_params=pltpu.CompilerParams(vmem_limit_bytes=60 * 1024 * 1024),
        cost_estimate=pl.CostEstimate(flops=0, bytes_accessed=4_000_000, transcendentals=0),
    )(*results)


def write_out(*refs):
    held, load_sem, store_sem = refs[16:]
    loads = [pltpu.make_async_copy(refs[i], held.at[i], load_sem.at[i]) for i in range(8)]
    stores = [pltpu.make_async_copy(held.at[i], refs[8 + i], store_sem.at[i]) for i in range(8)]
    for c in loads:
        c.start()
    for load, store in zip(loads, stores):
        load.wait()
        store.start()
    for c in stores:
        c.wait()


def solution(mesh):
    rows = P("ctx", "fsdp")
    wide = P(None, "fsdp")
    return jax.shard_map(
        shards,
        mesh=mesh,
        in_specs=(rows, rows, rows, rows, rows, wide, wide, wide, P("fsdp"), rows, rows),
        out_specs=(rows, rows, rows, rows, rows, rows, wide, rows),
        check_vma=False,
    )
```

```python
import math
import types

import jax
import jax.numpy as jnp
import ml_dtypes
import numpy as np
from jax import lax
from jax.experimental import pallas as pl
from jax.experimental.pallas import tpu as pltpu
from jax.sharding import PartitionSpec as P

BF = jnp.bfloat16
F32 = jnp.float32
MESH = pl.DeviceIdType.MESH
ROWS = 128
COLS = 512
MODES = 16
RING = 4
CHIPS = RING * RING
LANES = 128
GROUPS = COLS // LANES


def split_const(m):
    hi = m.astype(ml_dtypes.bfloat16)
    lo = (m - hi.astype(np.float64)).astype(ml_dtypes.bfloat16)
    return hi, lo


def transforms():
    theta = 2.0 * np.pi * (np.arange(ROWS) + 0.5)[:, None] / (2 * ROWS)

    def forward(places):
        return np.concatenate([np.cos(theta * places), -np.sin(theta * places)], axis=0)

    here = forward(np.arange(ROWS)[None, :].astype(np.float64))
    past = forward(np.arange(-ROWS, 0)[None, :].astype(np.float64))
    here_hi, here_lo = split_const(here)
    past_hi, past_lo = split_const(past)
    back_hi, back_lo = split_const(here.T / ROWS)
    return (
        np.concatenate([here_hi, here_hi, here_lo], axis=1),
        np.concatenate([past_hi, past_lo], axis=1),
        np.concatenate([back_hi, back_hi, back_lo], axis=1),
    )


def dot(a, b):
    return jnp.dot(a, b, preferred_element_type=F32)


def split3(v):
    hi = v.astype(BF)
    lo = (v - hi.astype(F32)).astype(BF)
    return jnp.concatenate([hi, lo, hi], axis=0)


def times(a, b):
    ar, ai, br, bi = a[:ROWS], a[ROWS:], b[:ROWS], b[ROWS:]
    return jnp.concatenate([ar * br - ai * bi, ar * bi + ai * br], axis=0)


def conj_times(a, b):
    ar, ai, br, bi = a[:ROWS], a[ROWS:], b[:ROWS], b[ROWS:]
    return jnp.concatenate([ar * br + ai * bi, ar * bi - ai * br], axis=0)


ID_A1 = 0
ID_A2 = 4
ID_C = 20
ID_HALO = 38
ID_BACK_HALO = 39
ID_SF1 = 40
ID_SF3 = 41
ID_SB1 = 42
ID_SB3 = 43
ID_MIX = 44
ID_GM = 45
ID_OUT = 46
ID_T1 = 47
ID_T4 = 48
ID_SF2 = 49
ID_SB2 = 65
ID_T2 = 81
ID_T3 = 97
ID_D1 = 113
ID_D2 = 129
ID_B = 133
ID_CR = 149
ID_COUNT = 181

SCRATCH = dict(
    product=((ROWS, COLS), BF),
    prev=((ROWS, COLS), BF),
    grad_halo=((ROWS, COLS), BF),
    after=((ROWS, COLS), BF),
    wg=((CHIPS, ROWS, COLS), BF),
    cg=((8, 2 * ROWS, 256), BF),
    mixed=((2 * ROWS, COLS), BF),
    mixed_mr=((ROWS, COLS), BF),
    tap_spec=((2 * ROWS, COLS), F32),
    long_spec=((2 * ROWS, COLS), F32),
    prod_spec=((2 * ROWS, COLS), F32),
    mr_conv=((ROWS, COLS), F32),
    signal=((ROWS, COLS), F32),
    li_out=((ROWS, COLS), F32),
    work=((ROWS, COLS), F32),
    d8=((MODES, 8, COLS), F32),
    up0=((MODES, 8, COLS), F32),
    up7=((MODES, 8, COLS), F32),
    c0=((MODES, 8, COLS), F32),
    c1=((MODES, 8, COLS), F32),
    c8=((MODES, 8, COLS), F32),
    dev_decay=((MODES, COLS), F32),
    chip_decay=((MODES, COLS), F32),
    f_own=((MODES, COLS), F32),
    f_mate=((MODES, COLS), F32),
    f_chip=((8, COLS), F32),
    f_slots=((CHIPS, 8, COLS), F32),
    f_in=((MODES, COLS), F32),
    b_own=((MODES, COLS), F32),
    b_mate=((MODES, COLS), F32),
    b_chip=((8, COLS), F32),
    b_slots=((CHIPS, 8, COLS), F32),
    b_in=((MODES, COLS), F32),
    enter=((MODES, COLS), F32),
    gm_part=((2 * ROWS, COLS), F32),
    gm_mate=((ROWS, COLS), F32),
    spec=((2 * ROWS, COLS), F32),
    grad_out=((ROWS, COLS), F32),
    dw_part=((CHIPS, ROWS, COLS), BF),
    dw_half=((RING, ROWS, COLS), BF),
    dw_from_prev=((RING, ROWS, COLS), BF),
    dw_from_next=((RING, ROWS, COLS), BF),
    dw_ring=((RING, ROWS, COLS), BF),
    dw_half2=((ROWS, COLS), BF),
    dw_from_prev2=((ROWS, COLS), BF),
    dw_from_next2=((ROWS, COLS), BF),
    o_part=((8, 2 * ROWS, 256), BF),
    o_came=((8, 2 * ROWS, 256), BF),
    o_sum=((2 * ROWS, 256), F32),
    o_mate=((ROWS, 256), F32),
    t_own=((ROWS, COLS), F32),
    t_mate=((ROWS // 2, COLS), F32),
    t_half=((ROWS // 2, COLS), F32),
    t_slots=((CHIPS, 8, 256), F32),
    t_done=((8, 256), F32),
    t_all=((ROWS, COLS), F32),
    out=((ROWS, COLS), F32),
    gqm=((ROWS, COLS), F32),
    gkm=((ROWS, COLS), F32),
    gvm=((ROWS, COLS), F32),
    gql=((ROWS, COLS), F32),
    gkl=((ROWS, COLS), F32),
    gw=((ROWS, COLS), F32),
)


INPUTS = (
    ((ROWS, COLS), BF),
    ((ROWS, COLS), BF),
    ((ROWS, COLS), BF),
    ((ROWS, COLS), BF),
    ((ROWS, COLS), F32),
    ((MODES, COLS), F32),
    ((MODES, COLS), F32),
    ((ROWS, COLS), BF),
    ((ROWS, COLS), BF),
    ((ROWS, COLS), BF),
    ((1, COLS), F32),
    ((2 * ROWS, 3 * ROWS), BF),
    ((2 * ROWS, 2 * ROWS), BF),
    ((ROWS, 6 * ROWS), BF),
)


def kernel(*refs):
    n_in = len(INPUTS)
    given = refs[:n_in]
    results = refs[n_in : n_in + 8]
    held = refs[n_in + 8 : n_in + 8 + n_in]
    (km, vm, cot, w, taps, time, residue, qm, kl, ql, skip, fwd3, past2, inv3) = held
    s = types.SimpleNamespace(**dict(zip(SCRATCH, refs[2 * n_in + 8 :])))
    out, gqm, gkm, gvm, gql, gkl, gw = s.out, s.gqm, s.gkm, s.gvm, s.gql, s.gkl, s.gw
    snd, rcv, ld, st = refs[2 * n_in + 8 + len(SCRATCH) :]

    def load(i):
        return pltpu.make_async_copy(given[i], held[i], ld.at[i])

    for i in range(n_in):
        load(i).start()

    stored = []

    def store(source, i):
        c = pltpu.make_async_copy(source, results[i], st.at[i])
        c.start()
        stored.append(c)

    n_z = 8
    grad_scale = 1.0 / math.sqrt(ROWS * 2 * CHIPS)
    me = lax.axis_index("ctx")
    z = lax.axis_index("fsdp")
    k = lax.rem(me, 2)
    chip = lax.div(me, 2)
    x, y = lax.div(chip, RING), lax.rem(chip, RING)
    a = x * (1 - k) + y * k
    b = y * (1 - k) + x * k

    def ring(v, by):
        return lax.rem(v + by + RING, RING)

    def at(pa, pb):
        return (pa * RING + pb) * (1 - k) + (pb * RING + pa) * k

    def plane(c, core):
        return (c * 2 + core, z)

    mate = (chip * 2 + (1 - k), z)

    def up(dz):
        return (me, lax.rem(z + dz + n_z, n_z))

    def copy(src, dst, i, to):
        return pltpu.make_async_remote_copy(
            src_ref=src, dst_ref=dst, send_sem=snd.at[i], recv_sem=rcv.at[i], device_id=to, device_id_type=MESH
        )

    pending = []

    def send(src, dst, i, to):
        c = copy(src, dst, i, to)
        c.start()
        pending.append(c)

    def arrived(dst, i, to):
        copy(dst, dst, i, to).wait_recv()

    def half(h):
        return pl.ds(pl.multiple_of(h * ROWS, ROWS), ROWS)

    def chip_off(by):
        return lax.rem(chip + by + CHIPS, CHIPS)

    barrier = pltpu.get_barrier_semaphore()
    pl.semaphore_signal(barrier, inc=1, device_id=mate, device_id_type=MESH)

    def greet_chip(d, carry):
        pl.semaphore_signal(barrier, inc=1, device_id=plane(chip_off(d), k), device_id_type=MESH)
        return carry

    lax.fori_loop(1, CHIPS, greet_chip, 0)

    for d in (1, -1):
        pl.semaphore_signal(barrier, inc=1, device_id=up(d), device_id_type=MESH)
    last = 2 * CHIPS - 1
    across = (me + 2 * k - 1, z)

    @pl.when((me > 0) & (me < last))
    def _():
        pl.semaphore_signal(barrier, inc=1, device_id=across, device_id_type=MESH)

    for i in range(4):
        load(i).wait()
    s.product[...] = (km[...].astype(F32) * vm[...].astype(F32)).astype(BF)
    for h in range(2):
        s.cg[z, half(k), h * LANES : (h + 1) * LANES] = cot[
            :, pl.ds(pl.multiple_of((2 * h + k) * LANES, LANES), LANES)
        ]
    s.wg[chip] = w[...]

    peers = 1 + (CHIPS - 1) + 2

    @pl.when((me == 0) | (me == last))
    def _():
        pl.semaphore_wait(barrier, peers)

    @pl.when((me > 0) & (me < last))
    def _():
        pl.semaphore_wait(barrier, peers + 1)

    nxt = (lax.rem(me + 1, last + 1), z)
    prv = (lax.rem(me + last, last + 1), z)

    halo = copy(s.product, s.prev, ID_HALO, nxt)

    @pl.when(me < last)
    def _():
        halo.start()

    a_next, a_prev = plane(at(ring(a, 1), b), k), plane(at(ring(a, -1), b), k)
    b_next, b_prev = plane(at(a, ring(b, 1)), k), plane(at(a, ring(b, -1)), k)
    a_over = plane(at(ring(a, 2), b), k)
    low, high = pl.ds(0, ROWS // 2), pl.ds(ROWS // 2, ROWS // 2)
    wg = s.wg

    def wblock(ra, rb):
        return wg.at[at(ring(a, ra), ring(b, rb))]

    REL = (0, -1, 1, 2)

    def a2_send(j):
        block = wblock(REL[j], 0)
        send(block, block, ID_A2 + 4 * j, b_next)
        send(block, block, ID_A2 + 4 * j + 1, b_prev)

    def a1_send():
        block = wblock(0, 0)
        send(block, block, ID_A1 + 2, a_over)
        send(block, block, ID_A1, a_next)
        send(block, block, ID_A1 + 1, a_prev)

    def a1_forward():
        arrived(wblock(1, 0), ID_A1 + 1, a_prev)
        a2_send(2)
        arrived(wblock(-1, 0), ID_A1, a_next)
        a2_send(1)

    def a1_finish():
        arrived(wblock(2, 0), ID_A1 + 2, a_over)
        a2_send(3)

    def whalf(ra, rb, rows):
        return wg.at[at(ring(a, ra), ring(b, rb)), rows]

    def a2_forward(j):
        ra, i = REL[j], ID_A2 + 4 * j
        arrived(wblock(ra, 1), i + 1, b_prev)
        if j == 0:
            send(wblock(ra, 1), wblock(ra, 1), i + 3, b_prev)
        else:
            send(whalf(ra, 1, high), whalf(ra, 1, high), i + 3, b_prev)
            arrived(wblock(ra, -1), i, b_next)
            send(whalf(ra, -1, low), whalf(ra, -1, low), i + 2, b_next)

    def a2_finish(j):
        ra, i = REL[j], ID_A2 + 4 * j
        if j == 0:
            arrived(wblock(ra, -1), i, b_next)
            arrived(wblock(ra, 2), i + 3, b_prev)
        else:
            arrived(whalf(ra, 2, high), i + 3, b_prev)
            arrived(whalf(ra, 2, low), i + 2, b_next)

    cg = s.cg
    z_next, z_prev = up(1), up(-1)

    def cblock(rz, chunk):
        core = k if chunk < 2 else 1 - k
        rows = pl.ds(pl.multiple_of(core * ROWS + chunk % 2 * 64, 64), 64)
        return cg.at[lax.rem(z + rz + n_z, n_z), rows]

    def c_id(direction, step, chunk):
        return ID_CR + direction * 16 + (step - 1) * 4 + chunk

    def c_send(direction, step, chunk):
        block = cblock(1 - step if direction == 0 else step - 1, chunk)
        send(block, block, c_id(direction, step, chunk), z_prev if direction else z_next)

    def c_mate_refs(h, core):
        return cg.at[z, half(k if core else 1 - k), pl.ds(h * LANES, LANES)]

    def c_start():
        for h in range(2):
            send(
                cot.at[:, pl.ds(pl.multiple_of((2 * h + 1 - k) * LANES, LANES), LANES)],
                c_mate_refs(h, True),
                ID_C + h,
                mate,
            )
        for chunk in range(2):
            for direction in range(2):
                c_send(direction, 1, chunk)

    def c_second():
        for h in range(2):
            arrived(c_mate_refs(h, False), ID_C + h, mate)
        for chunk in (2, 3):
            for direction in range(2):
                c_send(direction, 1, chunk)

    def c_forward(step, chunk):
        for direction in range(2):
            rz = step if direction else -step
            arrived(cblock(rz, chunk), c_id(direction, step, chunk), z_prev if direction else z_next)
            if step < 3 or chunk % 2 == direction:
                c_send(direction, step + 1, chunk)

    def c_finish():
        for chunk in range(4):
            direction = chunk % 2
            arrived(cblock(4, chunk), c_id(direction, 4, chunk), z_prev if direction else z_next)

    a1_send()
    c_start()
    a2_send(0)

    for i in range(4, n_in):
        load(i).wait()

    within = lax.broadcasted_iota(jnp.int32, (1, 8, LANES), 1).astype(F32)

    def tables(g, carry):
        lanes = pl.ds(pl.multiple_of(g * LANES, LANES), LANES)
        rate = 1.0 / time[:, lanes]
        u = 2.0 * rate
        series = 1.0 - u * (1.0 / 7.0)
        for n in (6, 5, 4, 3, 2):
            series = 1.0 - u * (1.0 / n) * series
        coef = residue[:, lanes] * jnp.sqrt(u * series)
        s.dev_decay[:, lanes] = jnp.exp(-rate * ROWS)
        s.chip_decay[:, lanes] = jnp.exp(-rate * (2 * ROWS))
        r3 = jnp.broadcast_to(rate[:, None, :], (MODES, 8, LANES))
        c3 = jnp.broadcast_to(coef[:, None, :], (MODES, 8, LANES))
        s.d8[:, :, lanes] = jnp.exp(-r3 * 8.0)
        up0 = jnp.exp(-r3 * within)
        s.up0[:, :, lanes] = up0
        s.up7[:, :, lanes] = jnp.exp(-r3 * (7.0 - within))
        s.c0[:, :, lanes] = c3 * up0
        s.c1[:, :, lanes] = c3 * jnp.exp(-r3 * (within + 1.0))
        s.c8[:, :, lanes] = c3 * jnp.exp(-r3 * (8.0 - within))
        return carry

    lax.fori_loop(0, GROUPS, tables, 0, unroll=True)

    def spread(table, state, target, descending):
        def one(g, carry):
            lanes = pl.ds(pl.multiple_of(g * LANES, LANES), LANES)
            d8 = s.d8[:, :, lanes]
            v = table[:, :, lanes]
            if state is not None:
                v = v * jnp.broadcast_to(state[:, lanes][:, None, :], (MODES, 8, LANES))
            for t in range(ROWS // 8):
                tile = ROWS // 8 - 1 - t if descending else t
                target[tile * 8 : tile * 8 + 8, lanes] = jnp.sum(v, axis=0)
                if t < ROWS // 8 - 1:
                    v = v * d8
            return carry

        lax.fori_loop(0, GROUPS, one, 0, unroll=True)

    def gather_state(source, table, target, descending):
        def one(g, carry):
            lanes = pl.ds(pl.multiple_of(g * LANES, LANES), LANES)
            d8 = s.d8[:, :, lanes]
            v = jnp.zeros((MODES, 8, LANES), F32)
            for t in range(ROWS // 8):
                tile = ROWS // 8 - 1 - t if descending else t
                rows = source[tile * 8 : tile * 8 + 8, lanes][None]
                v = v * d8 + rows if t else v + rows
            target[:, lanes] = jnp.sum(v * table[:, :, lanes], axis=1)
            return carry

        lax.fori_loop(0, GROUPS, one, 0, unroll=True)

    def transform(v):
        return dot(fwd3[...], split3(v))

    def inverse(v):
        return dot(inv3[...], split3(v))

    c_second()
    s.tap_spec[...] = transform(taps[...])
    spread(s.c0, None, s.work, False)
    c_forward(1, 0)
    c_forward(1, 1)
    a1_forward()
    c_forward(1, 2)
    a2_forward(0)
    c_forward(1, 3)
    s.long_spec[...] = transform(s.work[...])

    @pl.when(me > 0)
    def _():
        halo.wait_recv()

    @pl.when(me == 0)
    def _():
        s.prev[...] = jnp.zeros((ROWS, COLS), BF)

    here2 = jnp.concatenate([fwd3[:, :ROWS], fwd3[:, 2 * ROWS :]], axis=1)
    p, q = s.product[...], s.prev[...]
    s.prod_spec[...] = dot(here2, jnp.concatenate([p, p], axis=0)) + dot(
        past2[...], jnp.concatenate([q, q], axis=0)
    )
    a1_finish()
    c_forward(2, 0)
    s.mr_conv[...] = inverse(times(s.prod_spec[...], s.tap_spec[...]))
    mixed_mr = (qm[...].astype(F32) * s.mr_conv[...]).astype(BF)
    s.mixed_mr[...] = mixed_mr
    s.signal[...] = (kl[...].astype(F32) * mixed_mr.astype(F32)).astype(BF).astype(F32)

    own8 = pl.ds(pl.multiple_of(k * 8, 8), 8)

    def chip_state(own, theirs, into, slots, id2, descending):
        decay = s.dev_decay[own8, :]
        mine, other = own[own8, :], theirs[own8, :]
        near = jnp.where(k == 0, mine, other)
        far = jnp.where(k == 0, other, mine)
        into[...] = near + decay * far if descending else decay * near + far
        sign = -1 if descending else 1
        ahead = chip if descending else CHIPS - 1 - chip

        def put(d, carry):
            @pl.when(d <= ahead)
            def _():
                copy(into, slots.at[d], id2 + d, plane(chip_off(sign * d), k)).start()

            return carry

        for d in range(1, CHIPS):
            put(d, 0)

    def chip_finish(into, slots, id2, id3, target, descending):
        sign = -1 if descending else 1
        ahead = chip if descending else CHIPS - 1 - chip
        behind = CHIPS - 1 - chip if descending else chip

        def take(d, carry):
            @pl.when(d <= behind)
            def _():
                copy(into, slots.at[d], id2 + d, plane(chip_off(sign * d), k)).wait_recv()

            return carry

        for d in range(1, CHIPS):
            take(d, 0)
        decay = s.chip_decay[own8, :]
        total = jnp.zeros((8, COLS), F32)
        for d in range(CHIPS - 1, 0, -1):
            total = jnp.where(d <= behind, total * decay + slots[d], 0.0)
        target[own8, :] = total
        send(target.at[own8], target.at[own8], id3, mate)

        def sent(d, carry):
            @pl.when(d <= ahead)
            def _():
                copy(into, slots.at[d], id2 + d, plane(chip_off(sign * d), k)).wait_send()

            return carry

        return lambda: lax.fori_loop(1, CHIPS, sent, 0)

    other8 = pl.ds(pl.multiple_of((1 - k) * 8, 8), 8)

    c_forward(2, 1)
    c_forward(2, 2)
    gather_state(s.signal, s.up7, s.f_own, False)
    send(s.f_own, s.f_mate, ID_SF1, mate)
    c_forward(2, 3)
    a2_forward(2)
    a2_forward(1)
    arrived(s.f_mate, ID_SF1, mate)
    chip_state(s.f_own, s.f_mate, s.f_chip, s.f_slots, ID_SF2, False)
    c_forward(3, 0)
    c_forward(3, 1)
    a2_forward(3)
    spectrum = times(transform(s.signal[...]), s.long_spec[...])
    c_forward(3, 2)
    c_forward(3, 3)
    s.li_out[...] = inverse(spectrum) + skip[...] * s.signal[...]

    f_sent = chip_finish(s.f_chip, s.f_slots, ID_SF2, ID_SF3, s.f_in, False)
    arrived(s.f_in.at[other8], ID_SF3, mate)
    s.enter[...] = jnp.where(k == 0, s.f_in[...], s.dev_decay[...] * s.f_in[...] + s.f_mate[...])
    spread(s.c1, s.enter, s.work, False)
    s.li_out[...] = s.li_out[...] + s.work[...]
    s.mixed[half(k), :] = (ql[...].astype(F32) * s.li_out[...]).astype(BF)
    send(s.mixed.at[half(k)], s.mixed.at[half(k)], ID_MIX, mate)
    for j in range(4):
        a2_finish(j)
    c_finish()

    s.gm_part[...] = dot(
        jnp.concatenate([cg[j] for j in range(n_z)], axis=1), wg[...].reshape(CHIPS * ROWS, COLS)
    )
    send(s.gm_part.at[half(1 - k)], s.gm_mate, ID_GM, mate)

    arrived(s.mixed.at[half(1 - k)], ID_MIX, mate)

    def project(j, carry):
        part = lax.dot_general(
            cg[j], s.mixed[...], (((0,), (0,)), ((), ())), preferred_element_type=F32
        ).astype(BF)
        s.dw_part[2 * j] = part[:ROWS]
        s.dw_part[2 * j + 1] = part[ROWS:]
        return carry

    lax.fori_loop(0, n_z, project, 0, unroll=True)

    def dpart(ra, rb):
        return s.dw_part.at[at(ring(a, ra), ring(b, rb))]

    def drows(ra, rb, rows):
        return s.dw_part.at[at(ring(a, ra), ring(b, rb)), rows]

    def accumulate(target, came):
        target[...] = (target[...].astype(F32) + came[...].astype(F32)).astype(BF)

    def d_start(j):
        ra, i = REL[j], ID_D1 + 4 * j
        send(drows(ra, 2, low), s.dw_half.at[j, low], i, b_next)
        send(drows(ra, 2, high), s.dw_half.at[j, high], i + 1, b_prev)

    def d_middle(j):
        ra, i = REL[j], ID_D1 + 4 * j
        arrived(s.dw_half.at[j, low], i, b_next)
        accumulate(drows(ra, 1, low), s.dw_half.at[j, low])
        send(dpart(ra, 1), s.dw_from_prev.at[j], i + 2, b_next)
        arrived(s.dw_half.at[j, high], i + 1, b_prev)
        accumulate(drows(ra, -1, high), s.dw_half.at[j, high])
        send(dpart(ra, -1), s.dw_from_next.at[j], i + 3, b_prev)

    def d_sum(j):
        ra, i = REL[j], ID_D1 + 4 * j
        arrived(s.dw_from_prev.at[j], i + 2, b_next)
        arrived(s.dw_from_next.at[j], i + 3, b_prev)
        return (
            dpart(ra, 0)[...].astype(F32)
            + s.dw_from_prev[j].astype(F32)
            + s.dw_from_next[j].astype(F32)
        )

    def d_end(j):
        s.dw_ring[j] = d_sum(j).astype(BF)

    def d_turn():
        send(s.dw_ring.at[3, low], s.dw_half2.at[low], ID_D2, a_next)
        send(s.dw_ring.at[3, high], s.dw_half2.at[high], ID_D2 + 1, a_prev)

    def d_turn_middle():
        arrived(s.dw_half2.at[low], ID_D2, a_next)
        accumulate(s.dw_ring.at[2, low], s.dw_half2.at[low])
        send(s.dw_ring.at[2], s.dw_from_prev2, ID_D2 + 2, a_next)
        arrived(s.dw_half2.at[high], ID_D2 + 1, a_prev)
        accumulate(s.dw_ring.at[1, high], s.dw_half2.at[high])
        send(s.dw_ring.at[1], s.dw_from_next2, ID_D2 + 3, a_prev)

    for j in (3, 2, 1, 0):
        d_start(j)

    def share(j, carry):
        block = wg[pl.ds(2 * j, 2)].reshape(2 * ROWS, COLS)
        s.o_part[j] = lax.dot_general(
            s.mixed[...], block, (((1,), (1,)), ((), ())), preferred_element_type=F32
        ).astype(BF)
        return carry

    def opart(dz, chunk):
        return s.o_part.at[lax.rem(z + dz + n_z, n_z), pl.ds(chunk * ROWS, ROWS)]

    def ocame(direction, step, chunk):
        return s.o_came.at[direction * 4 + step - 1, pl.ds(chunk * ROWS, ROWS)]

    def b_send(direction, step, chunk):
        dz = (5 - step) * (1 if direction == 0 else -1)
        send(
            opart(dz, chunk),
            ocame(direction, step, chunk),
            ID_B + direction * 8 + (step - 1) * 2 + chunk,
            z_next if direction == 0 else z_prev,
        )

    def b_arrived(direction, step, chunk):
        arrived(
            ocame(direction, step, chunk),
            ID_B + direction * 8 + (step - 1) * 2 + chunk,
            z_next if direction == 0 else z_prev,
        )

    def b_start():
        for direction in range(2):
            b_send(direction, 1, direction)
            b_send(direction, 2, 1 - direction)

    def b_forward(step, chunk):
        for direction in range(2):
            if step == 1 and chunk != direction:
                continue
            b_arrived(direction, step, chunk)
            dz = (4 - step) * (1 if direction == 0 else -1)
            accumulate(opart(dz, chunk), ocame(direction, step, chunk))
            b_send(direction, step + 1, chunk)

    def loop(first, count, action):
        for d in range(first, count):
            action(d)

    arrived(s.gm_mate, ID_GM, mate)
    gm = s.gm_part[half(k), :] + s.gm_mate[...]
    s.grad_out[...] = gm * ql[...].astype(F32)
    gather_state(s.grad_out, s.up0, s.b_own, True)
    send(s.b_own, s.b_mate, ID_SB1, mate)
    gql[...] = gm * s.li_out[...]
    store(gql, 4)
    lax.fori_loop(0, n_z, share, 0, unroll=True)
    b_start()
    arrived(s.b_mate, ID_SB1, mate)
    chip_state(s.b_own, s.b_mate, s.b_chip, s.b_slots, ID_SB2, True)
    s.spec[...] = conj_times(s.long_spec[...], transform(s.grad_out[...]))
    d_middle(3)
    s.o_sum[...] = lax.dot_general(
        s.mixed[...],
        wg[pl.ds(2 * z, 2)].reshape(2 * ROWS, COLS),
        (((1,), (1,)), ((), ())),
        preferred_element_type=F32,
    )
    d_middle(2)
    b_forward(1, 0)
    b_forward(1, 1)
    s.grad_out[...] = inverse(s.spec[...]) + skip[...] * s.grad_out[...]
    d_middle(1)
    d_middle(0)

    b_sent = chip_finish(s.b_chip, s.b_slots, ID_SB2, ID_SB3, s.b_in, True)
    b_forward(2, 0)
    b_forward(2, 1)
    arrived(s.b_in.at[other8], ID_SB3, mate)
    s.enter[...] = jnp.where(
        k == 1, s.b_in[...], s.dev_decay[...] * s.b_in[...] + s.b_mate[...]
    )
    spread(s.c8, s.enter, s.work, True)
    gli = s.grad_out[...] + s.work[...]
    gkl[...] = gli * s.mixed_mr[...].astype(F32)
    gmm = gli * kl[...].astype(F32)
    gqm[...] = gmm * s.mr_conv[...]
    gconv = gmm * qm[...].astype(F32)
    s.work[...] = gconv
    s.grad_halo[...] = gconv.astype(BF)
    back = copy(s.grad_halo, s.after, ID_BACK_HALO, prv)

    @pl.when(me > 0)
    def _():
        back.start()

    store(gkl, 5)
    store(gqm, 1)

    spec = transform(s.work[...])
    s.spec[...] = spec
    s.t_own[...] = inverse(conj_times(s.prod_spec[...], spec))
    th = ROWS // 2

    def trows(core):
        return pl.ds(pl.multiple_of(core * th, th), th)

    send(s.t_own.at[trows(1 - k)], s.t_mate, ID_T1, mate)
    arrived(s.t_mate, ID_T1, mate)
    s.t_half[...] = s.t_own[trows(k), :] + s.t_mate[...]

    def piece(c, base):
        rows = pl.ds(pl.multiple_of(base + lax.div(c, 2) * 8, 8), 8)
        lanes = pl.ds(pl.multiple_of(lax.rem(c, 2) * 256, 256), 256)
        return rows, lanes

    def t2_copy(d):
        to = chip_off(d)
        rows, lanes = piece(to, 0)
        return copy(s.t_half.at[rows, lanes], s.t_slots.at[d], ID_T2 + d, plane(to, k))

    for d in range(1, CHIPS):
        t2_copy(d).start()
    d_end(3)
    d_turn()
    b_forward(3, 0)
    b_forward(3, 1)
    d_end(2)
    d_end(1)
    d_turn_middle()

    @pl.when(me == last)
    def _():
        s.after[...] = jnp.zeros((ROWS, COLS), BF)

    @pl.when(me < last)
    def _():
        back.wait_recv()

    n = s.after[...]
    spec = s.spec[...] - dot(past2[...], jnp.concatenate([n, n], axis=0))
    gp = inverse(conj_times(s.tap_spec[...], spec))
    gkm[...] = gp * vm[...].astype(F32)
    gvm[...] = gp * km[...].astype(F32)
    store(gkm, 2)
    store(gvm, 3)

    loop(1, CHIPS, lambda d: t2_copy(d).wait_recv())
    rows, lanes = piece(chip, 0)
    total = s.t_half[rows, lanes]
    for d in range(1, CHIPS):
        total = total + s.t_slots[d]
    total = total * grad_scale
    s.t_done[...] = total
    rows, lanes = piece(chip, k * th)
    s.t_all[rows, lanes] = total

    def t3_copy(d):
        return copy(s.t_done, s.t_all.at[rows, lanes], ID_T3 + d, plane(chip_off(d), k))

    def t3_arrived(d):
        rows_from, lanes_from = piece(chip_off(-d), k * th)
        copy(s.t_done, s.t_all.at[rows_from, lanes_from], ID_T3 + d, plane(chip_off(d), k)).wait_recv()

    for d in range(1, CHIPS):
        t3_copy(d).start()

    for direction in range(2):
        for chunk in range(2):
            b_arrived(direction, 4, chunk)
    s.o_sum[...] = s.o_sum[...] + s.o_came[3].astype(F32) + s.o_came[7].astype(F32)
    send(s.o_sum.at[half(1 - k)], s.o_mate, ID_OUT, mate)

    total = d_sum(0)
    arrived(s.dw_from_prev2, ID_D2 + 2, a_next)
    arrived(s.dw_from_next2, ID_D2 + 3, a_prev)
    total = total + s.dw_from_prev2[...].astype(F32) + s.dw_from_next2[...].astype(F32)
    gw[...] = total * grad_scale
    store(gw, 7)

    arrived(s.o_mate, ID_OUT, mate)
    for h in range(2):
        mine = pl.ds(pl.multiple_of((2 * h + k) * LANES, LANES), LANES)
        theirs = pl.ds(pl.multiple_of((2 * h + 1 - k) * LANES, LANES), LANES)
        out[:, mine] = s.o_sum[half(k), h * LANES : (h + 1) * LANES]
        out[:, theirs] = s.o_mate[:, h * LANES : (h + 1) * LANES]
    store(out, 0)

    loop(1, CHIPS, t3_arrived)
    send(s.t_all.at[trows(k)], s.t_all.at[trows(k)], ID_T4, mate)
    arrived(s.t_all.at[trows(1 - k)], ID_T4, mate)
    store(s.t_all, 6)

    for c in stored:
        c.wait()
    for c in pending:
        c.wait_send()
    f_sent()
    b_sent()
    loop(1, CHIPS, lambda d: t2_copy(d).wait_send())
    loop(1, CHIPS, lambda d: t3_copy(d).wait_send())

    @pl.when(me < last)
    def _():
        halo.wait_send()

    @pl.when(me > 0)
    def _():
        back.wait_send()


def shards(query_mr, key_mr, value_mr, query_li, key_li, mr_taps, li_time, li_residue, li_skip, out_weight, cotangent):
    consts = [jnp.asarray(m) for m in transforms()]
    args = (
        key_mr,
        value_mr,
        cotangent,
        out_weight,
        mr_taps,
        li_time,
        li_residue,
        query_mr,
        key_li,
        query_li,
        li_skip.reshape(1, COLS),
        *consts,
    )
    block = jax.ShapeDtypeStruct((ROWS, COLS), F32)
    hbm = pl.BlockSpec(memory_space=pltpu.HBM)
    results = pl.pallas_call(
        kernel,
        out_shape=(block,) * 8,
        in_specs=[hbm] * len(args),
        out_specs=(hbm,) * 8,
        scratch_shapes=[pltpu.VMEM(shape, kind) for shape, kind in INPUTS + tuple(SCRATCH.values())]
        + [pltpu.SemaphoreType.DMA((ID_COUNT,)), pltpu.SemaphoreType.DMA((ID_COUNT,)), pltpu.SemaphoreType.DMA((len(INPUTS),)), pltpu.SemaphoreType.DMA((8,))],
        compiler_params=pltpu.CompilerParams(
            collective_id=0, has_side_effects=True, vmem_limit_bytes=60 * 1024 * 1024
        ),
        cost_estimate=pl.CostEstimate(flops=3_000_000_000, bytes_accessed=4_000_000, transcendentals=1_000_000),
    )(*args)
    return pl.pallas_call(
        write_out,
        out_shape=(block,) * 8,
        in_specs=[hbm] * 8,
        out_specs=(hbm,) * 8,
        scratch_shapes=[
            pltpu.VMEM((8, ROWS, COLS), F32),
            pltpu.SemaphoreType.DMA((8,)),
            pltpu.SemaphoreType.DMA((8,)),
        ],
        compiler_params=pltpu.CompilerParams(vmem_limit_bytes=60 * 1024 * 1024),
        cost_estimate=pl.CostEstimate(flops=0, bytes_accessed=4_000_000, transcendentals=0),
    )(*results)


def write_out(*refs):
    held, load_sem, store_sem = refs[16:]
    loads = [pltpu.make_async_copy(refs[i], held.at[i], load_sem.at[i]) for i in range(8)]
    stores = [pltpu.make_async_copy(held.at[i], refs[8 + i], store_sem.at[i]) for i in range(8)]
    for c in loads:
        c.start()
    for load, store in zip(loads, stores):
        load.wait()
        store.start()
    for c in stores:
        c.wait()


def solution(mesh):
    rows = P("ctx", "fsdp")
    wide = P(None, "fsdp")
    return jax.shard_map(
        shards,
        mesh=mesh,
        in_specs=(rows, rows, rows, rows, rows, wide, wide, wide, P("fsdp"), rows, rows),
        out_specs=(rows, rows, rows, rows, rows, rows, wide, rows),
        check_vma=False,
    )
```

```python
import math
import types

import jax
import jax.numpy as jnp
import ml_dtypes
import numpy as np
from jax import lax
from jax.experimental import pallas as pl
from jax.experimental.pallas import tpu as pltpu
from jax.sharding import PartitionSpec as P

BF = jnp.bfloat16
F32 = jnp.float32
MESH = pl.DeviceIdType.MESH
ROWS = 128
COLS = 512
MODES = 16
RING = 4
CHIPS = RING * RING
LANES = 128
GROUPS = COLS // LANES


def split_const(m):
    hi = m.astype(ml_dtypes.bfloat16)
    lo = (m - hi.astype(np.float64)).astype(ml_dtypes.bfloat16)
    return hi, lo


def transforms():
    theta = 2.0 * np.pi * (np.arange(ROWS) + 0.5)[:, None] / (2 * ROWS)

    def forward(places):
        return np.concatenate([np.cos(theta * places), -np.sin(theta * places)], axis=0)

    here = forward(np.arange(ROWS)[None, :].astype(np.float64))
    past = forward(np.arange(-ROWS, 0)[None, :].astype(np.float64))
    here_hi, here_lo = split_const(here)
    past_hi, past_lo = split_const(past)
    back_hi, back_lo = split_const(here.T / ROWS)
    return (
        np.concatenate([here_hi, here_hi, here_lo], axis=1),
        np.concatenate([past_hi, past_lo], axis=1),
        np.concatenate([back_hi, back_hi, back_lo], axis=1),
    )


def dot(a, b):
    return jnp.dot(a, b, preferred_element_type=F32)


def split3(v):
    hi = v.astype(BF)
    lo = (v - hi.astype(F32)).astype(BF)
    return jnp.concatenate([hi, lo, hi], axis=0)


def times(a, b):
    ar, ai, br, bi = a[:ROWS], a[ROWS:], b[:ROWS], b[ROWS:]
    return jnp.concatenate([ar * br - ai * bi, ar * bi + ai * br], axis=0)


def conj_times(a, b):
    ar, ai, br, bi = a[:ROWS], a[ROWS:], b[:ROWS], b[ROWS:]
    return jnp.concatenate([ar * br + ai * bi, ar * bi - ai * br], axis=0)


ID_A1 = 0
ID_A2 = 4
ID_C = 20
ID_HALO = 38
ID_BACK_HALO = 39
ID_SF1 = 40
ID_SF3 = 41
ID_SB1 = 42
ID_SB3 = 43
ID_MIX = 44
ID_GM = 45
ID_OUT = 46
ID_T1 = 47
ID_T4 = 48
ID_SF2 = 49
ID_SB2 = 65
ID_T2 = 81
ID_T3 = 97
ID_D1 = 113
ID_D2 = 129
ID_B = 133
ID_CR = 149
ID_COUNT = 181

SCRATCH = dict(
    product=((ROWS, COLS), BF),
    prev=((ROWS, COLS), BF),
    grad_halo=((ROWS, COLS), BF),
    after=((ROWS, COLS), BF),
    wg=((CHIPS, ROWS, COLS), BF),
    cg=((8, 2 * ROWS, 256), BF),
    mixed=((2 * ROWS, COLS), BF),
    mixed_mr=((ROWS, COLS), BF),
    tap_spec=((2 * ROWS, COLS), F32),
    long_spec=((2 * ROWS, COLS), F32),
    prod_spec=((2 * ROWS, COLS), F32),
    mr_conv=((ROWS, COLS), F32),
    signal=((ROWS, COLS), F32),
    li_out=((ROWS, COLS), F32),
    work=((ROWS, COLS), F32),
    d8=((MODES, 8, COLS), F32),
    up0=((MODES, 8, COLS), F32),
    up7=((MODES, 8, COLS), F32),
    c0=((MODES, 8, COLS), F32),
    c1=((MODES, 8, COLS), F32),
    c8=((MODES, 8, COLS), F32),
    dev_decay=((MODES, COLS), F32),
    chip_decay=((MODES, COLS), F32),
    f_own=((MODES, COLS), F32),
    f_mate=((MODES, COLS), F32),
    f_chip=((8, COLS), F32),
    f_slots=((CHIPS, 8, COLS), F32),
    f_in=((MODES, COLS), F32),
    b_own=((MODES, COLS), F32),
    b_mate=((MODES, COLS), F32),
    b_chip=((8, COLS), F32),
    b_slots=((CHIPS, 8, COLS), F32),
    b_in=((MODES, COLS), F32),
    enter=((MODES, COLS), F32),
    gm_part=((2 * ROWS, COLS), F32),
    gm_mate=((ROWS, COLS), F32),
    spec=((2 * ROWS, COLS), F32),
    grad_out=((ROWS, COLS), F32),
    dw_part=((CHIPS, ROWS, COLS), BF),
    dw_half=((RING, ROWS, COLS), BF),
    dw_from_prev=((RING, ROWS, COLS), BF),
    dw_from_next=((RING, ROWS, COLS), BF),
    dw_ring=((RING, ROWS, COLS), BF),
    dw_half2=((ROWS, COLS), BF),
    dw_from_prev2=((ROWS, COLS), BF),
    dw_from_next2=((ROWS, COLS), BF),
    o_part=((8, 2 * ROWS, 256), BF),
    o_came=((8, 2 * ROWS, 256), BF),
    o_sum=((2 * ROWS, 256), F32),
    o_mate=((ROWS, 256), F32),
    t_own=((ROWS, COLS), F32),
    t_mate=((ROWS // 2, COLS), F32),
    t_half=((ROWS // 2, COLS), F32),
    t_slots=((CHIPS, 8, 256), F32),
    t_done=((8, 256), F32),
    t_all=((ROWS, COLS), F32),
    out=((ROWS, COLS), F32),
    gqm=((ROWS, COLS), F32),
    gkm=((ROWS, COLS), F32),
    gvm=((ROWS, COLS), F32),
    gql=((ROWS, COLS), F32),
    gkl=((ROWS, COLS), F32),
    gw=((ROWS, COLS), F32),
)


INPUTS = (
    ((ROWS, COLS), BF),
    ((ROWS, COLS), BF),
    ((ROWS, COLS), BF),
    ((ROWS, COLS), BF),
    ((ROWS, COLS), F32),
    ((MODES, COLS), F32),
    ((MODES, COLS), F32),
    ((ROWS, COLS), BF),
    ((ROWS, COLS), BF),
    ((ROWS, COLS), BF),
    ((1, COLS), F32),
    ((2 * ROWS, 3 * ROWS), BF),
    ((2 * ROWS, 2 * ROWS), BF),
    ((ROWS, 6 * ROWS), BF),
)


def kernel(*refs):
    n_in = len(INPUTS)
    given = refs[:n_in]
    results = refs[n_in : n_in + 8]
    held = refs[n_in + 8 : n_in + 8 + n_in]
    (km, vm, cot, w, taps, time, residue, qm, kl, ql, skip, fwd3, past2, inv3) = held
    s = types.SimpleNamespace(**dict(zip(SCRATCH, refs[2 * n_in + 8 :])))
    out, gqm, gkm, gvm, gql, gkl, gw = s.out, s.gqm, s.gkm, s.gvm, s.gql, s.gkl, s.gw
    snd, rcv, ld, st = refs[2 * n_in + 8 + len(SCRATCH) :]

    def load(i):
        return pltpu.make_async_copy(given[i], held[i], ld.at[i])

    for i in range(n_in):
        load(i).start()

    stored = []

    def store(source, i):
        c = pltpu.make_async_copy(source, results[i], st.at[i])
        c.start()
        stored.append(c)

    n_z = 8
    grad_scale = 1.0 / math.sqrt(ROWS * 2 * CHIPS)
    me = lax.axis_index("ctx")
    z = lax.axis_index("fsdp")
    k = lax.rem(me, 2)
    chip = lax.div(me, 2)
    x, y = lax.div(chip, RING), lax.rem(chip, RING)
    a = x * (1 - k) + y * k
    b = y * (1 - k) + x * k

    def ring(v, by):
        return lax.rem(v + by + RING, RING)

    def at(pa, pb):
        return (pa * RING + pb) * (1 - k) + (pb * RING + pa) * k

    def plane(c, core):
        return (c * 2 + core, z)

    mate = (chip * 2 + (1 - k), z)

    def up(dz):
        return (me, lax.rem(z + dz + n_z, n_z))

    def copy(src, dst, i, to):
        return pltpu.make_async_remote_copy(
            src_ref=src, dst_ref=dst, send_sem=snd.at[i], recv_sem=rcv.at[i], device_id=to, device_id_type=MESH
        )

    pending = []

    def send(src, dst, i, to):
        c = copy(src, dst, i, to)
        c.start()
        pending.append(c)

    def arrived(dst, i, to):
        copy(dst, dst, i, to).wait_recv()

    def half(h):
        return pl.ds(pl.multiple_of(h * ROWS, ROWS), ROWS)

    def chip_off(by):
        return lax.rem(chip + by + CHIPS, CHIPS)

    barrier = pltpu.get_barrier_semaphore()
    pl.semaphore_signal(barrier, inc=1, device_id=mate, device_id_type=MESH)

    def greet_chip(d, carry):
        pl.semaphore_signal(barrier, inc=1, device_id=plane(chip_off(d), k), device_id_type=MESH)
        return carry

    lax.fori_loop(1, CHIPS, greet_chip, 0)

    for d in (1, -1):
        pl.semaphore_signal(barrier, inc=1, device_id=up(d), device_id_type=MESH)
    last = 2 * CHIPS - 1
    across = (me + 2 * k - 1, z)

    @pl.when((me > 0) & (me < last))
    def _():
        pl.semaphore_signal(barrier, inc=1, device_id=across, device_id_type=MESH)

    for i in range(4):
        load(i).wait()
    s.product[...] = (km[...].astype(F32) * vm[...].astype(F32)).astype(BF)
    for h in range(2):
        s.cg[z, half(k), h * LANES : (h + 1) * LANES] = cot[
            :, pl.ds(pl.multiple_of((2 * h + k) * LANES, LANES), LANES)
        ]
    s.wg[chip] = w[...]

    peers = 1 + (CHIPS - 1) + 2

    @pl.when((me == 0) | (me == last))
    def _():
        pl.semaphore_wait(barrier, peers)

    @pl.when((me > 0) & (me < last))
    def _():
        pl.semaphore_wait(barrier, peers + 1)

    nxt = (lax.rem(me + 1, last + 1), z)
    prv = (lax.rem(me + last, last + 1), z)

    halo = copy(s.product, s.prev, ID_HALO, nxt)

    @pl.when(me < last)
    def _():
        halo.start()

    a_next, a_prev = plane(at(ring(a, 1), b), k), plane(at(ring(a, -1), b), k)
    b_next, b_prev = plane(at(a, ring(b, 1)), k), plane(at(a, ring(b, -1)), k)
    a_over = plane(at(ring(a, 2), b), k)
    low, high = pl.ds(0, ROWS // 2), pl.ds(ROWS // 2, ROWS // 2)
    wg = s.wg

    def wblock(ra, rb):
        return wg.at[at(ring(a, ra), ring(b, rb))]

    REL = (0, -1, 1, 2)

    def a2_send(j):
        block = wblock(REL[j], 0)
        send(block, block, ID_A2 + 4 * j, b_next)
        send(block, block, ID_A2 + 4 * j + 1, b_prev)

    def a1_send():
        block = wblock(0, 0)
        send(block, block, ID_A1 + 2, a_over)
        send(block, block, ID_A1, a_next)
        send(block, block, ID_A1 + 1, a_prev)

    def a1_forward():
        arrived(wblock(1, 0), ID_A1 + 1, a_prev)
        a2_send(2)
        arrived(wblock(-1, 0), ID_A1, a_next)
        a2_send(1)

    def a1_finish():
        arrived(wblock(2, 0), ID_A1 + 2, a_over)
        a2_send(3)

    def whalf(ra, rb, rows):
        return wg.at[at(ring(a, ra), ring(b, rb)), rows]

    def a2_forward(j):
        ra, i = REL[j], ID_A2 + 4 * j
        arrived(wblock(ra, 1), i + 1, b_prev)
        if j == 0:
            send(wblock(ra, 1), wblock(ra, 1), i + 3, b_prev)
        else:
            send(whalf(ra, 1, high), whalf(ra, 1, high), i + 3, b_prev)
            arrived(wblock(ra, -1), i, b_next)
            send(whalf(ra, -1, low), whalf(ra, -1, low), i + 2, b_next)

    def a2_finish(j):
        ra, i = REL[j], ID_A2 + 4 * j
        if j == 0:
            arrived(wblock(ra, -1), i, b_next)
            arrived(wblock(ra, 2), i + 3, b_prev)
        else:
            arrived(whalf(ra, 2, high), i + 3, b_prev)
            arrived(whalf(ra, 2, low), i + 2, b_next)

    cg = s.cg
    z_next, z_prev = up(1), up(-1)

    def cblock(rz, chunk):
        core = k if chunk < 2 else 1 - k
        rows = pl.ds(pl.multiple_of(core * ROWS + chunk % 2 * 64, 64), 64)
        return cg.at[lax.rem(z + rz + n_z, n_z), rows]

    def c_id(direction, step, chunk):
        return ID_CR + direction * 16 + (step - 1) * 4 + chunk

    def c_send(direction, step, chunk):
        block = cblock(1 - step if direction == 0 else step - 1, chunk)
        send(block, block, c_id(direction, step, chunk), z_prev if direction else z_next)

    def c_mate_refs(h, core):
        return cg.at[z, half(k if core else 1 - k), pl.ds(h * LANES, LANES)]

    def c_start():
        for h in range(2):
            send(
                cot.at[:, pl.ds(pl.multiple_of((2 * h + 1 - k) * LANES, LANES), LANES)],
                c_mate_refs(h, True),
                ID_C + h,
                mate,
            )
        for chunk in range(2):
            for direction in range(2):
                c_send(direction, 1, chunk)

    def c_second():
        for h in range(2):
            arrived(c_mate_refs(h, False), ID_C + h, mate)
        for chunk in (2, 3):
            for direction in range(2):
                c_send(direction, 1, chunk)

    def c_forward(step, chunk):
        for direction in range(2):
            rz = step if direction else -step
            arrived(cblock(rz, chunk), c_id(direction, step, chunk), z_prev if direction else z_next)
            if step < 3 or chunk % 2 == direction:
                c_send(direction, step + 1, chunk)

    def c_finish():
        for chunk in range(4):
            direction = chunk % 2
            arrived(cblock(4, chunk), c_id(direction, 4, chunk), z_prev if direction else z_next)

    a1_send()
    c_start()
    a2_send(0)

    for i in range(4, n_in):
        load(i).wait()

    within = lax.broadcasted_iota(jnp.int32, (1, 8, LANES), 1).astype(F32)

    def tables(g, carry):
        lanes = pl.ds(pl.multiple_of(g * LANES, LANES), LANES)
        rate = 1.0 / time[:, lanes]
        u = 2.0 * rate
        series = 1.0 - u * (1.0 / 7.0)
        for n in (6, 5, 4, 3, 2):
            series = 1.0 - u * (1.0 / n) * series
        coef = residue[:, lanes] * jnp.sqrt(u * series)
        s.dev_decay[:, lanes] = jnp.exp(-rate * ROWS)
        s.chip_decay[:, lanes] = jnp.exp(-rate * (2 * ROWS))
        r3 = jnp.broadcast_to(rate[:, None, :], (MODES, 8, LANES))
        c3 = jnp.broadcast_to(coef[:, None, :], (MODES, 8, LANES))
        s.d8[:, :, lanes] = jnp.exp(-r3 * 8.0)
        up0 = jnp.exp(-r3 * within)
        s.up0[:, :, lanes] = up0
        s.up7[:, :, lanes] = jnp.exp(-r3 * (7.0 - within))
        s.c0[:, :, lanes] = c3 * up0
        s.c1[:, :, lanes] = c3 * jnp.exp(-r3 * (within + 1.0))
        s.c8[:, :, lanes] = c3 * jnp.exp(-r3 * (8.0 - within))
        return carry

    lax.fori_loop(0, GROUPS, tables, 0, unroll=True)

    def spread(table, state, target, descending):
        def one(g, carry):
            lanes = pl.ds(pl.multiple_of(g * LANES, LANES), LANES)
            d8 = s.d8[:, :, lanes]
            v = table[:, :, lanes]
            if state is not None:
                v = v * jnp.broadcast_to(state[:, lanes][:, None, :], (MODES, 8, LANES))
            for t in range(ROWS // 8):
                tile = ROWS // 8 - 1 - t if descending else t
                target[tile * 8 : tile * 8 + 8, lanes] = jnp.sum(v, axis=0)
                if t < ROWS // 8 - 1:
                    v = v * d8
            return carry

        lax.fori_loop(0, GROUPS, one, 0, unroll=True)

    def gather_state(source, table, target, descending):
        def one(g, carry):
            lanes = pl.ds(pl.multiple_of(g * LANES, LANES), LANES)
            d8 = s.d8[:, :, lanes]
            v = jnp.zeros((MODES, 8, LANES), F32)
            for t in range(ROWS // 8):
                tile = ROWS // 8 - 1 - t if descending else t
                rows = source[tile * 8 : tile * 8 + 8, lanes][None]
                v = v * d8 + rows if t else v + rows
            target[:, lanes] = jnp.sum(v * table[:, :, lanes], axis=1)
            return carry

        lax.fori_loop(0, GROUPS, one, 0, unroll=True)

    def transform(v):
        return dot(fwd3[...], split3(v))

    def inverse(v):
        return dot(inv3[...], split3(v))

    c_second()
    s.tap_spec[...] = transform(taps[...])
    spread(s.c0, None, s.work, False)
    c_forward(1, 0)
    c_forward(1, 1)
    a1_forward()
    c_forward(1, 2)
    a2_forward(0)
    c_forward(1, 3)
    s.long_spec[...] = transform(s.work[...])

    @pl.when(me > 0)
    def _():
        halo.wait_recv()

    @pl.when(me == 0)
    def _():
        s.prev[...] = jnp.zeros((ROWS, COLS), BF)

    here2 = jnp.concatenate([fwd3[:, :ROWS], fwd3[:, 2 * ROWS :]], axis=1)
    p, q = s.product[...], s.prev[...]
    s.prod_spec[...] = dot(here2, jnp.concatenate([p, p], axis=0)) + dot(
        past2[...], jnp.concatenate([q, q], axis=0)
    )
    a1_finish()
    c_forward(2, 0)
    s.mr_conv[...] = inverse(times(s.prod_spec[...], s.tap_spec[...]))
    mixed_mr = (qm[...].astype(F32) * s.mr_conv[...]).astype(BF)
    s.mixed_mr[...] = mixed_mr
    s.signal[...] = (kl[...].astype(F32) * mixed_mr.astype(F32)).astype(BF).astype(F32)

    own8 = pl.ds(pl.multiple_of(k * 8, 8), 8)

    def chip_state(own, theirs, into, slots, id2, descending):
        decay = s.dev_decay[own8, :]
        mine, other = own[own8, :], theirs[own8, :]
        near = jnp.where(k == 0, mine, other)
        far = jnp.where(k == 0, other, mine)
        into[...] = near + decay * far if descending else decay * near + far
        sign = -1 if descending else 1
        ahead = chip if descending else CHIPS - 1 - chip

        def put(d, carry):
            @pl.when(d <= ahead)
            def _():
                copy(into, slots.at[d], id2 + d, plane(chip_off(sign * d), k)).start()

            return carry

        for d in range(1, CHIPS):
            put(d, 0)

    def chip_finish(into, slots, id2, id3, target, descending):
        sign = -1 if descending else 1
        ahead = chip if descending else CHIPS - 1 - chip
        behind = CHIPS - 1 - chip if descending else chip

        def take(d, carry):
            @pl.when(d <= behind)
            def _():
                copy(into, slots.at[d], id2 + d, plane(chip_off(sign * d), k)).wait_recv()

            return carry

        for d in range(1, CHIPS):
            take(d, 0)
        decay = s.chip_decay[own8, :]
        total = jnp.zeros((8, COLS), F32)
        for d in range(CHIPS - 1, 0, -1):
            total = jnp.where(d <= behind, total * decay + slots[d], 0.0)
        target[own8, :] = total
        send(target.at[own8], target.at[own8], id3, mate)

        def sent(d, carry):
            @pl.when(d <= ahead)
            def _():
                copy(into, slots.at[d], id2 + d, plane(chip_off(sign * d), k)).wait_send()

            return carry

        return lambda: lax.fori_loop(1, CHIPS, sent, 0)

    other8 = pl.ds(pl.multiple_of((1 - k) * 8, 8), 8)

    c_forward(2, 1)
    c_forward(2, 2)
    gather_state(s.signal, s.up7, s.f_own, False)
    send(s.f_own, s.f_mate, ID_SF1, mate)
    c_forward(2, 3)
    a2_forward(2)
    a2_forward(1)
    arrived(s.f_mate, ID_SF1, mate)
    chip_state(s.f_own, s.f_mate, s.f_chip, s.f_slots, ID_SF2, False)
    c_forward(3, 0)
    c_forward(3, 1)
    spectrum = times(transform(s.signal[...]), s.long_spec[...])
    c_forward(3, 2)
    c_forward(3, 3)
    a2_forward(3)
    s.li_out[...] = inverse(spectrum) + skip[...] * s.signal[...]

    f_sent = chip_finish(s.f_chip, s.f_slots, ID_SF2, ID_SF3, s.f_in, False)
    arrived(s.f_in.at[other8], ID_SF3, mate)
    s.enter[...] = jnp.where(k == 0, s.f_in[...], s.dev_decay[...] * s.f_in[...] + s.f_mate[...])
    spread(s.c1, s.enter, s.work, False)
    s.li_out[...] = s.li_out[...] + s.work[...]
    s.mixed[half(k), :] = (ql[...].astype(F32) * s.li_out[...]).astype(BF)
    send(s.mixed.at[half(k)], s.mixed.at[half(k)], ID_MIX, mate)
    for j in range(4):
        a2_finish(j)
    c_finish()

    s.gm_part[...] = dot(
        jnp.concatenate([cg[j] for j in range(n_z)], axis=1), wg[...].reshape(CHIPS * ROWS, COLS)
    )
    send(s.gm_part.at[half(1 - k)], s.gm_mate, ID_GM, mate)

    arrived(s.mixed.at[half(1 - k)], ID_MIX, mate)

    def project(j, carry):
        part = lax.dot_general(
            cg[j], s.mixed[...], (((0,), (0,)), ((), ())), preferred_element_type=F32
        ).astype(BF)
        s.dw_part[2 * j] = part[:ROWS]
        s.dw_part[2 * j + 1] = part[ROWS:]
        return carry

    lax.fori_loop(0, n_z, project, 0, unroll=True)

    def dpart(ra, rb):
        return s.dw_part.at[at(ring(a, ra), ring(b, rb))]

    def drows(ra, rb, rows):
        return s.dw_part.at[at(ring(a, ra), ring(b, rb)), rows]

    def accumulate(target, came):
        target[...] = (target[...].astype(F32) + came[...].astype(F32)).astype(BF)

    def d_start(j):
        ra, i = REL[j], ID_D1 + 4 * j
        send(drows(ra, 2, low), s.dw_half.at[j, low], i, b_next)
        send(drows(ra, 2, high), s.dw_half.at[j, high], i + 1, b_prev)

    def d_middle(j):
        ra, i = REL[j], ID_D1 + 4 * j
        arrived(s.dw_half.at[j, low], i, b_next)
        accumulate(drows(ra, 1, low), s.dw_half.at[j, low])
        send(dpart(ra, 1), s.dw_from_prev.at[j], i + 2, b_next)
        arrived(s.dw_half.at[j, high], i + 1, b_prev)
        accumulate(drows(ra, -1, high), s.dw_half.at[j, high])
        send(dpart(ra, -1), s.dw_from_next.at[j], i + 3, b_prev)

    def d_sum(j):
        ra, i = REL[j], ID_D1 + 4 * j
        arrived(s.dw_from_prev.at[j], i + 2, b_next)
        arrived(s.dw_from_next.at[j], i + 3, b_prev)
        return (
            dpart(ra, 0)[...].astype(F32)
            + s.dw_from_prev[j].astype(F32)
            + s.dw_from_next[j].astype(F32)
        )

    def d_end(j):
        s.dw_ring[j] = d_sum(j).astype(BF)

    def d_turn():
        send(s.dw_ring.at[3, low], s.dw_half2.at[low], ID_D2, a_next)
        send(s.dw_ring.at[3, high], s.dw_half2.at[high], ID_D2 + 1, a_prev)

    def d_turn_middle():
        arrived(s.dw_half2.at[low], ID_D2, a_next)
        accumulate(s.dw_ring.at[2, low], s.dw_half2.at[low])
        send(s.dw_ring.at[2], s.dw_from_prev2, ID_D2 + 2, a_next)
        arrived(s.dw_half2.at[high], ID_D2 + 1, a_prev)
        accumulate(s.dw_ring.at[1, high], s.dw_half2.at[high])
        send(s.dw_ring.at[1], s.dw_from_next2, ID_D2 + 3, a_prev)

    for j in (3, 2, 1, 0):
        d_start(j)

    def share(j, carry):
        block = wg[pl.ds(2 * j, 2)].reshape(2 * ROWS, COLS)
        s.o_part[j] = lax.dot_general(
            s.mixed[...], block, (((1,), (1,)), ((), ())), preferred_element_type=F32
        ).astype(BF)
        return carry

    def opart(dz, chunk):
        return s.o_part.at[lax.rem(z + dz + n_z, n_z), pl.ds(chunk * ROWS, ROWS)]

    def ocame(direction, step, chunk):
        return s.o_came.at[direction * 4 + step - 1, pl.ds(chunk * ROWS, ROWS)]

    def b_send(direction, step, chunk):
        dz = (5 - step) * (1 if direction == 0 else -1)
        send(
            opart(dz, chunk),
            ocame(direction, step, chunk),
            ID_B + direction * 8 + (step - 1) * 2 + chunk,
            z_next if direction == 0 else z_prev,
        )

    def b_arrived(direction, step, chunk):
        arrived(
            ocame(direction, step, chunk),
            ID_B + direction * 8 + (step - 1) * 2 + chunk,
            z_next if direction == 0 else z_prev,
        )

    def b_start():
        for direction in range(2):
            b_send(direction, 1, direction)
            b_send(direction, 2, 1 - direction)

    def b_forward(step, chunk):
        for direction in range(2):
            if step == 1 and chunk != direction:
                continue
            b_arrived(direction, step, chunk)
            dz = (4 - step) * (1 if direction == 0 else -1)
            accumulate(opart(dz, chunk), ocame(direction, step, chunk))
            b_send(direction, step + 1, chunk)

    def loop(first, count, action):
        for d in range(first, count):
            action(d)

    arrived(s.gm_mate, ID_GM, mate)
    gm = s.gm_part[half(k), :] + s.gm_mate[...]
    s.grad_out[...] = gm * ql[...].astype(F32)
    gather_state(s.grad_out, s.up0, s.b_own, True)
    send(s.b_own, s.b_mate, ID_SB1, mate)
    gql[...] = gm * s.li_out[...]
    store(gql, 4)
    lax.fori_loop(0, n_z, share, 0, unroll=True)
    b_start()
    arrived(s.b_mate, ID_SB1, mate)
    chip_state(s.b_own, s.b_mate, s.b_chip, s.b_slots, ID_SB2, True)
    s.spec[...] = conj_times(s.long_spec[...], transform(s.grad_out[...]))
    d_middle(3)
    s.o_sum[...] = lax.dot_general(
        s.mixed[...],
        wg[pl.ds(2 * z, 2)].reshape(2 * ROWS, COLS),
        (((1,), (1,)), ((), ())),
        preferred_element_type=F32,
    )
    d_middle(2)
    b_forward(1, 0)
    b_forward(1, 1)
    s.grad_out[...] = inverse(s.spec[...]) + skip[...] * s.grad_out[...]
    d_middle(1)
    d_middle(0)

    b_sent = chip_finish(s.b_chip, s.b_slots, ID_SB2, ID_SB3, s.b_in, True)
    b_forward(2, 0)
    b_forward(2, 1)
    arrived(s.b_in.at[other8], ID_SB3, mate)
    s.enter[...] = jnp.where(
        k == 1, s.b_in[...], s.dev_decay[...] * s.b_in[...] + s.b_mate[...]
    )
    spread(s.c8, s.enter, s.work, True)
    gli = s.grad_out[...] + s.work[...]
    gkl[...] = gli * s.mixed_mr[...].astype(F32)
    gmm = gli * kl[...].astype(F32)
    gqm[...] = gmm * s.mr_conv[...]
    gconv = gmm * qm[...].astype(F32)
    s.work[...] = gconv
    s.grad_halo[...] = gconv.astype(BF)
    back = copy(s.grad_halo, s.after, ID_BACK_HALO, prv)

    @pl.when(me > 0)
    def _():
        back.start()

    store(gkl, 5)
    store(gqm, 1)

    spec = transform(s.work[...])
    s.spec[...] = spec
    s.t_own[...] = inverse(conj_times(s.prod_spec[...], spec))
    th = ROWS // 2

    def trows(core):
        return pl.ds(pl.multiple_of(core * th, th), th)

    send(s.t_own.at[trows(1 - k)], s.t_mate, ID_T1, mate)
    arrived(s.t_mate, ID_T1, mate)
    s.t_half[...] = s.t_own[trows(k), :] + s.t_mate[...]

    def piece(c, base):
        rows = pl.ds(pl.multiple_of(base + lax.div(c, 2) * 8, 8), 8)
        lanes = pl.ds(pl.multiple_of(lax.rem(c, 2) * 256, 256), 256)
        return rows, lanes

    def t2_copy(d):
        to = chip_off(d)
        rows, lanes = piece(to, 0)
        return copy(s.t_half.at[rows, lanes], s.t_slots.at[d], ID_T2 + d, plane(to, k))

    for d in range(1, CHIPS):
        t2_copy(d).start()
    d_end(3)
    d_turn()
    b_forward(3, 0)
    b_forward(3, 1)
    d_end(2)
    d_end(1)
    d_turn_middle()

    @pl.when(me == last)
    def _():
        s.after[...] = jnp.zeros((ROWS, COLS), BF)

    @pl.when(me < last)
    def _():
        back.wait_recv()

    n = s.after[...]
    spec = s.spec[...] - dot(past2[...], jnp.concatenate([n, n], axis=0))
    gp = inverse(conj_times(s.tap_spec[...], spec))
    gkm[...] = gp * vm[...].astype(F32)
    gvm[...] = gp * km[...].astype(F32)
    store(gkm, 2)
    store(gvm, 3)

    loop(1, CHIPS, lambda d: t2_copy(d).wait_recv())
    rows, lanes = piece(chip, 0)
    total = s.t_half[rows, lanes]
    for d in range(1, CHIPS):
        total = total + s.t_slots[d]
    total = total * grad_scale
    s.t_done[...] = total
    rows, lanes = piece(chip, k * th)
    s.t_all[rows, lanes] = total

    def t3_copy(d):
        return copy(s.t_done, s.t_all.at[rows, lanes], ID_T3 + d, plane(chip_off(d), k))

    def t3_arrived(d):
        rows_from, lanes_from = piece(chip_off(-d), k * th)
        copy(s.t_done, s.t_all.at[rows_from, lanes_from], ID_T3 + d, plane(chip_off(d), k)).wait_recv()

    for d in range(1, CHIPS):
        t3_copy(d).start()

    for direction in range(2):
        for chunk in range(2):
            b_arrived(direction, 4, chunk)
    s.o_sum[...] = s.o_sum[...] + s.o_came[3].astype(F32) + s.o_came[7].astype(F32)
    send(s.o_sum.at[half(1 - k)], s.o_mate, ID_OUT, mate)

    total = d_sum(0)
    arrived(s.dw_from_prev2, ID_D2 + 2, a_next)
    arrived(s.dw_from_next2, ID_D2 + 3, a_prev)
    total = total + s.dw_from_prev2[...].astype(F32) + s.dw_from_next2[...].astype(F32)
    gw[...] = total * grad_scale
    store(gw, 7)

    arrived(s.o_mate, ID_OUT, mate)
    for h in range(2):
        mine = pl.ds(pl.multiple_of((2 * h + k) * LANES, LANES), LANES)
        theirs = pl.ds(pl.multiple_of((2 * h + 1 - k) * LANES, LANES), LANES)
        out[:, mine] = s.o_sum[half(k), h * LANES : (h + 1) * LANES]
        out[:, theirs] = s.o_mate[:, h * LANES : (h + 1) * LANES]
    store(out, 0)

    loop(1, CHIPS, t3_arrived)
    send(s.t_all.at[trows(k)], s.t_all.at[trows(k)], ID_T4, mate)
    arrived(s.t_all.at[trows(1 - k)], ID_T4, mate)
    store(s.t_all, 6)

    for c in stored:
        c.wait()
    for c in pending:
        c.wait_send()
    f_sent()
    b_sent()
    loop(1, CHIPS, lambda d: t2_copy(d).wait_send())
    loop(1, CHIPS, lambda d: t3_copy(d).wait_send())

    @pl.when(me < last)
    def _():
        halo.wait_send()

    @pl.when(me > 0)
    def _():
        back.wait_send()


def shards(query_mr, key_mr, value_mr, query_li, key_li, mr_taps, li_time, li_residue, li_skip, out_weight, cotangent):
    consts = [jnp.asarray(m) for m in transforms()]
    args = (
        key_mr,
        value_mr,
        cotangent,
        out_weight,
        mr_taps,
        li_time,
        li_residue,
        query_mr,
        key_li,
        query_li,
        li_skip.reshape(1, COLS),
        *consts,
    )
    block = jax.ShapeDtypeStruct((ROWS, COLS), F32)
    hbm = pl.BlockSpec(memory_space=pltpu.HBM)
    results = pl.pallas_call(
        kernel,
        out_shape=(block,) * 8,
        in_specs=[hbm] * len(args),
        out_specs=(hbm,) * 8,
        scratch_shapes=[pltpu.VMEM(shape, kind) for shape, kind in INPUTS + tuple(SCRATCH.values())]
        + [pltpu.SemaphoreType.DMA((ID_COUNT,)), pltpu.SemaphoreType.DMA((ID_COUNT,)), pltpu.SemaphoreType.DMA((len(INPUTS),)), pltpu.SemaphoreType.DMA((8,))],
        compiler_params=pltpu.CompilerParams(
            collective_id=0, has_side_effects=True, vmem_limit_bytes=60 * 1024 * 1024
        ),
        cost_estimate=pl.CostEstimate(flops=3_000_000_000, bytes_accessed=4_000_000, transcendentals=1_000_000),
    )(*args)
    return pl.pallas_call(
        write_out,
        out_shape=(block,) * 8,
        in_specs=[hbm] * 8,
        out_specs=(hbm,) * 8,
        scratch_shapes=[
            pltpu.VMEM((8, ROWS, COLS), F32),
            pltpu.SemaphoreType.DMA((8,)),
            pltpu.SemaphoreType.DMA((8,)),
        ],
        compiler_params=pltpu.CompilerParams(vmem_limit_bytes=60 * 1024 * 1024),
        cost_estimate=pl.CostEstimate(flops=0, bytes_accessed=4_000_000, transcendentals=0),
    )(*results)


def write_out(*refs):
    held, load_sem, store_sem = refs[16:]
    loads = [pltpu.make_async_copy(refs[i], held.at[i], load_sem.at[i]) for i in range(8)]
    stores = [pltpu.make_async_copy(held.at[i], refs[8 + i], store_sem.at[i]) for i in range(8)]
    for c in loads:
        c.start()
    for load, store in zip(loads, stores):
        load.wait()
        store.start()
    for c in stores:
        c.wait()


def solution(mesh):
    rows = P("ctx", "fsdp")
    wide = P(None, "fsdp")
    return jax.shard_map(
        shards,
        mesh=mesh,
        in_specs=(rows, rows, rows, rows, rows, wide, wide, wide, P("fsdp"), rows, rows),
        out_specs=(rows, rows, rows, rows, rows, rows, wide, rows),
        check_vma=False,
    )
```
